128 devices in a mesh: group: 2 (over z_hi), fsdp: 64 (over y, x, z_lo, core).
Axes of the slice: x: 4, y: 4, z: 4 (z_hi: 2, z_lo: 2; z = z_hi * 2 + z_lo), core: 2. Of those that a mesh axis runs over, the one named last changes fastest.
Arguments:
- latent_noise: float32 [64, 256, 64], P('fsdp'), may hold values from -6 to 6
- fresh_noise: float32 [64, 256, 64], P('fsdp'), may hold values from -6 to 6
- text_states: bfloat16 [64, 128, 1536], P('fsdp'), may hold values from -6 to 6
- step_index: int32 [64], P('fsdp'), may hold values from 0 to 999
- base_qkv: bfloat16 [1536, 4608], P('fsdp'), may hold values from -0.30618622 to 0.30618622
- latent_in: bfloat16 [64, 1536], replicated, may hold values from -0.75 to 0.75
- modulation: float32 [1536], replicated, may hold values from -3 to 3
- velocity_out: bfloat16 [1536, 64], replicated, may hold values from -0.15625 to 0.15625
- gen_down: bfloat16 [1536, 192], P('fsdp'), may hold values from -0.00015258789 to 0.00015258789
- gen_up: bfloat16 [3, 64, 1536], P(None, None, 'fsdp'), may hold values from -0.0007324219 to 0.0007324219
- critic_down: bfloat16 [1536, 192], P('fsdp'), may hold values from -0.15625 to 0.15625
- critic_up: bfloat16 [3, 64, 1536], P(None, None, 'fsdp'), may hold values from -0.75 to 0.75
Outputs:
- sample_out: float32 [64, 256, 64], P('fsdp')
- grad_down: float32 [2, 1536, 192], P('group', 'fsdp')
- grad_up: float32 [2, 3, 64, 1536], P('group', None, None, 'fsdp')
The draws below stay inside these ranges and needn't reach their ends.
All inputs are finite; a program needn't handle non-finite values. Where the reference program divides by a largest or mean magnitude, that divisor is 1e-20 or more.
Results may differ from the reference program's by a relative error of at most 0.014.
Values may be sent and summed in bfloat16 or wider, within the bound.
No kernel may reach another device: no remote copies, remote signals or barrier semaphores. Data moves between devices by JAX's collectives and lax.ppermute only.
A program may use at most 128 MiB of HBM per device.

```python
import jax
import jax.numpy as jnp
from jax import lax

D = 1536
HEADS = 12
HD = 128
CH = 64
RANK = 64
NSTEPS = 1000
IMG = 256
TXT = 128
HW = 1536
SAMPLES = 64


def draw_base_qkv(key, part):
    first_key = jax.random.fold_in(key, 0)
    weight_scale = D ** (-0.5)
    result = jnp.clip(jax.random.normal(first_key, (D, 3 * HW), jnp.float32), -6.0, 6.0) * weight_scale
    return result.astype(jnp.bfloat16)


def with_ends(values, key, low, top_value):
    dims = values.shape
    spot = [jax.random.randint(jax.random.fold_in(key, axis), (), 0, dims[axis]) for axis in range(len(dims))]
    values = values.at[tuple(spot)].set(low)
    longest = dims.index(max(dims))
    spot[longest] = (spot[longest] + 1) % dims[longest]
    return values.at[tuple(spot)].set(top_value)


def steps_of(own_key, dims, pieces, low, high):
    def one(dim, blocks):
        steps = jax.random.uniform(jax.random.fold_in(jax.random.fold_in(own_key, 6), dim), (blocks,), jnp.float32, low / len(pieces), high / len(pieces))
        return jnp.repeat(jnp.exp(steps), dims[dim] // blocks).reshape((-1,) + (1,) * (len(dims) - dim - 1))

    gain = one(*pieces[0])
    for cut in pieces[1:]:
        gain = gain * one(*cut)
    return gain


def gaussian(stream_key, dims, scale, most, shards=(), kind=jnp.bfloat16):
    array = jax.random.normal(stream_key, dims, jnp.float32) * scale
    if len(shards) > 0:
        array = steps_of(stream_key, dims, shards, -0.22, 0.18) * array
    return jnp.clip(array, min=-most, max=most).astype(kind)


def setup_inputs(seed: int = 0) -> dict:
    seeds = jax.random.split(jax.random.key(seed), 13)
    return {
        "latent_noise": gaussian(seeds[0], (SAMPLES, IMG, CH), 1.0, 6.0, ((0, 64),), jnp.float32),
        "fresh_noise": gaussian(seeds[1], (SAMPLES, IMG, CH), 1.0, 6.0, ((0, 64),), jnp.float32),
        "text_states": gaussian(seeds[2], (SAMPLES, TXT, D), 1.0, 6.0, ((0, 64),)),
        "step_index": with_ends(jax.random.randint(seeds[3], (SAMPLES,), 0, NSTEPS), jax.random.fold_in(seeds[3], 1), 0, NSTEPS - 1).astype(jnp.int32),
        "base_qkv": draw_base_qkv(jax.random.fold_in(seeds[12], 71), 0),
        "latent_in": gaussian(seeds[5], (CH, D), CH ** -0.5, 0.75),
        "modulation": gaussian(seeds[6], (D,), 0.5, 3.0, (), jnp.float32),
        "velocity_out": gaussian(seeds[7], (HW, CH), HW ** -0.5, 0.15625),
        "gen_down": gaussian(seeds[8], (D, 3 * RANK), (D * 1000000) ** -0.5, 0.00015258789, ((0, 64),)),
        "gen_up": gaussian(seeds[9], (3, RANK, HW), (RANK * 1000000) ** -0.5, 0.0007324219, ((2, 64),)),
        "critic_down": gaussian(seeds[10], (D, 3 * RANK), D ** -0.5, 0.15625, ((0, 64),)),
        "critic_up": gaussian(seeds[11], (3, RANK, HW), RANK ** -0.5, 0.75, ((2, 64),)),
    }


def normalize(values):
    return values * lax.rsqrt(lax.optimization_barrier(jnp.mean(values * values, axis=-1, keepdims=True)) + 1e-06)

def embed_tokens(latent, prompt_states, noise_level, latent_in, modulation):
    hidden = jnp.dot(latent.astype(jnp.bfloat16), latent_in, preferred_element_type=jnp.float32)
    picture = (normalize(hidden) * (1.0 + noise_level * modulation)).astype(jnp.bfloat16)
    prompt = normalize(prompt_states.astype(jnp.float32)).astype(jnp.bfloat16)
    return jnp.concatenate([prompt, picture], axis=0)

def attend(queries, key_rows, value_rows):
    query_count = queries.shape[0]
    key_count = key_rows.shape[0]
    query_heads = queries.astype(jnp.float32).reshape(query_count, HEADS, HD)
    key_heads = key_rows.astype(jnp.float32).reshape(key_count, HEADS, HD)
    value_heads = value_rows.astype(jnp.float32).reshape(key_count, HEADS, HD)
    scores = jnp.einsum('qhd,khd->hqk', query_heads, key_heads) * HD ** (-0.5)
    largest = lax.optimization_barrier(jnp.max(scores, axis=-1, keepdims=True))
    weights = jnp.exp(scores - largest)
    shares = (weights / lax.optimization_barrier(jnp.sum(weights, axis=-1, keepdims=True))).astype(jnp.bfloat16)
    shares = lax.optimization_barrier(shares).astype(jnp.float32)
    attended = jnp.einsum('hqk,khd->qhd', shares, value_heads)
    return attended.reshape(query_count, HEADS * HD)

def adapter_out(reduced, up_map):
    return jnp.concatenate([jnp.dot(reduced[:, block * RANK:(block + 1) * RANK], up_map[block], preferred_element_type=jnp.float32) for block in range(3)], axis=1)

def split_heads(qkv):
    head_span = HEADS * HD
    return (qkv[TXT:, :head_span], qkv[:, head_span:2 * head_span], qkv[:, 2 * head_span:])

def readout(qkv, velocity_out):
    queries, key_rows, value_rows = split_heads(qkv)
    attended = attend(queries, key_rows, value_rows)
    return jnp.dot(attended.astype(jnp.bfloat16), velocity_out, preferred_element_type=jnp.float32)

def adapter_grads(tokens, reduced, qkv, up_map, cotangent, velocity_out):
    head_span = HEADS * HD
    upstream = jnp.dot(cotangent.astype(jnp.bfloat16), velocity_out.T, preferred_element_type=jnp.float32)
    queries, key_rows, value_rows = split_heads(qkv)
    unused, backward = jax.vjp(attend, queries, key_rows, value_rows)
    grad_query, grad_key, grad_value = backward(upstream)
    text_zeros = jnp.zeros((TXT, head_span), grad_query.dtype)
    grad_qkv = jnp.concatenate([jnp.concatenate([text_zeros, grad_query], axis=0), grad_key, grad_value], axis=1)
    grad_upmap = jnp.stack([jnp.dot(reduced[:, block * RANK:(block + 1) * RANK].T, grad_qkv[:, block * head_span:(block + 1) * head_span], preferred_element_type=jnp.float32) for block in range(3)])
    grad_reduced = jnp.concatenate([jnp.dot(grad_qkv[:, block * head_span:(block + 1) * head_span], up_map[block].T, preferred_element_type=jnp.float32) for block in range(3)], axis=1).astype(jnp.bfloat16)
    grad_downmap = jnp.dot(tokens.T, grad_reduced, preferred_element_type=jnp.float32)
    return (grad_downmap, grad_upmap)

def reference(latent_noise, fresh_noise, text_states, step_index, base_qkv, latent_in, modulation, velocity_out, gen_down, gen_up, critic_down, critic_up):

    def per_sample(inputs):
        noise_start, fresh, prompt_states, timestep = inputs
        noise_level = (timestep + 1).astype(jnp.float32) / NSTEPS
        tokens_gen = embed_tokens(noise_start, prompt_states, 1.0, latent_in, modulation)
        reduced_gen = jnp.dot(tokens_gen, gen_down, preferred_element_type=jnp.float32).astype(jnp.bfloat16)
        qkv_gen = (jnp.dot(tokens_gen, base_qkv, preferred_element_type=jnp.float32) + adapter_out(reduced_gen, gen_up)).astype(jnp.bfloat16)
        sample = noise_start - readout(qkv_gen, velocity_out)
        noised = (1.0 - noise_level) * sample + noise_level * fresh
        tokens_score = embed_tokens(noised, prompt_states, noise_level, latent_in, modulation)
        base_score = jnp.dot(tokens_score, base_qkv, preferred_element_type=jnp.float32)
        reduced_critic = jnp.dot(tokens_score, critic_down, preferred_element_type=jnp.float32).astype(jnp.bfloat16)
        velocity_real = readout(base_score.astype(jnp.bfloat16), velocity_out)
        qkv_fake = (base_score + adapter_out(reduced_critic, critic_up)).astype(jnp.bfloat16)
        velocity_fake = readout(qkv_fake, velocity_out)
        clean_real = noised - noise_level * velocity_real
        clean_fake = noised - noise_level * velocity_fake
        spread = jnp.mean(jnp.abs(sample - clean_real)) + 1e-05
        cot_gen = -(clean_fake - clean_real) / spread
        cot_critic = 2.0 * (velocity_fake - (fresh - sample)) / (IMG * CH)
        gen_downgrad, gen_upgrad = adapter_grads(tokens_gen, reduced_gen, qkv_gen, gen_up, cot_gen, velocity_out)
        critic_downgrad, critic_upgrad = adapter_grads(tokens_score, reduced_critic, qkv_fake, critic_up, cot_critic, velocity_out)
        return (sample, gen_downgrad, gen_upgrad, critic_downgrad, critic_upgrad)
    results = lax.map(per_sample, (latent_noise, fresh_noise, text_states, step_index))
    grad_down = jnp.stack([lax.optimization_barrier(jnp.sum(results[1], axis=0)), lax.optimization_barrier(jnp.sum(results[3], axis=0))])
    grad_up = jnp.stack([lax.optimization_barrier(jnp.sum(results[2], axis=0)), lax.optimization_barrier(jnp.sum(results[4], axis=0))])
    return (results[0], grad_down, grad_up)
```

```python
import jax
import jax.numpy as jnp
from jax import lax
from jax.experimental import pallas as pl
from jax.experimental.pallas import tpu as pltpu
from jax.sharding import PartitionSpec as P

HEADS = 12
HD = 128
CH = 64
RANK = 64
NSTEPS = 1000
IMG = 256
TXT = 128
ROWS = TXT + IMG
HW = HEADS * HD
CHUNK = 512
BF = jnp.bfloat16
F32 = jnp.float32
SCALE = HD ** (-0.5)


def dot(left, right, left_dim=1, right_dim=0):
    dims = (((left_dim,), (right_dim,)), ((), ()))
    return lax.dot_general(left, right, dims, preferred_element_type=F32)


def high_low(values):
    high = values.astype(BF)
    return high, (values - high.astype(F32)).astype(BF)


def forward_kernel(
    flag_ref,
    sigma_ref,
    latent_ref,
    fresh_ref,
    prompt_ref,
    latent_in_ref,
    modulation_ref,
    velocity_out_ref,
    fold_ref,
    text_ref,
    gen_down_ref,
    gen_up_ref,
    role_down_ref,
    role_up_ref,
    sample_ref,
    velocity_ref,
    q_ref,
    k_ref,
    v_ref,
    weights_ref,
    inverse_ref,
    attended_ref,
    reduced_ref,
    picture_ref,
    stacked,
    q_now,
    k_now,
    v_now,
    attended_now,
):
    flag = flag_ref[0, 0]
    sigma = sigma_ref[0, 0]

    def readout(latent, noise_level, down_ref, up_ref, switch, save):
        narrow = latent.astype(BF)
        hidden = dot(narrow, latent_in_ref[...])
        inverse_rms = lax.rsqrt(jnp.mean(hidden * hidden, axis=-1, keepdims=True) + 1e-06)
        picture = (hidden * inverse_rms * (1.0 + noise_level * modulation_ref[...])).astype(BF)
        reduced_picture = dot(picture, down_ref[...]).astype(BF)
        reduced_prompt = dot(prompt_ref[...], down_ref[:, RANK:]).astype(BF)

        @save
        def _():
            picture_ref[...] = picture
            reduced_ref[TXT:, :] = reduced_picture
            reduced_ref[:TXT, :RANK] = jnp.zeros((TXT, RANK), BF)
            reduced_ref[:TXT, RANK:] = reduced_prompt

        if switch is not None:
            reduced_picture = reduced_picture * switch.astype(BF)
            reduced_prompt = reduced_prompt * switch.astype(BF)
        scaled_high, scaled_low = high_low(narrow.astype(F32) * inverse_rms)
        for block, now in enumerate((q_now, k_now, v_now)):
            rank_span = slice(block * RANK, (block + 1) * RANK)
            left = jnp.concatenate(
                [scaled_high, scaled_low, scaled_high, reduced_picture[:, rank_span]], axis=1
            )
            for start in range(0, HW, CHUNK):
                own = slice(start, start + CHUNK)
                wide = slice(block * HW + start, block * HW + start + CHUNK)
                fold = fold_ref[:CH, wide] + noise_level * fold_ref[CH:, wide]
                fold_high, fold_low = high_low(fold)
                stacked[:CH, :] = fold_high
                stacked[CH : 2 * CH, :] = fold_high
                stacked[2 * CH : 3 * CH, :] = fold_low
                stacked[3 * CH :, :] = up_ref[rank_span, own]
                picture_part = dot(left, stacked[...]).astype(BF)
                if block == 0:
                    now[:, own] = picture_part
                else:
                    now[TXT:, own] = picture_part
                    prompt_span = slice((block - 1) * RANK, block * RANK)
                    text_span = slice((block - 1) * HW + start, (block - 1) * HW + start + CHUNK)
                    adapter = dot(reduced_prompt[:, prompt_span], up_ref[rank_span, own])
                    now[:TXT, own] = (text_ref[:, text_span] + adapter).astype(BF)

        def head(index, carry):
            span = pl.ds(pl.multiple_of(index * HD, HD), HD)
            queries, keys, values = q_now[:, span], k_now[:, span], v_now[:, span]
            scores = dot(queries, keys, 1, 1) * SCALE
            largest = jnp.max(scores, axis=-1, keepdims=True)
            weights = jnp.exp(scores - largest)
            inverse = 1.0 / jnp.sum(weights, axis=-1, keepdims=True)
            weights = weights.astype(BF)
            attended = (dot(weights, values) * inverse).astype(BF)
            attended_now[:, span] = attended

            @save
            def _():
                q_ref[:, span] = queries
                k_ref[:, span] = keys
                v_ref[:, span] = values
                attended_ref[:, span] = attended
                weights_ref[index] = weights
                inverse_ref[index] = inverse

            return carry

        lax.fori_loop(0, HEADS, head, 0, unroll=2)
        return dot(attended_now[...], velocity_out_ref[...])

    latent = latent_ref[...]
    sample = latent - readout(latent, 1.0, gen_down_ref, gen_up_ref, None, lambda f: f())
    sample_ref[...] = sample
    noised = (1.0 - sigma) * sample + sigma * fresh_ref[...]
    velocity_ref[...] = readout(
        noised, sigma, role_down_ref, role_up_ref, flag.astype(F32), pl.when(flag == 1)
    )


def backward_kernel(
    flag_ref,
    sigma_ref,
    sample_ref,
    fresh_ref,
    own_ref,
    fake_ref,
    prompt_ref,
    velocity_out_ref,
    role_up_ref,
    q_ref,
    k_ref,
    v_ref,
    weights_ref,
    inverse_ref,
    attended_ref,
    reduced_ref,
    picture_ref,
    grads_ref,
    grad_q,
    grad_k,
    grad_v,
):
    flag = flag_ref[0, 0]
    sigma = sigma_ref[0, 0]
    sample = sample_ref[...]
    own = own_ref[...]
    noised = (1.0 - sigma) * sample + sigma * fresh_ref[...]
    clean_real = noised - sigma * own
    clean_fake = noised - sigma * fake_ref[...].astype(F32)
    distance = jnp.sum(jnp.sum(jnp.abs(sample - clean_real), axis=1, keepdims=True), axis=0, keepdims=True)
    spread = distance * (1.0 / (IMG * CH)) + 1e-05
    cot_gen = -(clean_fake - clean_real) / spread
    cot_critic = 2.0 * (own - (fresh_ref[...] - sample)) / (IMG * CH)
    cotangent = jnp.where(flag == 0, cot_gen, cot_critic).astype(BF)

    def head(index, carry):
        span = pl.ds(pl.multiple_of(index * HD, HD), HD)
        queries, keys, values = q_ref[:, span], k_ref[:, span], v_ref[:, span]
        weights = weights_ref[index]
        upstream = dot(cotangent, velocity_out_ref[span, :], 1, 1) * inverse_ref[index]
        inner = jnp.sum(upstream * attended_ref[:, span].astype(F32), axis=-1, keepdims=True)
        upstream = upstream.astype(BF)
        grad_v[:, span] = dot(weights, upstream, 0, 0).astype(BF)
        grad_weights = dot(upstream, values, 1, 1)
        grad_scores = (weights.astype(F32) * (grad_weights - inner) * SCALE).astype(BF)
        grad_q[:, span] = dot(grad_scores, keys).astype(BF)
        grad_k[:, span] = dot(grad_scores, queries, 0, 0).astype(BF)
        return carry

    lax.fori_loop(0, HEADS, head, 0, unroll=2)
    spans = [slice(block * RANK, (block + 1) * RANK) for block in range(3)]
    reduced_q = dot(grad_q[...], role_up_ref[spans[0], :], 1, 1).astype(BF)
    reduced_k = dot(grad_k[...], role_up_ref[spans[1], :], 1, 1).astype(BF)
    reduced_v = dot(grad_v[...], role_up_ref[spans[2], :], 1, 1).astype(BF)
    reduced_kv = jnp.concatenate([reduced_k, reduced_v], axis=1)
    down_q = dot(reduced_q, picture_ref[...], 0, 0)
    down_kv = dot(reduced_kv[:TXT], prompt_ref[...], 0, 0) + dot(reduced_kv[TXT:], picture_ref[...], 0, 0)
    up_q = dot(reduced_ref[TXT:, spans[0]], grad_q[...], 0, 0)
    up_k = dot(reduced_ref[:, spans[1]], grad_k[...], 0, 0)
    up_v = dot(reduced_ref[:, spans[2]], grad_v[...], 0, 0)
    grads = jnp.concatenate([down_q, down_kv, up_q, up_k, up_v], axis=0)
    grads_ref[...] = grads.T.astype(BF)


def vmem():
    return pl.BlockSpec(memory_space=pltpu.VMEM)


def smem():
    return pl.BlockSpec(memory_space=pltpu.SMEM)


def run_forward(*operands):
    shape = jax.ShapeDtypeStruct
    return pl.pallas_call(
        forward_kernel,
        out_shape=(
            shape((IMG, CH), F32),
            shape((IMG, CH), F32),
            shape((IMG, HW), BF),
            shape((ROWS, HW), BF),
            shape((ROWS, HW), BF),
            shape((HEADS, IMG, ROWS), BF),
            shape((HEADS, IMG, 1), F32),
            shape((IMG, HW), BF),
            shape((ROWS, 3 * RANK), BF),
            shape((IMG, HW), BF),
        ),
        in_specs=[smem()] * 2 + [vmem()] * (len(operands) - 2),
        out_specs=tuple([vmem()] * 10),
        scratch_shapes=[
            pltpu.VMEM((4 * CH, CHUNK), BF),
            pltpu.VMEM((IMG, HW), BF),
            pltpu.VMEM((ROWS, HW), BF),
            pltpu.VMEM((ROWS, HW), BF),
            pltpu.VMEM((IMG, HW), BF),
        ],
        compiler_params=pltpu.CompilerParams(vmem_limit_bytes=48 * 2**20),
        name="forward",
    )(*operands)


def run_backward(*operands):
    return pl.pallas_call(
        backward_kernel,
        out_shape=jax.ShapeDtypeStruct((HW, 6 * RANK), BF),
        in_specs=[smem()] * 2 + [vmem()] * (len(operands) - 2),
        out_specs=vmem(),
        scratch_shapes=[
            pltpu.VMEM((IMG, HW), BF),
            pltpu.VMEM((ROWS, HW), BF),
            pltpu.VMEM((ROWS, HW), BF),
        ],
        compiler_params=pltpu.CompilerParams(vmem_limit_bytes=48 * 2**20),
        name="backward",
    )(*operands)


def per_device(
    latent_noise,
    fresh_noise,
    text_states,
    step_index,
    base_qkv,
    latent_in,
    modulation,
    velocity_out,
    gen_down,
    gen_up,
    critic_down,
    critic_up,
):
    devices = lax.axis_size("fsdp")
    group_index = lax.axis_index("group")
    leading = group_index == 0
    flag = group_index.astype(jnp.int32).reshape(1, 1)
    sigma = ((step_index + 1).astype(F32) / NSTEPS).reshape(1, 1)
    shard = base_qkv.shape[0]

    weights = lax.all_gather(base_qkv, "fsdp", axis=0, tiled=True)
    role_down = jnp.where(leading, gen_down, critic_down)
    role_up = jnp.where(leading, gen_up, critic_up)
    rows = jnp.concatenate(
        [
            gen_down,
            role_down,
            gen_up.reshape(3 * RANK, shard).T,
            role_up.reshape(3 * RANK, shard).T,
        ],
        axis=1,
    )
    adapters = lax.all_to_all(jnp.broadcast_to(rows[None], (devices,) + rows.shape), "fsdp", 0, 0)
    adapters = adapters.reshape(devices * shard, 12 * RANK)
    gen_down_full = adapters[:, : 3 * RANK]
    role_down_full = adapters[:, 3 * RANK : 6 * RANK]
    ups = adapters[:, 6 * RANK :].T
    gen_up_full, role_up_full = ups[: 3 * RANK], ups[3 * RANK :]

    states = text_states[0].astype(F32)
    prompt = (
        states * lax.rsqrt(jnp.mean(states * states, axis=-1, keepdims=True) + 1e-06)
    ).astype(BF)
    scaled_in = (latent_in.astype(F32) * modulation).astype(BF)
    fold = dot(jnp.concatenate([latent_in, scaled_in], axis=0), weights)
    text = dot(prompt, weights[:, HW:])

    sample, own_velocity, *saved = run_forward(
        flag,
        sigma,
        latent_noise[0],
        fresh_noise[0],
        prompt,
        latent_in,
        modulation.reshape(1, HW),
        velocity_out,
        fold,
        text,
        gen_down_full,
        gen_up_full,
        role_down_full,
        role_up_full,
    )
    fake_velocity = lax.ppermute(own_velocity.astype(BF), "group", [(1, 0)])
    grads = run_backward(
        flag,
        sigma,
        sample,
        fresh_noise[0],
        own_velocity,
        fake_velocity,
        prompt,
        velocity_out,
        role_up_full,
        *saved,
    )
    shares = lax.all_to_all(grads.reshape(devices, shard, 6 * RANK), "fsdp", 0, 0)
    share = jnp.sum(shares.astype(F32), axis=0)
    share_down = share[:, : 3 * RANK]
    share_up = share[:, 3 * RANK :].T.reshape(3, RANK, shard)
    return (sample[None], share_down[None], share_up[None])


def solution(mesh):
    in_specs = (
        P("fsdp", None, None),
        P("fsdp", None, None),
        P("fsdp", None, None),
        P("fsdp"),
        P("fsdp", None),
        P(),
        P(),
        P(),
        P("fsdp", None),
        P(None, None, "fsdp"),
        P("fsdp", None),
        P(None, None, "fsdp"),
    )
    out_specs = (P("fsdp", None, None), P("group", "fsdp", None), P("group", None, None, "fsdp"))
    return jax.shard_map(
        per_device, mesh=mesh, in_specs=in_specs, out_specs=out_specs, check_vma=False
    )
```

```python
import jax
import jax.numpy as jnp
from jax import lax
from jax.experimental import pallas as pl
from jax.experimental.pallas import tpu as pltpu
from jax.sharding import PartitionSpec as P

HEADS = 12
HD = 128
CH = 64
RANK = 64
NSTEPS = 1000
IMG = 256
TXT = 128
ROWS = TXT + IMG
HW = HEADS * HD
CHUNK = 512
QUARTER = HW // 2
SIDE = 6 * RANK
SHARE = 72
PART = 128
BF = jnp.bfloat16
F32 = jnp.float32
SCALE = HD ** (-0.5)


def dot(left, right, left_dim=1, right_dim=0):
    dims = (((left_dim,), (right_dim,)), ((), ()))
    return lax.dot_general(left, right, dims, preferred_element_type=F32)


def high_low(values):
    high = values.astype(BF)
    return high, (values - high.astype(F32)).astype(BF)


def unit_rows(values):
    values = values.astype(F32)
    return (values * lax.rsqrt(jnp.mean(values * values, axis=-1, keepdims=True) + 1e-06)).astype(BF)


def pack_kernel(
    place_ref, base_ref, gen_down_ref, gen_up_ref, critic_down_ref, critic_up_ref, packed_ref, pair
):
    group = place_ref[0]

    def both(gen_ref, critic_ref):
        gen, critic = gen_ref[...].astype(F32), critic_ref[...].astype(F32)
        return jnp.concatenate([gen, jnp.where(group == 0, gen, critic)], axis=1).astype(BF)

    for core, side in enumerate(
        (both(gen_down_ref, critic_down_ref), both(gen_up_ref, critic_up_ref))
    ):
        start = pl.multiple_of(HW + group * HW + core * QUARTER, QUARTER)
        pair[core, :, :QUARTER] = base_ref[:, pl.ds(start, QUARTER)]
        pair[core, :, QUARTER:] = side
    rows = base_ref.shape[0]
    for device in range(packed_ref.shape[0]):
        packed_ref[device, :, : QUARTER + SIDE] = pair[device % 2]
        columns = base_ref[:, device * SHARE : (device + 1) * SHARE]
        packed_ref[device, :, QUARTER + SIDE :] = jnp.concatenate(
            [columns, jnp.zeros((rows, PART - SHARE), BF)], axis=1
        )


def mix_kernel(
    text_ref,
    other_text_ref,
    latent_in_ref,
    modulation_ref,
    packed_ref,
    prompt_ref,
    own_ref,
    other_ref,
    share_ref,
    side_ref,
):
    prompt = unit_rows(text_ref[...])
    prompt_ref[...] = prompt
    side_ref[...] = packed_ref[:, QUARTER : QUARTER + SIDE]
    prompts = jnp.concatenate([prompt, unit_rows(other_text_ref[...])], axis=0)
    quarter = dot(prompts, packed_ref[:, :QUARTER]).astype(BF)
    own_ref[...] = quarter[:TXT]
    other_ref[...] = quarter[TXT:]
    scaled_in = (latent_in_ref[...].astype(F32) * modulation_ref[...]).astype(BF)
    folds = jnp.concatenate([latent_in_ref[...], scaled_in], axis=0)
    share = dot(folds, packed_ref[:, QUARTER + SIDE :]).T[:SHARE].astype(BF)
    for device in range(share_ref.shape[0]):
        share_ref[device] = share


def forward_kernel(
    place_ref,
    sigma_ref,
    latent_ref,
    fresh_ref,
    prompt_ref,
    latent_in_ref,
    modulation_ref,
    velocity_out_ref,
    fold_ref,
    text_own_ref,
    text_core_ref,
    text_group_ref,
    text_both_ref,
    side_own_ref,
    side_core_ref,
    sample_ref,
    velocity_ref,
    narrow_velocity_ref,
    q_ref,
    k_ref,
    v_ref,
    weights_ref,
    inverse_ref,
    attended_ref,
    reduced_ref,
    picture_ref,
    role_up_ref,
    stacked,
    q_now,
    k_now,
    v_now,
    attended_now,
    text,
    downs,
    ups,
):
    group, core = place_ref[0], place_ref[1]
    sigma = sigma_ref[0, 0]
    for part_ref, part_group, part_core in (
        (text_own_ref, group, core),
        (text_core_ref, group, 1 - core),
        (text_group_ref, 1 - group, core),
        (text_both_ref, 1 - group, 1 - core),
    ):
        start = pl.multiple_of(part_group * HW + part_core * QUARTER, QUARTER)
        text[:, pl.ds(start, QUARTER)] = part_ref[...]

    @pl.when(core == 0)
    def _():
        downs[...] = side_own_ref[...]
        ups[...] = side_core_ref[...]

    @pl.when(core == 1)
    def _():
        downs[...] = side_core_ref[...]
        ups[...] = side_own_ref[...]

    role_up_ref[...] = ups[:, 3 * RANK :]

    def readout(latent, noise_level, role, switch, save):
        base = role * 3 * RANK
        narrow = latent.astype(BF)
        hidden = dot(narrow, latent_in_ref[...])
        inverse_rms = lax.rsqrt(jnp.mean(hidden * hidden, axis=-1, keepdims=True) + 1e-06)
        picture = (hidden * inverse_rms * (1.0 + noise_level * modulation_ref[...])).astype(BF)
        reduced_picture = dot(picture, downs[:, base : base + 3 * RANK]).astype(BF)
        reduced_prompt = dot(prompt_ref[...], downs[:, base : base + 3 * RANK]).astype(BF)

        @save
        def _():
            picture_ref[...] = picture
            reduced_ref[TXT:, :] = reduced_picture
            reduced_ref[:TXT, :] = reduced_prompt

        if switch is not None:
            reduced_picture = reduced_picture * switch.astype(BF)
            reduced_prompt = reduced_prompt * switch.astype(BF)
        scaled_high, scaled_low = high_low(narrow.astype(F32) * inverse_rms)
        for block, now in enumerate((q_now, k_now, v_now)):
            rank_span = slice(block * RANK, (block + 1) * RANK)
            up_span = slice(base + block * RANK, base + (block + 1) * RANK)
            left = jnp.concatenate(
                [scaled_high, scaled_low, scaled_high, reduced_picture[:, rank_span]], axis=1
            )
            for start in range(0, HW, CHUNK):
                own = slice(start, start + CHUNK)
                wide = slice(block * HW + start, block * HW + start + CHUNK)
                parts = fold_ref[wide, :].astype(F32)
                fold_high, fold_low = high_low(parts[:, :CH] + noise_level * parts[:, CH:])
                up = ups[own, up_span]
                stacked[...] = jnp.concatenate([fold_high, fold_high, fold_low, up], axis=1)
                picture_part = dot(left, stacked[...], 1, 1).astype(BF)
                if block == 0:
                    now[:, own] = picture_part
                else:
                    now[TXT:, own] = picture_part
                    text_span = slice((block - 1) * HW + start, (block - 1) * HW + start + CHUNK)
                    adapter = dot(reduced_prompt[:, rank_span], up, 1, 1)
                    now[:TXT, own] = (text[:, text_span].astype(F32) + adapter).astype(BF)

        def head(index, carry):
            span = pl.ds(pl.multiple_of(index * HD, HD), HD)
            queries, keys, values = q_now[:, span], k_now[:, span], v_now[:, span]
            scores = dot(queries, keys, 1, 1) * SCALE
            largest = jnp.max(scores, axis=-1, keepdims=True)
            weights = jnp.exp(scores - largest)
            inverse = 1.0 / jnp.sum(weights, axis=-1, keepdims=True)
            weights = weights.astype(BF)
            attended = (dot(weights, values) * inverse).astype(BF)
            attended_now[:, span] = attended

            @save
            def _():
                q_ref[:, span] = queries
                k_ref[:, span] = keys
                v_ref[:, span] = values
                attended_ref[:, span] = attended
                weights_ref[index] = weights
                inverse_ref[index] = inverse

            return carry

        lax.fori_loop(0, HEADS, head, 0, unroll=2)
        return dot(attended_now[...], velocity_out_ref[...])

    latent = latent_ref[...]
    sample = latent - readout(latent, 1.0, 0, None, lambda f: f())
    sample_ref[...] = sample
    noised = (1.0 - sigma) * sample + sigma * fresh_ref[...]
    velocity = readout(noised, sigma, 1, group.astype(F32), pl.when(group == 1))
    velocity_ref[...] = velocity
    narrow_velocity_ref[...] = velocity.astype(BF)


def backward_kernel(
    place_ref,
    sigma_ref,
    sample_ref,
    fresh_ref,
    own_ref,
    fake_ref,
    prompt_ref,
    velocity_out_ref,
    role_up_ref,
    q_ref,
    k_ref,
    v_ref,
    weights_ref,
    inverse_ref,
    attended_ref,
    reduced_ref,
    picture_ref,
    grads_ref,
    grad_q,
    grad_k,
    grad_v,
):
    flag = place_ref[0]
    sigma = sigma_ref[0, 0]
    sample = sample_ref[...]
    own = own_ref[...]
    noised = (1.0 - sigma) * sample + sigma * fresh_ref[...]
    clean_real = noised - sigma * own
    clean_fake = noised - sigma * fake_ref[...].astype(F32)
    distance = jnp.sum(jnp.sum(jnp.abs(sample - clean_real), axis=1, keepdims=True), axis=0, keepdims=True)
    spread = distance * (1.0 / (IMG * CH)) + 1e-05
    cot_gen = -(clean_fake - clean_real) / spread
    cot_critic = 2.0 * (own - (fresh_ref[...] - sample)) / (IMG * CH)
    cotangent = jnp.where(flag == 0, cot_gen, cot_critic).astype(BF)

    def head(index, carry):
        span = pl.ds(pl.multiple_of(index * HD, HD), HD)
        queries, keys, values = q_ref[:, span], k_ref[:, span], v_ref[:, span]
        weights = weights_ref[index]
        upstream = dot(cotangent, velocity_out_ref[span, :], 1, 1) * inverse_ref[index]
        inner = jnp.sum(upstream * attended_ref[:, span].astype(F32), axis=-1, keepdims=True)
        upstream = upstream.astype(BF)
        grad_v[:, span] = dot(weights, upstream, 0, 0).astype(BF)
        grad_weights = dot(upstream, values, 1, 1)
        grad_scores = (weights.astype(F32) * (grad_weights - inner) * SCALE).astype(BF)
        grad_q[:, span] = dot(grad_scores, keys).astype(BF)
        grad_k[:, span] = dot(grad_scores, queries, 0, 0).astype(BF)
        return carry

    lax.fori_loop(0, HEADS, head, 0, unroll=2)
    spans = [slice(block * RANK, (block + 1) * RANK) for block in range(3)]
    reduced_q = dot(grad_q[...], role_up_ref[:, spans[0]]).astype(BF)
    reduced_k = dot(grad_k[...], role_up_ref[:, spans[1]]).astype(BF)
    reduced_v = dot(grad_v[...], role_up_ref[:, spans[2]]).astype(BF)
    reduced_kv = jnp.concatenate([reduced_k, reduced_v], axis=1)
    down_q = dot(reduced_q, picture_ref[...], 0, 0)
    down_kv = dot(reduced_kv[:TXT], prompt_ref[...], 0, 0) + dot(reduced_kv[TXT:], picture_ref[...], 0, 0)
    up_q = dot(reduced_ref[TXT:, spans[0]], grad_q[...], 0, 0)
    up_k = dot(reduced_ref[:, spans[1]], grad_k[...], 0, 0)
    up_v = dot(reduced_ref[:, spans[2]], grad_v[...], 0, 0)
    grads = jnp.concatenate([down_q, down_kv, up_q, up_k, up_v], axis=0)
    grads_ref[...] = grads.T.astype(BF)


def vmem():
    return pl.BlockSpec(memory_space=pltpu.VMEM)


def smem():
    return pl.BlockSpec(memory_space=pltpu.SMEM)


def run(kernel, name, scalars, outputs, scratch, *operands):
    shapes = tuple(jax.ShapeDtypeStruct(*output) for output in outputs)
    return pl.pallas_call(
        kernel,
        out_shape=shapes,
        in_specs=[smem()] * scalars + [vmem()] * (len(operands) - scalars),
        out_specs=tuple([vmem()] * len(outputs)),
        scratch_shapes=[pltpu.VMEM(*buffer) for buffer in scratch],
        compiler_params=pltpu.CompilerParams(vmem_limit_bytes=48 * 2**20),
        name=name,
    )(*operands)


def per_device(
    latent_noise,
    fresh_noise,
    text_states,
    step_index,
    base_qkv,
    latent_in,
    modulation,
    velocity_out,
    gen_down,
    gen_up,
    critic_down,
    critic_up,
):
    devices = lax.axis_size("fsdp")
    group = lax.axis_index("group")
    core = lax.rem(lax.axis_index("fsdp"), 2)
    place = jnp.stack([group, core]).astype(jnp.int32)
    sigma = ((step_index + 1).astype(F32) / NSTEPS).reshape(1, 1)
    shard = base_qkv.shape[0]
    cores = [(device, device ^ 1) for device in range(devices)]
    both = [
        (g * devices + device, (1 - g) * devices + (device ^ 1))
        for g in range(2)
        for device in range(devices)
    ]
    fresh = fresh_noise[0]
    text = text_states[0]
    gain = modulation.reshape(1, HW)

    other_text = lax.ppermute(text, "fsdp", cores)
    (packed,) = run(
        pack_kernel,
        "pack",
        1,
        [((devices, shard, QUARTER + SIDE + PART), BF)],
        [((2, shard, QUARTER + SIDE), BF)],
        place,
        base_qkv,
        gen_down,
        gen_up.reshape(3 * RANK, shard).T,
        critic_down,
        critic_up.reshape(3 * RANK, shard).T,
    )
    packed = lax.all_to_all(packed, "fsdp", 0, 0).reshape(HW, QUARTER + SIDE + PART)
    prompt, text_own, text_other, share, side_own = run(
        mix_kernel,
        "mix",
        0,
        [
            ((TXT, HW), BF),
            ((TXT, QUARTER), BF),
            ((TXT, QUARTER), BF),
            ((devices, SHARE, PART), BF),
            ((HW, SIDE), BF),
        ],
        [],
        text,
        other_text,
        latent_in,
        gain,
        packed,
    )
    text_core = lax.ppermute(text_other, "fsdp", cores)
    text_group = lax.ppermute(text_own, "group", [(0, 1), (1, 0)])
    text_both = lax.ppermute(text_other, ("group", "fsdp"), both)
    side_core = lax.ppermute(side_own, "fsdp", cores)
    fold = lax.all_to_all(share, "fsdp", 0, 0).reshape(devices * SHARE, PART)

    sample, velocity, narrow_velocity, *saved, role_up = run(
        forward_kernel,
        "forward",
        2,
        [
            ((IMG, CH), F32),
            ((IMG, CH), F32),
            ((IMG, CH), BF),
            ((IMG, HW), BF),
            ((ROWS, HW), BF),
            ((ROWS, HW), BF),
            ((HEADS, IMG, ROWS), BF),
            ((HEADS, IMG, 1), F32),
            ((IMG, HW), BF),
            ((ROWS, 3 * RANK), BF),
            ((IMG, HW), BF),
            ((HW, 3 * RANK), BF),
        ],
        [
            ((CHUNK, 4 * CH), BF),
            ((IMG, HW), BF),
            ((ROWS, HW), BF),
            ((ROWS, HW), BF),
            ((IMG, HW), BF),
            ((TXT, 2 * HW), BF),
            ((HW, SIDE), BF),
            ((HW, SIDE), BF),
        ],
        place,
        sigma,
        latent_noise[0],
        fresh,
        prompt,
        latent_in,
        gain,
        velocity_out,
        fold,
        text_own,
        text_core,
        text_group,
        text_both,
        side_own,
        side_core,
    )
    fake_velocity = lax.ppermute(narrow_velocity, "group", [(1, 0)])
    (grads,) = run(
        backward_kernel,
        "backward",
        2,
        [((HW, SIDE), BF)],
        [((IMG, HW), BF), ((ROWS, HW), BF), ((ROWS, HW), BF)],
        place,
        sigma,
        sample,
        fresh,
        velocity,
        fake_velocity,
        prompt,
        velocity_out,
        role_up,
        *saved,
    )
    shares = lax.all_to_all(grads.reshape(devices, shard, SIDE), "fsdp", 0, 0)
    total = jnp.sum(shares.astype(F32), axis=0)
    share_down = total[:, : 3 * RANK]
    share_up = total[:, 3 * RANK :].T.reshape(3, RANK, shard)
    return (sample[None], share_down[None], share_up[None])


def solution(mesh):
    in_specs = (
        P("fsdp", None, None),
        P("fsdp", None, None),
        P("fsdp", None, None),
        P("fsdp"),
        P("fsdp", None),
        P(),
        P(),
        P(),
        P("fsdp", None),
        P(None, None, "fsdp"),
        P("fsdp", None),
        P(None, None, "fsdp"),
    )
    out_specs = (P("fsdp", None, None), P("group", "fsdp", None), P("group", None, None, "fsdp"))
    return jax.shard_map(
        per_device, mesh=mesh, in_specs=in_specs, out_specs=out_specs, check_vma=False
    )
```

```python
import jax
import jax.numpy as jnp
from jax import lax
from jax.experimental import pallas as pl
from jax.experimental.pallas import tpu as pltpu
from jax.sharding import PartitionSpec as P

HEADS = 12
HD = 128
CH = 64
RANK = 64
NSTEPS = 1000
IMG = 256
TXT = 128
ROWS = TXT + IMG
HW = HEADS * HD
CHUNK = 512
EIGHTH = HW // 4
SIDE = 6 * RANK
SHARE = 72
PART = 128
MOVES = tuple((group, near) for group in range(2) for near in range(4))
BF = jnp.bfloat16
F32 = jnp.float32
SCALE = HD ** (-0.5)


def dot(left, right, left_dim=1, right_dim=0):
    dims = (((left_dim,), (right_dim,)), ((), ()))
    return lax.dot_general(left, right, dims, preferred_element_type=F32)


def high_low(values):
    high = values.astype(BF)
    return high, (values - high.astype(F32)).astype(BF)


def unit_rows(values):
    values = values.astype(F32)
    return (values * lax.rsqrt(jnp.mean(values * values, axis=-1, keepdims=True) + 1e-06)).astype(BF)


def pack_kernel(
    place_ref,
    base_ref,
    gen_down_ref,
    gen_up_ref,
    critic_down_ref,
    critic_up_ref,
    packed_ref,
):
    group = place_ref[0]

    def both(gen, critic):
        gen, critic = gen.astype(F32), critic.astype(F32)
        return jnp.concatenate([gen, jnp.where(group == 0, gen, critic)], axis=1).astype(BF)

    sides = (
        both(gen_down_ref[...], critic_down_ref[...]),
        both(gen_up_ref[...].T, critic_up_ref[...].T),
    )
    rows = base_ref.shape[0]
    for near in range(4):
        start = pl.multiple_of(HW + group * HW + near * EIGHTH, EIGHTH)
        eighth = base_ref[:, pl.ds(start, EIGHTH)]
        for device in range(near, packed_ref.shape[0], 4):
            packed_ref[device, :, :EIGHTH] = eighth
            packed_ref[device, :, EIGHTH : EIGHTH + SIDE] = sides[near % 2]
            columns = base_ref[:, device * SHARE : (device + 1) * SHARE]
            packed_ref[device, :, EIGHTH + SIDE :] = jnp.concatenate(
                [columns, jnp.zeros((rows, PART - SHARE), BF)], axis=1
            )


def fold_kernel(latent_in_ref, modulation_ref, packed_ref, share_ref, side_ref):
    scaled_in = (latent_in_ref[...].astype(F32) * modulation_ref[...]).astype(BF)
    folds = jnp.concatenate([latent_in_ref[...], scaled_in], axis=0)
    share = dot(folds, packed_ref[:, EIGHTH + SIDE :]).T[:SHARE].astype(BF)
    for device in range(share_ref.shape[0]):
        share_ref[device] = share
    side_ref[...] = packed_ref[:, EIGHTH : EIGHTH + SIDE]


def mix_kernel(
    text_0_ref,
    text_1_ref,
    text_2_ref,
    text_3_ref,
    packed_ref,
    prompt_ref,
    out_0_ref,
    out_1_ref,
    out_2_ref,
    out_3_ref,
):
    prompt = unit_rows(text_0_ref[...])
    prompt_ref[...] = prompt
    out_0_ref[...] = dot(prompt, packed_ref[:, :EIGHTH]).astype(BF)
    for text_ref, out_ref in (
        (text_1_ref, out_1_ref),
        (text_2_ref, out_2_ref),
        (text_3_ref, out_3_ref),
    ):
        out_ref[...] = dot(unit_rows(text_ref[...]), packed_ref[:, :EIGHTH]).astype(BF)


def forward_kernel(
    place_ref,
    sigma_ref,
    latent_ref,
    fresh_ref,
    prompt_ref,
    latent_in_ref,
    modulation_ref,
    velocity_out_ref,
    fold_ref,
    text_0_ref,
    text_1_ref,
    text_2_ref,
    text_3_ref,
    text_4_ref,
    text_5_ref,
    text_6_ref,
    text_7_ref,
    side_own_ref,
    side_core_ref,
    sample_ref,
    velocity_ref,
    narrow_velocity_ref,
    q_ref,
    k_ref,
    v_ref,
    weights_ref,
    inverse_ref,
    attended_ref,
    reduced_ref,
    picture_ref,
    role_up_ref,
    stacked,
    q_now,
    k_now,
    v_now,
    attended_now,
    text,
    downs,
    ups,
):
    group, near, core = place_ref[0], place_ref[1], place_ref[2]
    sigma = sigma_ref[0, 0]
    text_refs = (
        text_0_ref,
        text_1_ref,
        text_2_ref,
        text_3_ref,
        text_4_ref,
        text_5_ref,
        text_6_ref,
        text_7_ref,
    )
    for (across, move), text_ref in zip(MOVES, text_refs):
        start = (group ^ across) * HW + (near ^ move) * EIGHTH
        text[:, pl.ds(pl.multiple_of(start, EIGHTH), EIGHTH)] = text_ref[...]

    @pl.when(core == 0)
    def _():
        downs[...] = side_own_ref[...]
        ups[...] = side_core_ref[...]

    @pl.when(core == 1)
    def _():
        downs[...] = side_core_ref[...]
        ups[...] = side_own_ref[...]

    role_up_ref[...] = ups[:, 3 * RANK :]

    def readout(latent, noise_level, role, switch, save):
        base = role * 3 * RANK
        narrow = latent.astype(BF)
        hidden = dot(narrow, latent_in_ref[...])
        inverse_rms = lax.rsqrt(jnp.mean(hidden * hidden, axis=-1, keepdims=True) + 1e-06)
        picture = (hidden * inverse_rms * (1.0 + noise_level * modulation_ref[...])).astype(BF)
        reduced_picture = dot(picture, downs[:, base : base + 3 * RANK]).astype(BF)
        reduced_prompt = dot(prompt_ref[...], downs[:, base : base + 3 * RANK]).astype(BF)

        @save
        def _():
            picture_ref[...] = picture
            reduced_ref[TXT:, :] = reduced_picture
            reduced_ref[:TXT, :] = reduced_prompt

        if switch is not None:
            reduced_picture = reduced_picture * switch.astype(BF)
            reduced_prompt = reduced_prompt * switch.astype(BF)
        scaled_high, scaled_low = high_low(narrow.astype(F32) * inverse_rms)
        for block, now in enumerate((q_now, k_now, v_now)):
            rank_span = slice(block * RANK, (block + 1) * RANK)
            up_span = slice(base + block * RANK, base + (block + 1) * RANK)
            left = jnp.concatenate(
                [scaled_high, scaled_low, scaled_high, reduced_picture[:, rank_span]], axis=1
            )
            for start in range(0, HW, CHUNK):
                own = slice(start, start + CHUNK)
                wide = slice(block * HW + start, block * HW + start + CHUNK)
                parts = fold_ref[wide, :].astype(F32)
                fold_high, fold_low = high_low(parts[:, :CH] + noise_level * parts[:, CH:])
                up = ups[own, up_span]
                stacked[...] = jnp.concatenate([fold_high, fold_high, fold_low, up], axis=1)
                picture_part = dot(left, stacked[...], 1, 1).astype(BF)
                if block == 0:
                    now[:, own] = picture_part
                else:
                    now[TXT:, own] = picture_part
                    text_span = slice((block - 1) * HW + start, (block - 1) * HW + start + CHUNK)
                    adapter = dot(reduced_prompt[:, rank_span], up, 1, 1)
                    now[:TXT, own] = (text[:, text_span].astype(F32) + adapter).astype(BF)

        def head(index, carry):
            span = pl.ds(pl.multiple_of(index * HD, HD), HD)
            queries, keys, values = q_now[:, span], k_now[:, span], v_now[:, span]
            scores = dot(queries, keys, 1, 1) * SCALE
            largest = jnp.max(scores, axis=-1, keepdims=True)
            weights = jnp.exp(scores - largest)
            inverse = 1.0 / jnp.sum(weights, axis=-1, keepdims=True)
            weights = weights.astype(BF)
            attended = (dot(weights, values) * inverse).astype(BF)
            attended_now[:, span] = attended

            @save
            def _():
                q_ref[:, span] = queries
                k_ref[:, span] = keys
                v_ref[:, span] = values
                attended_ref[:, span] = attended
                weights_ref[index] = weights
                inverse_ref[index] = inverse

            return carry

        lax.fori_loop(0, HEADS, head, 0, unroll=2)
        return dot(attended_now[...], velocity_out_ref[...])

    latent = latent_ref[...]
    sample = latent - readout(latent, 1.0, 0, None, lambda f: f())
    sample_ref[...] = sample
    noised = (1.0 - sigma) * sample + sigma * fresh_ref[...]
    velocity = readout(noised, sigma, 1, group.astype(F32), pl.when(group == 1))
    velocity_ref[...] = velocity
    narrow_velocity_ref[...] = velocity.astype(BF)


def backward_kernel(
    place_ref,
    sigma_ref,
    sample_ref,
    fresh_ref,
    own_ref,
    fake_ref,
    prompt_ref,
    velocity_out_ref,
    role_up_ref,
    q_ref,
    k_ref,
    v_ref,
    weights_ref,
    inverse_ref,
    attended_ref,
    reduced_ref,
    picture_ref,
    grads_ref,
    grad_q,
    grad_k,
    grad_v,
):
    flag = place_ref[0]
    sigma = sigma_ref[0, 0]
    sample = sample_ref[...]
    own = own_ref[...]
    noised = (1.0 - sigma) * sample + sigma * fresh_ref[...]
    clean_real = noised - sigma * own
    clean_fake = noised - sigma * fake_ref[...].astype(F32)
    distance = jnp.sum(jnp.sum(jnp.abs(sample - clean_real), axis=1, keepdims=True), axis=0, keepdims=True)
    spread = distance * (1.0 / (IMG * CH)) + 1e-05
    cot_gen = -(clean_fake - clean_real) / spread
    cot_critic = 2.0 * (own - (fresh_ref[...] - sample)) / (IMG * CH)
    cotangent = jnp.where(flag == 0, cot_gen, cot_critic).astype(BF)

    def head(index, carry):
        span = pl.ds(pl.multiple_of(index * HD, HD), HD)
        queries, keys, values = q_ref[:, span], k_ref[:, span], v_ref[:, span]
        weights = weights_ref[index]
        upstream = dot(cotangent, velocity_out_ref[span, :], 1, 1) * inverse_ref[index]
        inner = jnp.sum(upstream * attended_ref[:, span].astype(F32), axis=-1, keepdims=True)
        upstream = upstream.astype(BF)
        grad_v[:, span] = dot(weights, upstream, 0, 0).astype(BF)
        grad_weights = dot(upstream, values, 1, 1)
        grad_scores = (weights.astype(F32) * (grad_weights - inner) * SCALE).astype(BF)
        grad_q[:, span] = dot(grad_scores, keys).astype(BF)
        grad_k[:, span] = dot(grad_scores, queries, 0, 0).astype(BF)
        return carry

    lax.fori_loop(0, HEADS, head, 0, unroll=2)
    spans = [slice(block * RANK, (block + 1) * RANK) for block in range(3)]
    reduced_q = dot(grad_q[...], role_up_ref[:, spans[0]]).astype(BF)
    reduced_k = dot(grad_k[...], role_up_ref[:, spans[1]]).astype(BF)
    reduced_v = dot(grad_v[...], role_up_ref[:, spans[2]]).astype(BF)
    reduced_kv = jnp.concatenate([reduced_k, reduced_v], axis=1)
    down_q = dot(reduced_q, picture_ref[...], 0, 0)
    down_kv = dot(reduced_kv[:TXT], prompt_ref[...], 0, 0) + dot(reduced_kv[TXT:], picture_ref[...], 0, 0)
    up_q = dot(reduced_ref[TXT:, spans[0]], grad_q[...], 0, 0)
    up_k = dot(reduced_ref[:, spans[1]], grad_k[...], 0, 0)
    up_v = dot(reduced_ref[:, spans[2]], grad_v[...], 0, 0)
    grads = jnp.concatenate([down_q, down_kv, up_q, up_k, up_v], axis=0)
    grads_ref[...] = grads.T.astype(BF)


def vmem():
    return pl.BlockSpec(memory_space=pltpu.VMEM)


def smem():
    return pl.BlockSpec(memory_space=pltpu.SMEM)


def run(kernel, name, megabytes, scalars, outputs, scratch, *operands):
    shapes = tuple(jax.ShapeDtypeStruct(*output) for output in outputs)
    return pl.pallas_call(
        kernel,
        out_shape=shapes,
        in_specs=[smem()] * scalars + [vmem()] * (len(operands) - scalars),
        out_specs=tuple([vmem()] * len(outputs)),
        scratch_shapes=[pltpu.VMEM(*buffer) for buffer in scratch],
        compiler_params=pltpu.CompilerParams(vmem_limit_bytes=megabytes * 2**20),
        name=name,
    )(*operands)


def per_device(
    latent_noise,
    fresh_noise,
    text_states,
    step_index,
    base_qkv,
    latent_in,
    modulation,
    velocity_out,
    gen_down,
    gen_up,
    critic_down,
    critic_up,
):
    devices = lax.axis_size("fsdp")
    group = lax.axis_index("group")
    index = lax.axis_index("fsdp")
    place = jnp.stack([group, lax.rem(index, 4), lax.rem(index, 2)]).astype(jnp.int32)
    sigma = ((step_index + 1).astype(F32) / NSTEPS).reshape(1, 1)
    shard = base_qkv.shape[0]

    def move(array, across, near):
        pairs = [
            (g * devices + device, (g ^ across) * devices + (device ^ near))
            for g in range(2)
            for device in range(devices)
        ]
        return lax.ppermute(array, ("group", "fsdp"), pairs)

    fresh = fresh_noise[0]
    text = text_states[0]
    gain = modulation.reshape(1, HW)

    texts = [text, move(text, 0, 1), move(text, 1, 2), move(text, 1, 3)]
    (packed,) = run(
        pack_kernel,
        "pack",
        16,
        1,
        [((devices, shard, EIGHTH + SIDE + PART), BF)],
        [],
        place,
        base_qkv,
        gen_down,
        gen_up.reshape(3 * RANK, shard),
        critic_down,
        critic_up.reshape(3 * RANK, shard),
    )
    packed = lax.all_to_all(packed, "fsdp", 0, 0).reshape(HW, EIGHTH + SIDE + PART)
    packed, *texts = lax.optimization_barrier((packed, *texts))
    share, side_own = run(
        fold_kernel,
        "fold",
        16,
        0,
        [((devices, SHARE, PART), BF), ((HW, SIDE), BF)],
        [],
        latent_in,
        gain,
        packed,
    )
    fold = lax.all_to_all(share, "fsdp", 0, 0).reshape(devices * SHARE, PART)
    side_core = move(side_own, 0, 1)
    prompt, *parts = run(
        mix_kernel,
        "mix",
        16,
        0,
        [((TXT, HW), BF)] + [((TXT, EIGHTH), BF)] * 4,
        [],
        *texts,
        packed,
    )
    pieces = [
        parts[near] if (across, near) == (0, 0) else move(parts[near], across, near)
        for across, near in MOVES
    ]

    sample, velocity, narrow_velocity, *saved, role_up = run(
        forward_kernel,
        "forward",
        32,
        2,
        [
            ((IMG, CH), F32),
            ((IMG, CH), F32),
            ((IMG, CH), BF),
            ((IMG, HW), BF),
            ((ROWS, HW), BF),
            ((ROWS, HW), BF),
            ((HEADS, IMG, ROWS), BF),
            ((HEADS, IMG, 1), F32),
            ((IMG, HW), BF),
            ((ROWS, 3 * RANK), BF),
            ((IMG, HW), BF),
            ((HW, 3 * RANK), BF),
        ],
        [
            ((CHUNK, 4 * CH), BF),
            ((IMG, HW), BF),
            ((ROWS, HW), BF),
            ((ROWS, HW), BF),
            ((IMG, HW), BF),
            ((TXT, 2 * HW), BF),
            ((HW, SIDE), BF),
            ((HW, SIDE), BF),
        ],
        place,
        sigma,
        latent_noise[0],
        fresh,
        prompt,
        latent_in,
        gain,
        velocity_out,
        fold,
        *pieces,
        side_own,
        side_core,
    )
    fake_velocity = lax.ppermute(narrow_velocity, "group", [(1, 0)])
    (grads,) = run(
        backward_kernel,
        "backward",
        24,
        2,
        [((HW, SIDE), BF)],
        [((IMG, HW), BF), ((ROWS, HW), BF), ((ROWS, HW), BF)],
        place,
        sigma,
        sample,
        fresh,
        velocity,
        fake_velocity,
        prompt,
        velocity_out,
        role_up,
        *saved,
    )
    shares = lax.all_to_all(grads.reshape(devices, shard, SIDE), "fsdp", 0, 0)
    total = jnp.sum(shares.astype(F32), axis=0)
    share_down = total[:, : 3 * RANK]
    share_up = total[:, 3 * RANK :].T.reshape(3, RANK, shard)
    return (sample[None], share_down[None], share_up[None])


def solution(mesh):
    in_specs = (
        P("fsdp", None, None),
        P("fsdp", None, None),
        P("fsdp", None, None),
        P("fsdp"),
        P("fsdp", None),
        P(),
        P(),
        P(),
        P("fsdp", None),
        P(None, None, "fsdp"),
        P("fsdp", None),
        P(None, None, "fsdp"),
    )
    out_specs = (P("fsdp", None, None), P("group", "fsdp", None), P("group", None, None, "fsdp"))
    return jax.shard_map(
        per_device, mesh=mesh, in_specs=in_specs, out_specs=out_specs, check_vma=False
    )
```

```python
import jax
import jax.numpy as jnp
from jax import lax
from jax.experimental import pallas as pl
from jax.experimental.pallas import tpu as pltpu
from jax.sharding import PartitionSpec as P

HEADS = 12
HD = 128
CH = 64
RANK = 64
NSTEPS = 1000
IMG = 256
TXT = 128
ROWS = TXT + IMG
HW = HEADS * HD
CHUNK = 512
EIGHTH = HW // 4
SIDE = 6 * RANK
SHARE = 72
PART = 128
WRITES = 4
MOVES = tuple((group, near) for group in range(2) for near in range(4))
BF = jnp.bfloat16
F32 = jnp.float32
SCALE = HD ** (-0.5)


def dot(left, right, left_dim=1, right_dim=0):
    dims = (((left_dim,), (right_dim,)), ((), ()))
    return lax.dot_general(left, right, dims, preferred_element_type=F32)


def high_low(values):
    high = values.astype(BF)
    return high, (values - high.astype(F32)).astype(BF)


def unit_rows(values):
    values = values.astype(F32)
    return (values * lax.rsqrt(jnp.mean(values * values, axis=-1, keepdims=True) + 1e-06)).astype(BF)


def pack_kernel(
    place_ref,
    base_ref,
    gen_down_ref,
    critic_down_ref,
    gen_up_ref,
    critic_up_ref,
    packed_ref,
    base,
    downs,
    ups,
    packed,
    read_sem,
    write_sem,
):
    reads = [
        pltpu.make_async_copy(base_ref, base, read_sem.at[0]),
        pltpu.make_async_copy(gen_down_ref, downs.at[0], read_sem.at[1]),
        pltpu.make_async_copy(critic_down_ref, downs.at[1], read_sem.at[2]),
        pltpu.make_async_copy(gen_up_ref, ups.at[0], read_sem.at[3]),
        pltpu.make_async_copy(critic_up_ref, ups.at[1], read_sem.at[4]),
    ]
    for read in reads:
        read.start()
    for read in reads:
        read.wait()
    group = place_ref[0]

    def both(gen, critic):
        gen, critic = gen.astype(F32), critic.astype(F32)
        return jnp.concatenate([gen, jnp.where(group == 0, gen, critic)], axis=1).astype(BF)

    up_rows = [jnp.concatenate([ups[role, block] for block in range(3)], axis=1) for role in range(2)]
    sides = (both(downs[0], downs[1]), both(up_rows[0], up_rows[1]))
    eighths = []
    for near in range(4):
        start = pl.multiple_of(HW + group * HW + near * EIGHTH, EIGHTH)
        eighths.append(base[:, pl.ds(start, EIGHTH)])
    rows = base.shape[0]
    batch = packed.shape[0] // WRITES
    writes = []
    for step in range(WRITES):
        for device in range(step * batch, (step + 1) * batch):
            packed[device, :, :EIGHTH] = eighths[device % 4]
            packed[device, :, EIGHTH : EIGHTH + SIDE] = sides[device % 2]
            columns = base[:, device * SHARE : (device + 1) * SHARE]
            packed[device, :, EIGHTH + SIDE :] = jnp.concatenate(
                [columns, jnp.zeros((rows, PART - SHARE), BF)], axis=1
            )
        span = pl.ds(step * batch, batch)
        write = pltpu.make_async_copy(packed.at[span], packed_ref.at[span], write_sem.at[step])
        write.start()
        writes.append(write)
    for write in writes:
        write.wait()


def prompt_kernel(text_0_ref, text_1_ref, text_2_ref, text_3_ref, prompts_ref):
    for index, text_ref in enumerate((text_0_ref, text_1_ref, text_2_ref, text_3_ref)):
        prompts_ref[index * TXT : (index + 1) * TXT, :] = unit_rows(text_ref[...])


def sum_kernel(shares_ref, down_ref, up_ref):
    total = jnp.sum(shares_ref[...].astype(F32), axis=0)
    down_ref[...] = total[:, : 3 * RANK]
    for block in range(3):
        up_ref[block] = total[:, (3 + block) * RANK : (4 + block) * RANK]


def fold_kernel(latent_in_ref, modulation_ref, packed_ref, share_ref, side_ref):
    scaled_in = (latent_in_ref[...].astype(F32) * modulation_ref[...]).astype(BF)
    folds = jnp.concatenate([latent_in_ref[...], scaled_in], axis=0)
    share = dot(folds, packed_ref[:, EIGHTH + SIDE :]).T[:SHARE].astype(BF)
    for device in range(share_ref.shape[0]):
        share_ref[device] = share
    side_ref[...] = packed_ref[:, EIGHTH : EIGHTH + SIDE]


def mix_kernel(prompts_ref, packed_ref, out_0_ref, out_1_ref, out_2_ref, out_3_ref):
    eighth = dot(prompts_ref[...], packed_ref[:, :EIGHTH]).astype(BF)
    for index, out_ref in enumerate((out_0_ref, out_1_ref, out_2_ref, out_3_ref)):
        out_ref[...] = eighth[index * TXT : (index + 1) * TXT]


def forward_kernel(
    place_ref,
    sigma_ref,
    latent_ref,
    fresh_ref,
    prompt_ref,
    latent_in_ref,
    modulation_ref,
    velocity_out_ref,
    fold_ref,
    text_0_ref,
    text_1_ref,
    text_2_ref,
    text_3_ref,
    text_4_ref,
    text_5_ref,
    text_6_ref,
    text_7_ref,
    side_own_ref,
    side_core_ref,
    sample_ref,
    sample_again_ref,
    velocity_ref,
    narrow_velocity_ref,
    q_ref,
    k_ref,
    v_ref,
    weights_ref,
    inverse_ref,
    attended_ref,
    reduced_ref,
    picture_ref,
    role_up_ref,
    stacked,
    q_now,
    k_now,
    v_now,
    attended_now,
    text,
    downs,
    ups,
):
    group, near, core = place_ref[0], place_ref[1], place_ref[2]
    sigma = sigma_ref[0, 0]
    text_refs = (
        text_0_ref,
        text_1_ref,
        text_2_ref,
        text_3_ref,
        text_4_ref,
        text_5_ref,
        text_6_ref,
        text_7_ref,
    )
    for (across, move), text_ref in zip(MOVES, text_refs):
        start = (group ^ across) * HW + (near ^ move) * EIGHTH
        text[:, pl.ds(pl.multiple_of(start, EIGHTH), EIGHTH)] = text_ref[...]

    @pl.when(core == 0)
    def _():
        downs[...] = side_own_ref[...]
        ups[...] = side_core_ref[...]

    @pl.when(core == 1)
    def _():
        downs[...] = side_core_ref[...]
        ups[...] = side_own_ref[...]

    role_up_ref[...] = ups[:, 3 * RANK :]

    def readout(latent, noise_level, role, switch, save):
        base = role * 3 * RANK
        narrow = latent.T.astype(BF)
        hidden = dot(narrow, latent_in_ref[...])
        inverse_rms = lax.rsqrt(jnp.mean(hidden * hidden, axis=-1, keepdims=True) + 1e-06)
        picture = (hidden * inverse_rms * (1.0 + noise_level * modulation_ref[...])).astype(BF)
        reduced_picture = dot(picture, downs[:, base : base + 3 * RANK]).astype(BF)
        reduced_prompt = dot(prompt_ref[:TXT, :], downs[:, base : base + 3 * RANK]).astype(BF)

        @save
        def _():
            picture_ref[...] = picture
            reduced_ref[TXT:, :] = reduced_picture
            reduced_ref[:TXT, :] = reduced_prompt

        if switch is not None:
            reduced_picture = reduced_picture * switch.astype(BF)
            reduced_prompt = reduced_prompt * switch.astype(BF)
        scaled_high, scaled_low = high_low(narrow.astype(F32) * inverse_rms)
        for block, now in enumerate((q_now, k_now, v_now)):
            rank_span = slice(block * RANK, (block + 1) * RANK)
            up_span = slice(base + block * RANK, base + (block + 1) * RANK)
            left = jnp.concatenate(
                [scaled_high, scaled_low, scaled_high, reduced_picture[:, rank_span]], axis=1
            )
            for start in range(0, HW, CHUNK):
                own = slice(start, start + CHUNK)
                wide = slice(block * HW + start, block * HW + start + CHUNK)
                parts = fold_ref[wide, :].astype(F32)
                fold_high, fold_low = high_low(parts[:, :CH] + noise_level * parts[:, CH:])
                up = ups[own, up_span]
                stacked[...] = jnp.concatenate([fold_high, fold_high, fold_low, up], axis=1)
                picture_part = dot(left, stacked[...], 1, 1).astype(BF)
                if block == 0:
                    now[:, own] = picture_part
                else:
                    now[TXT:, own] = picture_part
                    text_span = slice((block - 1) * HW + start, (block - 1) * HW + start + CHUNK)
                    adapter = dot(reduced_prompt[:, rank_span], up, 1, 1)
                    now[:TXT, own] = (text[:, text_span].astype(F32) + adapter).astype(BF)

        def head(index, carry):
            span = pl.ds(pl.multiple_of(index * HD, HD), HD)
            queries, keys, values = q_now[:, span], k_now[:, span], v_now[:, span]
            scores = dot(queries, keys, 1, 1) * SCALE
            largest = jnp.max(scores, axis=-1, keepdims=True)
            weights = jnp.exp(scores - largest)
            inverse = 1.0 / jnp.sum(weights, axis=-1, keepdims=True)
            weights = weights.astype(BF)
            attended = (dot(weights, values) * inverse).astype(BF)
            attended_now[:, span] = attended

            @save
            def _():
                q_ref[:, span] = queries
                k_ref[:, span] = keys
                v_ref[:, span] = values
                attended_ref[:, span] = attended
                weights_ref[index] = weights
                inverse_ref[index] = inverse

            return carry

        lax.fori_loop(0, HEADS, head, 0, unroll=2)
        return dot(velocity_out_ref[...], attended_now[...], 1, 1)

    latent = latent_ref[...]
    sample = latent - readout(latent, 1.0, 0, None, lambda f: f())
    sample_ref[...] = sample
    sample_again_ref[...] = sample
    noised = (1.0 - sigma) * sample + sigma * fresh_ref[...]
    velocity = readout(noised, sigma, 1, group.astype(F32), pl.when(group == 1))
    velocity_ref[...] = velocity
    narrow_velocity_ref[...] = velocity.astype(BF)


def backward_kernel(
    place_ref,
    sigma_ref,
    sample_ref,
    fresh_ref,
    own_ref,
    fake_ref,
    prompt_ref,
    velocity_out_ref,
    role_up_ref,
    q_ref,
    k_ref,
    v_ref,
    weights_ref,
    inverse_ref,
    attended_ref,
    reduced_ref,
    picture_ref,
    grads_ref,
    grad_q,
    grad_k,
    grad_v,
):
    flag = place_ref[0]
    sigma = sigma_ref[0, 0]
    sample = sample_ref[...]
    own = own_ref[...]
    noised = (1.0 - sigma) * sample + sigma * fresh_ref[...]
    clean_real = noised - sigma * own
    clean_fake = noised - sigma * fake_ref[...].astype(F32)
    distance = jnp.sum(jnp.sum(jnp.abs(sample - clean_real), axis=1, keepdims=True), axis=0, keepdims=True)
    spread = distance * (1.0 / (IMG * CH)) + 1e-05
    cot_gen = -(clean_fake - clean_real) / spread
    cot_critic = 2.0 * (own - (fresh_ref[...] - sample)) / (IMG * CH)
    cotangent = jnp.where(flag == 0, cot_gen, cot_critic).T.astype(BF)

    def head(index, carry):
        span = pl.ds(pl.multiple_of(index * HD, HD), HD)
        queries, keys, values = q_ref[:, span], k_ref[:, span], v_ref[:, span]
        weights = weights_ref[index]
        upstream = dot(cotangent, velocity_out_ref[:, span]) * inverse_ref[index]
        inner = jnp.sum(upstream * attended_ref[:, span].astype(F32), axis=-1, keepdims=True)
        upstream = upstream.astype(BF)
        grad_v[:, span] = dot(weights, upstream, 0, 0).astype(BF)
        grad_weights = dot(upstream, values, 1, 1)
        grad_scores = (weights.astype(F32) * (grad_weights - inner) * SCALE).astype(BF)
        grad_q[:, span] = dot(grad_scores, keys).astype(BF)
        grad_k[:, span] = dot(grad_scores, queries, 0, 0).astype(BF)
        return carry

    lax.fori_loop(0, HEADS, head, 0, unroll=2)
    spans = [slice(block * RANK, (block + 1) * RANK) for block in range(3)]
    reduced_q = dot(grad_q[...], role_up_ref[:, spans[0]]).astype(BF)
    reduced_k = dot(grad_k[...], role_up_ref[:, spans[1]]).astype(BF)
    reduced_v = dot(grad_v[...], role_up_ref[:, spans[2]]).astype(BF)
    reduced_kv = jnp.concatenate([reduced_k, reduced_v], axis=1)
    down_q = dot(reduced_q, picture_ref[...], 0, 0)
    down_kv = dot(reduced_kv[:TXT], prompt_ref[:TXT, :], 0, 0) + dot(reduced_kv[TXT:], picture_ref[...], 0, 0)
    up_q = dot(reduced_ref[TXT:, spans[0]], grad_q[...], 0, 0)
    up_k = dot(reduced_ref[:, spans[1]], grad_k[...], 0, 0)
    up_v = dot(reduced_ref[:, spans[2]], grad_v[...], 0, 0)
    grads = jnp.concatenate([down_q, down_kv, up_q, up_k, up_v], axis=0)
    grads_ref[...] = grads.T.astype(BF)


def smem():
    return pl.BlockSpec(memory_space=pltpu.SMEM)


def run(kernel, name, megabytes, scalars, outputs, scratch, *operands, space=pltpu.VMEM):
    shapes = tuple(jax.ShapeDtypeStruct(*output) for output in outputs)
    return pl.pallas_call(
        kernel,
        out_shape=shapes,
        in_specs=[smem()] * scalars + [pl.BlockSpec(memory_space=space)] * (len(operands) - scalars),
        out_specs=tuple([pl.BlockSpec(memory_space=space)] * len(outputs)),
        scratch_shapes=scratch,
        compiler_params=pltpu.CompilerParams(vmem_limit_bytes=megabytes * 2**20),
        name=name,
    )(*operands)


def per_device(
    latent_noise,
    fresh_noise,
    text_states,
    step_index,
    base_qkv,
    latent_in,
    modulation,
    velocity_out,
    gen_down,
    gen_up,
    critic_down,
    critic_up,
):
    devices = lax.axis_size("fsdp")
    group = lax.axis_index("group")
    index = lax.axis_index("fsdp")
    place = jnp.stack([group, lax.rem(index, 4), lax.rem(index, 2)]).astype(jnp.int32)
    sigma = ((step_index + 1).astype(F32) / NSTEPS).reshape(1, 1)
    shard = base_qkv.shape[0]

    def move(array, across, near):
        pairs = [
            (g * devices + device, (g ^ across) * devices + (device ^ near))
            for g in range(2)
            for device in range(devices)
        ]
        return lax.ppermute(array, ("group", "fsdp"), pairs)

    latent = latent_noise[0].T
    fresh = fresh_noise[0].T
    text = text_states[0]
    gain = modulation.reshape(1, HW)
    out_map = velocity_out.T

    texts = [text, move(text, 0, 1), move(text, 1, 2), move(text, 1, 3)]
    (packed,) = run(
        pack_kernel,
        "pack",
        60,
        1,
        [((devices, shard, EIGHTH + SIDE + PART), BF)],
        [
            pltpu.VMEM((shard, 3 * HW), BF),
            pltpu.VMEM((2, shard, 3 * RANK), BF),
            pltpu.VMEM((2, 3, shard, RANK), BF),
            pltpu.VMEM((devices, shard, EIGHTH + SIDE + PART), BF),
            pltpu.SemaphoreType.DMA((5,)),
            pltpu.SemaphoreType.DMA((WRITES,)),
        ],
        place,
        base_qkv,
        gen_down,
        critic_down,
        gen_up.transpose(0, 2, 1),
        critic_up.transpose(0, 2, 1),
        space=pl.ANY,
    )
    packed = lax.all_to_all(packed, "fsdp", 0, 0).reshape(HW, EIGHTH + SIDE + PART)
    (prompts,) = run(prompt_kernel, "prompts", 16, 0, [((4 * TXT, HW), BF)], [], *texts)
    packed, prompts = lax.optimization_barrier((packed, prompts))
    share, side_own = run(
        fold_kernel,
        "fold",
        16,
        0,
        [((devices, SHARE, PART), BF), ((HW, SIDE), BF)],
        [],
        latent_in,
        gain,
        packed,
    )
    fold = lax.all_to_all(share, "fsdp", 0, 0).reshape(devices * SHARE, PART)
    side_core = move(side_own, 0, 1)
    prompts, side_core = lax.optimization_barrier((prompts, side_core))
    parts = run(
        mix_kernel,
        "mix",
        16,
        0,
        [((TXT, EIGHTH), BF)] * 4,
        [],
        prompts,
        packed,
    )
    pieces = [
        parts[near] if (across, near) == (0, 0) else move(parts[near], across, near)
        for across, near in MOVES
    ]

    sample, sample_again, velocity, narrow_velocity, *saved, role_up = run(
        forward_kernel,
        "forward",
        32,
        2,
        [
            ((CH, IMG), F32),
            ((CH, IMG), F32),
            ((CH, IMG), F32),
            ((CH, IMG), BF),
            ((IMG, HW), BF),
            ((ROWS, HW), BF),
            ((ROWS, HW), BF),
            ((HEADS, IMG, ROWS), BF),
            ((HEADS, IMG, 1), F32),
            ((IMG, HW), BF),
            ((ROWS, 3 * RANK), BF),
            ((IMG, HW), BF),
            ((HW, 3 * RANK), BF),
        ],
        [
            pltpu.VMEM((CHUNK, 4 * CH), BF),
            pltpu.VMEM((IMG, HW), BF),
            pltpu.VMEM((ROWS, HW), BF),
            pltpu.VMEM((ROWS, HW), BF),
            pltpu.VMEM((IMG, HW), BF),
            pltpu.VMEM((TXT, 2 * HW), BF),
            pltpu.VMEM((HW, SIDE), BF),
            pltpu.VMEM((HW, SIDE), BF),
        ],
        place,
        sigma,
        latent,
        fresh,
        prompts,
        latent_in,
        gain,
        out_map,
        fold,
        *pieces,
        side_own,
        side_core,
    )
    fake_velocity = lax.ppermute(narrow_velocity, "group", [(1, 0)])
    (grads,) = run(
        backward_kernel,
        "backward",
        24,
        2,
        [((HW, SIDE), BF)],
        [pltpu.VMEM((IMG, HW), BF), pltpu.VMEM((ROWS, HW), BF), pltpu.VMEM((ROWS, HW), BF)],
        place,
        sigma,
        sample_again,
        fresh,
        velocity,
        fake_velocity,
        prompts,
        out_map,
        role_up,
        *saved,
    )
    shares = lax.all_to_all(grads.reshape(devices, shard, SIDE), "fsdp", 0, 0)
    share_down, share_up = run(
        sum_kernel,
        "total",
        16,
        0,
        [((shard, 3 * RANK), F32), ((3, shard, RANK), F32)],
        [],
        shares,
    )
    return (sample.T[None], share_down[None], share_up.transpose(0, 2, 1)[None])


def solution(mesh):
    in_specs = (
        P("fsdp", None, None),
        P("fsdp", None, None),
        P("fsdp", None, None),
        P("fsdp"),
        P("fsdp", None),
        P(),
        P(),
        P(),
        P("fsdp", None),
        P(None, None, "fsdp"),
        P("fsdp", None),
        P(None, None, "fsdp"),
    )
    out_specs = (P("fsdp", None, None), P("group", "fsdp", None), P("group", None, None, "fsdp"))
    return jax.shard_map(
        per_device, mesh=mesh, in_specs=in_specs, out_specs=out_specs, check_vma=False
    )
```

```python
import jax
import jax.numpy as jnp
from jax import lax
from jax.experimental import pallas as pl
from jax.experimental.pallas import tpu as pltpu
from jax.sharding import PartitionSpec as P

HEADS = 12
HD = 128
CH = 64
RANK = 64
NSTEPS = 1000
IMG = 256
TXT = 128
ROWS = TXT + IMG
HW = HEADS * HD
CHUNK = 512
EIGHTH = HW // 4
SIDE = 6 * RANK
SHARE = 72
PART = 128
WRITES = 4
MOVES = ((0, 0), (1, 0), (0, 2), (1, 2))
BF = jnp.bfloat16
F32 = jnp.float32
SCALE = HD ** (-0.5)


def dot(left, right, left_dim=1, right_dim=0):
    dims = (((left_dim,), (right_dim,)), ((), ()))
    return lax.dot_general(left, right, dims, preferred_element_type=F32)


def high_low(values):
    high = values.astype(BF)
    return high, (values - high.astype(F32)).astype(BF)


def unit_rows(values):
    values = values.astype(F32)
    return (values * lax.rsqrt(jnp.mean(values * values, axis=-1, keepdims=True) + 1e-06)).astype(BF)


def pack_kernel(
    place_ref,
    base_ref,
    gen_down_ref,
    critic_down_ref,
    gen_up_ref,
    critic_up_ref,
    packed_ref,
    base,
    downs,
    ups,
    packed,
    read_sem,
    write_sem,
):
    reads = [
        pltpu.make_async_copy(base_ref, base, read_sem.at[0]),
        pltpu.make_async_copy(gen_down_ref, downs.at[0], read_sem.at[1]),
        pltpu.make_async_copy(critic_down_ref, downs.at[1], read_sem.at[2]),
        pltpu.make_async_copy(gen_up_ref, ups.at[0], read_sem.at[3]),
        pltpu.make_async_copy(critic_up_ref, ups.at[1], read_sem.at[4]),
    ]
    for read in reads:
        read.start()
    for read in reads:
        read.wait()
    group = place_ref[0]

    def both(gen, critic):
        gen, critic = gen.astype(F32), critic.astype(F32)
        return jnp.concatenate([gen, jnp.where(group == 0, gen, critic)], axis=1).astype(BF)

    up_rows = [jnp.concatenate([ups[role, block] for block in range(3)], axis=1) for role in range(2)]
    sides = (both(downs[0], downs[1]), both(up_rows[0], up_rows[1]))
    eighths = []
    for near in range(4):
        start = pl.multiple_of(HW + group * HW + near * EIGHTH, EIGHTH)
        eighths.append(base[:, pl.ds(start, EIGHTH)])
    rows = base.shape[0]
    batch = packed.shape[0] // WRITES
    writes = []
    for step in range(WRITES):
        for device in range(step * batch, (step + 1) * batch):
            packed[device, :, :EIGHTH] = eighths[device % 4]
            packed[device, :, EIGHTH : EIGHTH + SIDE] = sides[device % 2]
            columns = base[:, device * SHARE : (device + 1) * SHARE]
            packed[device, :, EIGHTH + SIDE :] = jnp.concatenate(
                [columns, jnp.zeros((rows, PART - SHARE), BF)], axis=1
            )
        span = pl.ds(step * batch, batch)
        write = pltpu.make_async_copy(packed.at[span], packed_ref.at[span], write_sem.at[step])
        write.start()
        writes.append(write)
    for write in writes:
        write.wait()


def prompt_kernel(text_0_ref, text_1_ref, text_2_ref, text_3_ref, prompts_ref):
    for index, text_ref in enumerate((text_0_ref, text_1_ref, text_2_ref, text_3_ref)):
        prompts_ref[index * TXT : (index + 1) * TXT, :] = unit_rows(text_ref[...])


def sum_kernel(shares_ref, down_ref, up_ref):
    total = jnp.sum(shares_ref[...].astype(F32), axis=0)
    down_ref[...] = total[:, : 3 * RANK]
    for block in range(3):
        up_ref[block] = total[:, (3 + block) * RANK : (4 + block) * RANK]


def fold_kernel(
    latent_in_ref, modulation_ref, packed_ref, share_ref, side_ref, columns, shares, read_sem, write_sem
):
    read = pltpu.make_async_copy(packed_ref.at[:, EIGHTH + SIDE :], columns, read_sem.at[0])
    read.start()
    side = pltpu.make_async_copy(packed_ref.at[:, EIGHTH : EIGHTH + SIDE], side_ref, read_sem.at[1])
    side.start()
    scaled_in = (latent_in_ref[...].astype(F32) * modulation_ref[...]).astype(BF)
    folds = jnp.concatenate([latent_in_ref[...], scaled_in], axis=0)
    read.wait()
    share = dot(folds, columns[...]).T[:SHARE].astype(BF)
    batch = shares.shape[0]
    for device in range(batch):
        shares[device] = share
    writes = [
        pltpu.make_async_copy(shares, share_ref.at[pl.ds(step * batch, batch)], write_sem.at[step])
        for step in range(share_ref.shape[0] // batch)
    ]
    for write in writes:
        write.start()
    for write in writes:
        write.wait()
    side.wait()


def mix_kernel(prompts_ref, packed_ref, mine_ref, theirs_ref, columns, read_sem):
    read = pltpu.make_async_copy(packed_ref.at[:, :EIGHTH], columns, read_sem.at[0])
    read.start()
    read.wait()
    eighth = dot(prompts_ref[...], columns[...]).astype(BF)
    mine_ref[:TXT, :] = eighth[:TXT]
    theirs_ref[:TXT, :] = eighth[TXT : 2 * TXT]
    mine_ref[TXT:, :] = eighth[2 * TXT : 3 * TXT]
    theirs_ref[TXT:, :] = eighth[3 * TXT :]


def pair_kernel(mine_ref, received_ref, own_ref, near_ref):
    for place, part_ref in enumerate((mine_ref, received_ref)):
        own_ref[place] = part_ref[:TXT, :]
        near_ref[place] = part_ref[TXT:, :]


def forward_kernel(
    place_ref,
    sigma_ref,
    latent_ref,
    fresh_ref,
    prompt_ref,
    latent_in_ref,
    modulation_ref,
    velocity_out_ref,
    fold_ref,
    text_0_ref,
    text_1_ref,
    text_2_ref,
    text_3_ref,
    side_own_ref,
    side_core_ref,
    sample_ref,
    sample_again_ref,
    velocity_ref,
    narrow_velocity_ref,
    q_ref,
    k_ref,
    v_ref,
    weights_ref,
    inverse_ref,
    attended_ref,
    reduced_ref,
    picture_ref,
    role_up_ref,
    stacked,
    q_now,
    k_now,
    v_now,
    attended_now,
    text,
    downs,
    ups,
):
    group, near, core = place_ref[0], place_ref[1], place_ref[2]
    sigma = sigma_ref[0, 0]
    for (across, move), text_ref in zip(MOVES, (text_0_ref, text_1_ref, text_2_ref, text_3_ref)):
        for place in range(2):
            start = (group ^ across) * HW + (near ^ move ^ place) * EIGHTH
            text[:, pl.ds(pl.multiple_of(start, EIGHTH), EIGHTH)] = text_ref[place]

    @pl.when(core == 0)
    def _():
        downs[...] = side_own_ref[...]
        ups[...] = side_core_ref[...]

    @pl.when(core == 1)
    def _():
        downs[...] = side_core_ref[...]
        ups[...] = side_own_ref[...]

    role_up_ref[...] = ups[:, 3 * RANK :]

    def readout(latent, noise_level, role, switch, save):
        base = role * 3 * RANK
        narrow = latent.T.astype(BF)
        hidden = dot(narrow, latent_in_ref[...])
        inverse_rms = lax.rsqrt(jnp.mean(hidden * hidden, axis=-1, keepdims=True) + 1e-06)
        picture = (hidden * inverse_rms * (1.0 + noise_level * modulation_ref[...])).astype(BF)
        reduced_picture = dot(picture, downs[:, base : base + 3 * RANK]).astype(BF)
        reduced_prompt = dot(prompt_ref[:TXT, :], downs[:, base : base + 3 * RANK]).astype(BF)

        @save
        def _():
            picture_ref[...] = picture
            reduced_ref[TXT:, :] = reduced_picture
            reduced_ref[:TXT, :] = reduced_prompt

        if switch is not None:
            reduced_picture = reduced_picture * switch.astype(BF)
            reduced_prompt = reduced_prompt * switch.astype(BF)
        scaled_high, scaled_low = high_low(narrow.astype(F32) * inverse_rms)
        for block, now in enumerate((q_now, k_now, v_now)):
            rank_span = slice(block * RANK, (block + 1) * RANK)
            up_span = slice(base + block * RANK, base + (block + 1) * RANK)
            left = jnp.concatenate(
                [scaled_high, scaled_low, scaled_high, reduced_picture[:, rank_span]], axis=1
            )
            for start in range(0, HW, CHUNK):
                own = slice(start, start + CHUNK)
                wide = slice(block * HW + start, block * HW + start + CHUNK)
                parts = fold_ref[wide, :].astype(F32)
                fold_high, fold_low = high_low(parts[:, :CH] + noise_level * parts[:, CH:])
                up = ups[own, up_span]
                stacked[...] = jnp.concatenate([fold_high, fold_high, fold_low, up], axis=1)
                picture_part = dot(left, stacked[...], 1, 1).astype(BF)
                if block == 0:
                    now[:, own] = picture_part
                else:
                    now[TXT:, own] = picture_part
                    text_span = slice((block - 1) * HW + start, (block - 1) * HW + start + CHUNK)
                    adapter = dot(reduced_prompt[:, rank_span], up, 1, 1)
                    now[:TXT, own] = (text[:, text_span].astype(F32) + adapter).astype(BF)

        def head(index, carry):
            span = pl.ds(pl.multiple_of(index * HD, HD), HD)
            queries, keys, values = q_now[:, span], k_now[:, span], v_now[:, span]
            scores = dot(queries, keys, 1, 1) * SCALE
            largest = jnp.max(scores, axis=-1, keepdims=True)
            weights = jnp.exp(scores - largest)
            inverse = 1.0 / jnp.sum(weights, axis=-1, keepdims=True)
            weights = weights.astype(BF)
            attended = (dot(weights, values) * inverse).astype(BF)
            attended_now[:, span] = attended

            @save
            def _():
                q_ref[:, span] = queries
                k_ref[:, span] = keys
                v_ref[:, span] = values
                attended_ref[:, span] = attended
                weights_ref[index] = weights
                inverse_ref[index] = inverse

            return carry

        lax.fori_loop(0, HEADS, head, 0, unroll=2)
        return dot(velocity_out_ref[...], attended_now[...], 1, 1)

    latent = latent_ref[...]
    sample = latent - readout(latent, 1.0, 0, None, lambda f: f())
    sample_ref[...] = sample
    sample_again_ref[...] = sample
    noised = (1.0 - sigma) * sample + sigma * fresh_ref[...]
    velocity = readout(noised, sigma, 1, group.astype(F32), pl.when(group == 1))
    velocity_ref[...] = velocity
    narrow_velocity_ref[...] = velocity.astype(BF)


def backward_kernel(
    place_ref,
    sigma_ref,
    sample_ref,
    fresh_ref,
    own_ref,
    fake_ref,
    prompt_ref,
    velocity_out_ref,
    role_up_ref,
    q_ref,
    k_ref,
    v_ref,
    weights_ref,
    inverse_ref,
    attended_ref,
    reduced_ref,
    picture_ref,
    grads_ref,
    grad_q,
    grad_k,
    grad_v,
):
    flag = place_ref[0]
    sigma = sigma_ref[0, 0]
    sample = sample_ref[...]
    own = own_ref[...]
    noised = (1.0 - sigma) * sample + sigma * fresh_ref[...]
    clean_real = noised - sigma * own
    clean_fake = noised - sigma * fake_ref[...].astype(F32)
    distance = jnp.sum(jnp.sum(jnp.abs(sample - clean_real), axis=1, keepdims=True), axis=0, keepdims=True)
    spread = distance * (1.0 / (IMG * CH)) + 1e-05
    cot_gen = -(clean_fake - clean_real) / spread
    cot_critic = 2.0 * (own - (fresh_ref[...] - sample)) / (IMG * CH)
    cotangent = jnp.where(flag == 0, cot_gen, cot_critic).T.astype(BF)

    def head(index, carry):
        span = pl.ds(pl.multiple_of(index * HD, HD), HD)
        queries, keys, values = q_ref[:, span], k_ref[:, span], v_ref[:, span]
        weights = weights_ref[index]
        upstream = dot(cotangent, velocity_out_ref[:, span]) * inverse_ref[index]
        inner = jnp.sum(upstream * attended_ref[:, span].astype(F32), axis=-1, keepdims=True)
        upstream = upstream.astype(BF)
        grad_v[:, span] = dot(weights, upstream, 0, 0).astype(BF)
        grad_weights = dot(upstream, values, 1, 1)
        grad_scores = (weights.astype(F32) * (grad_weights - inner) * SCALE).astype(BF)
        grad_q[:, span] = dot(grad_scores, keys).astype(BF)
        grad_k[:, span] = dot(grad_scores, queries, 0, 0).astype(BF)
        return carry

    lax.fori_loop(0, HEADS, head, 0, unroll=12)
    spans = [slice(block * RANK, (block + 1) * RANK) for block in range(3)]
    reduced_q = dot(grad_q[...], role_up_ref[:, spans[0]]).astype(BF)
    reduced_k = dot(grad_k[...], role_up_ref[:, spans[1]]).astype(BF)
    reduced_v = dot(grad_v[...], role_up_ref[:, spans[2]]).astype(BF)
    reduced_kv = jnp.concatenate([reduced_k, reduced_v], axis=1)
    down_q = dot(reduced_q, picture_ref[...], 0, 0)
    down_kv = dot(reduced_kv[:TXT], prompt_ref[:TXT, :], 0, 0) + dot(reduced_kv[TXT:], picture_ref[...], 0, 0)
    up_q = dot(reduced_ref[TXT:, spans[0]], grad_q[...], 0, 0)
    up_k = dot(reduced_ref[:, spans[1]], grad_k[...], 0, 0)
    up_v = dot(reduced_ref[:, spans[2]], grad_v[...], 0, 0)
    grads = jnp.concatenate([down_q, down_kv, up_q, up_k, up_v], axis=0)
    grads_ref[...] = grads.T.astype(BF)


def run(kernel, name, megabytes, scalars, outputs, scratch, *operands, far=(), out_space=pltpu.VMEM):
    shapes = tuple(jax.ShapeDtypeStruct(*output) for output in outputs)
    return pl.pallas_call(
        kernel,
        out_shape=shapes,
        in_specs=[
            pl.BlockSpec(
                memory_space=pltpu.SMEM if k < scalars else pl.ANY if k in far else pltpu.VMEM
            )
            for k in range(len(operands))
        ],
        out_specs=tuple([pl.BlockSpec(memory_space=out_space)] * len(outputs)),
        scratch_shapes=scratch,
        compiler_params=pltpu.CompilerParams(vmem_limit_bytes=megabytes * 2**20),
        name=name,
    )(*operands)


def per_device(
    latent_noise,
    fresh_noise,
    text_states,
    step_index,
    base_qkv,
    latent_in,
    modulation,
    velocity_out,
    gen_down,
    gen_up,
    critic_down,
    critic_up,
):
    devices = lax.axis_size("fsdp")
    group = lax.axis_index("group")
    index = lax.axis_index("fsdp")
    place = jnp.stack([group, lax.rem(index, 4), lax.rem(index, 2)]).astype(jnp.int32)
    sigma = ((step_index + 1).astype(F32) / NSTEPS).reshape(1, 1)
    shard = base_qkv.shape[0]

    def move(array, across, near):
        pairs = [
            (g * devices + device, (g ^ across) * devices + (device ^ near))
            for g in range(2)
            for device in range(devices)
        ]
        return lax.ppermute(array, ("group", "fsdp"), pairs)

    latent = latent_noise[0].T
    fresh = fresh_noise[0].T
    text = text_states[0]
    gain = modulation.reshape(1, HW)
    out_map = velocity_out.T

    texts = [text, move(text, 0, 1), move(text, 1, 2), move(text, 1, 3)]
    (packed,) = run(
        pack_kernel,
        "pack",
        60,
        1,
        [((devices, shard, EIGHTH + SIDE + PART), BF)],
        [
            pltpu.VMEM((shard, 3 * HW), BF),
            pltpu.VMEM((2, shard, 3 * RANK), BF),
            pltpu.VMEM((2, 3, shard, RANK), BF),
            pltpu.VMEM((devices, shard, EIGHTH + SIDE + PART), BF),
            pltpu.SemaphoreType.DMA((5,)),
            pltpu.SemaphoreType.DMA((WRITES,)),
        ],
        place,
        base_qkv,
        gen_down,
        critic_down,
        gen_up.transpose(0, 2, 1),
        critic_up.transpose(0, 2, 1),
        far=(1, 2, 3, 4, 5),
        out_space=pl.ANY,
    )
    packed = lax.all_to_all(packed, "fsdp", 0, 0).reshape(HW, EIGHTH + SIDE + PART)
    (prompts,) = run(prompt_kernel, "prompts", 16, 0, [((4 * TXT, HW), BF)], [], *texts)
    packed, prompts = lax.optimization_barrier((packed, prompts))
    share, side_own = run(
        fold_kernel,
        "fold",
        16,
        0,
        [((devices, SHARE, PART), BF), ((HW, SIDE), BF)],
        [
            pltpu.VMEM((HW, PART), BF),
            pltpu.VMEM((devices // 8, SHARE, PART), BF),
            pltpu.SemaphoreType.DMA((2,)),
            pltpu.SemaphoreType.DMA((8,)),
        ],
        latent_in,
        gain,
        packed,
        far=(2,),
        out_space=pl.ANY,
    )
    fold = lax.all_to_all(share, "fsdp", 0, 0).reshape(devices * SHARE, PART)
    side_core = move(side_own, 0, 1)
    prompts, side_core = lax.optimization_barrier((prompts, side_core))
    mine, theirs = run(
        mix_kernel,
        "mix",
        16,
        0,
        [((2 * TXT, EIGHTH), BF)] * 2,
        [pltpu.VMEM((HW, EIGHTH), BF), pltpu.SemaphoreType.DMA((1,))],
        prompts,
        packed,
        far=(1,),
    )
    received = move(theirs, 0, 1)
    own_pair, near_pair = run(
        pair_kernel, "pair", 16, 0, [((2, TXT, EIGHTH), BF)] * 2, [], mine, received
    )
    pieces = [own_pair, move(own_pair, 1, 0), move(near_pair, 0, 2), move(near_pair, 1, 2)]

    sample, sample_again, velocity, narrow_velocity, *saved, role_up = run(
        forward_kernel,
        "forward",
        32,
        2,
        [
            ((CH, IMG), F32),
            ((CH, IMG), F32),
            ((CH, IMG), F32),
            ((CH, IMG), BF),
            ((IMG, HW), BF),
            ((ROWS, HW), BF),
            ((ROWS, HW), BF),
            ((HEADS, IMG, ROWS), BF),
            ((HEADS, IMG, 1), F32),
            ((IMG, HW), BF),
            ((ROWS, 3 * RANK), BF),
            ((IMG, HW), BF),
            ((HW, 3 * RANK), BF),
        ],
        [
            pltpu.VMEM((CHUNK, 4 * CH), BF),
            pltpu.VMEM((IMG, HW), BF),
            pltpu.VMEM((ROWS, HW), BF),
            pltpu.VMEM((ROWS, HW), BF),
            pltpu.VMEM((IMG, HW), BF),
            pltpu.VMEM((TXT, 2 * HW), BF),
            pltpu.VMEM((HW, SIDE), BF),
            pltpu.VMEM((HW, SIDE), BF),
        ],
        place,
        sigma,
        latent,
        fresh,
        prompts,
        latent_in,
        gain,
        out_map,
        fold,
        *pieces,
        side_own,
        side_core,
    )
    fake_velocity = lax.ppermute(narrow_velocity, "group", [(1, 0)])
    (grads,) = run(
        backward_kernel,
        "backward",
        24,
        2,
        [((HW, SIDE), BF)],
        [pltpu.VMEM((IMG, HW), BF), pltpu.VMEM((ROWS, HW), BF), pltpu.VMEM((ROWS, HW), BF)],
        place,
        sigma,
        sample_again,
        fresh,
        velocity,
        fake_velocity,
        prompts,
        out_map,
        role_up,
        *saved,
    )
    shares = lax.all_to_all(grads.reshape(devices, shard, SIDE), "fsdp", 0, 0)
    share_down, share_up = run(
        sum_kernel,
        "total",
        16,
        0,
        [((shard, 3 * RANK), F32), ((3, shard, RANK), F32)],
        [],
        shares,
    )
    return (sample.T[None], share_down[None], share_up.transpose(0, 2, 1)[None])


def solution(mesh):
    in_specs = (
        P("fsdp", None, None),
        P("fsdp", None, None),
        P("fsdp", None, None),
        P("fsdp"),
        P("fsdp", None),
        P(),
        P(),
        P(),
        P("fsdp", None),
        P(None, None, "fsdp"),
        P("fsdp", None),
        P(None, None, "fsdp"),
    )
    out_specs = (P("fsdp", None, None), P("group", "fsdp", None), P("group", None, None, "fsdp"))
    return jax.shard_map(
        per_device, mesh=mesh, in_specs=in_specs, out_specs=out_specs, check_vma=False
    )
```

```python
import jax
import jax.numpy as jnp
from jax import lax
from jax.experimental import pallas as pl
from jax.experimental.pallas import tpu as pltpu
from jax.sharding import PartitionSpec as P

HEADS = 12
HD = 128
CH = 64
RANK = 64
NSTEPS = 1000
IMG = 256
TXT = 128
ROWS = TXT + IMG
HW = HEADS * HD
CHUNK = 512
EIGHTH = HW // 4
SIDE = 6 * RANK
SHARE = 72
PART = 128
WRITES = 4
MOVES = ((0, 0), (1, 0), (0, 2), (1, 2))
BF = jnp.bfloat16
F32 = jnp.float32
SCALE = HD ** (-0.5)


def dot(left, right, left_dim=1, right_dim=0):
    dims = (((left_dim,), (right_dim,)), ((), ()))
    return lax.dot_general(left, right, dims, preferred_element_type=F32)


def high_low(values):
    high = values.astype(BF)
    return high, (values - high.astype(F32)).astype(BF)


def unit_rows(values):
    values = values.astype(F32)
    return (values * lax.rsqrt(jnp.mean(values * values, axis=-1, keepdims=True) + 1e-06)).astype(BF)


def pack_kernel(
    place_ref,
    base_ref,
    gen_down_ref,
    critic_down_ref,
    gen_up_ref,
    critic_up_ref,
    packed_ref,
    base,
    downs,
    ups,
    packed,
    read_sem,
    write_sem,
):
    reads = [
        pltpu.make_async_copy(base_ref, base, read_sem.at[0]),
        pltpu.make_async_copy(gen_down_ref, downs.at[0], read_sem.at[1]),
        pltpu.make_async_copy(critic_down_ref, downs.at[1], read_sem.at[2]),
        pltpu.make_async_copy(gen_up_ref, ups.at[0], read_sem.at[3]),
        pltpu.make_async_copy(critic_up_ref, ups.at[1], read_sem.at[4]),
    ]
    for read in reads:
        read.start()
    for read in reads:
        read.wait()
    group = place_ref[0]

    def both(gen, critic):
        gen, critic = gen.astype(F32), critic.astype(F32)
        return jnp.concatenate([gen, jnp.where(group == 0, gen, critic)], axis=1).astype(BF)

    up_rows = [jnp.concatenate([ups[role, block] for block in range(3)], axis=1) for role in range(2)]
    sides = (both(downs[0], downs[1]), both(up_rows[0], up_rows[1]))
    eighths = []
    for near in range(4):
        start = pl.multiple_of(HW + group * HW + near * EIGHTH, EIGHTH)
        eighths.append(base[:, pl.ds(start, EIGHTH)])
    rows = base.shape[0]
    batch = packed.shape[0] // WRITES
    writes = []
    for step in range(WRITES):
        for device in range(step * batch, (step + 1) * batch):
            packed[device, :, :EIGHTH] = eighths[device % 4]
            packed[device, :, EIGHTH : EIGHTH + SIDE] = sides[device % 2]
            columns = base[:, device * SHARE : (device + 1) * SHARE]
            packed[device, :, EIGHTH + SIDE :] = jnp.concatenate(
                [columns, jnp.zeros((rows, PART - SHARE), BF)], axis=1
            )
        span = pl.ds(step * batch, batch)
        write = pltpu.make_async_copy(packed.at[span], packed_ref.at[span], write_sem.at[step])
        write.start()
        writes.append(write)
    for write in writes:
        write.wait()


def prompt_kernel(text_0_ref, text_1_ref, text_2_ref, text_3_ref, prompts_ref):
    for index, text_ref in enumerate((text_0_ref, text_1_ref, text_2_ref, text_3_ref)):
        prompts_ref[index * TXT : (index + 1) * TXT, :] = unit_rows(text_ref[...])


def sum_kernel(shares_ref, down_ref, up_ref):
    total = jnp.sum(shares_ref[...].astype(F32), axis=0)
    down_ref[...] = total[:, : 3 * RANK]
    for block in range(3):
        up_ref[block] = total[:, (3 + block) * RANK : (4 + block) * RANK]


def fold_kernel(
    latent_in_ref,
    modulation_ref,
    packed_ref,
    share_ref,
    side_ref,
    columns,
    sides,
    shares,
    read_sem,
    write_sem,
):
    read = pltpu.make_async_copy(packed_ref.at[:, EIGHTH + SIDE :], columns, read_sem.at[0])
    read.start()
    side = pltpu.make_async_copy(packed_ref.at[:, EIGHTH : EIGHTH + SIDE], sides, read_sem.at[1])
    side.start()
    scaled_in = (latent_in_ref[...].astype(F32) * modulation_ref[...]).astype(BF)
    folds = jnp.concatenate([latent_in_ref[...], scaled_in], axis=0)
    read.wait()
    share = dot(folds, columns[...]).T[:SHARE].astype(BF)
    batch = shares.shape[0]
    for device in range(batch):
        shares[device] = share
    writes = [
        pltpu.make_async_copy(shares, share_ref.at[pl.ds(step * batch, batch)], write_sem.at[step])
        for step in range(share_ref.shape[0] // batch)
    ]
    for write in writes:
        write.start()
    side.wait()
    side = pltpu.make_async_copy(sides, side_ref, read_sem.at[1])
    side.start()
    for write in writes:
        write.wait()
    side.wait()


def mix_kernel(prompts_ref, packed_ref, mine_ref, theirs_ref, columns, read_sem):
    read = pltpu.make_async_copy(packed_ref.at[:, :EIGHTH], columns, read_sem.at[0])
    read.start()
    read.wait()
    eighth = dot(prompts_ref[...], columns[...]).astype(BF)
    mine_ref[:TXT, :] = eighth[:TXT]
    theirs_ref[:TXT, :] = eighth[TXT : 2 * TXT]
    mine_ref[TXT:, :] = eighth[2 * TXT : 3 * TXT]
    theirs_ref[TXT:, :] = eighth[3 * TXT :]


def pair_kernel(mine_ref, received_ref, own_ref, near_ref):
    for place, part_ref in enumerate((mine_ref, received_ref)):
        own_ref[place] = part_ref[:TXT, :]
        near_ref[place] = part_ref[TXT:, :]


def forward_kernel(
    place_ref,
    sigma_ref,
    latent_ref,
    fresh_ref,
    prompt_ref,
    latent_in_ref,
    modulation_ref,
    velocity_out_ref,
    fold_ref,
    text_0_ref,
    text_1_ref,
    text_2_ref,
    text_3_ref,
    side_own_ref,
    side_core_ref,
    sample_ref,
    sample_again_ref,
    velocity_ref,
    narrow_velocity_ref,
    q_ref,
    k_ref,
    v_ref,
    weights_ref,
    inverse_ref,
    attended_ref,
    reduced_ref,
    picture_ref,
    role_up_ref,
    stacked,
    q_now,
    k_now,
    v_now,
    attended_now,
    text,
    downs,
    ups,
):
    group, near, core = place_ref[0], place_ref[1], place_ref[2]
    sigma = sigma_ref[0, 0]
    for (across, move), text_ref in zip(MOVES, (text_0_ref, text_1_ref, text_2_ref, text_3_ref)):
        for place in range(2):
            start = (group ^ across) * HW + (near ^ move ^ place) * EIGHTH
            text[:, pl.ds(pl.multiple_of(start, EIGHTH), EIGHTH)] = text_ref[place]

    @pl.when(core == 0)
    def _():
        downs[...] = side_own_ref[...]
        ups[...] = side_core_ref[...]

    @pl.when(core == 1)
    def _():
        downs[...] = side_core_ref[...]
        ups[...] = side_own_ref[...]

    role_up_ref[...] = ups[:, 3 * RANK :]

    def readout(latent, noise_level, role, switch, save):
        base = role * 3 * RANK
        narrow = latent.T.astype(BF)
        hidden = dot(narrow, latent_in_ref[...])
        inverse_rms = lax.rsqrt(jnp.mean(hidden * hidden, axis=-1, keepdims=True) + 1e-06)
        picture = (hidden * inverse_rms * (1.0 + noise_level * modulation_ref[...])).astype(BF)
        reduced_picture = dot(picture, downs[:, base : base + 3 * RANK]).astype(BF)
        reduced_prompt = dot(prompt_ref[:TXT, :], downs[:, base : base + 3 * RANK]).astype(BF)

        @save
        def _():
            picture_ref[...] = picture
            reduced_ref[TXT:, :] = reduced_picture
            reduced_ref[:TXT, :] = reduced_prompt

        if switch is not None:
            reduced_picture = reduced_picture * switch.astype(BF)
            reduced_prompt = reduced_prompt * switch.astype(BF)
        scaled_high, scaled_low = high_low(narrow.astype(F32) * inverse_rms)
        for block, now in enumerate((q_now, k_now, v_now)):
            rank_span = slice(block * RANK, (block + 1) * RANK)
            up_span = slice(base + block * RANK, base + (block + 1) * RANK)
            left = jnp.concatenate(
                [scaled_high, scaled_low, scaled_high, reduced_picture[:, rank_span]], axis=1
            )
            for start in range(0, HW, CHUNK):
                own = slice(start, start + CHUNK)
                wide = slice(block * HW + start, block * HW + start + CHUNK)
                parts = fold_ref[wide, :].astype(F32)
                fold_high, fold_low = high_low(parts[:, :CH] + noise_level * parts[:, CH:])
                up = ups[own, up_span]
                stacked[...] = jnp.concatenate([fold_high, fold_high, fold_low, up], axis=1)
                picture_part = dot(left, stacked[...], 1, 1).astype(BF)
                if block == 0:
                    now[:, own] = picture_part
                else:
                    now[TXT:, own] = picture_part
                    text_span = slice((block - 1) * HW + start, (block - 1) * HW + start + CHUNK)
                    adapter = dot(reduced_prompt[:, rank_span], up, 1, 1)
                    now[:TXT, own] = (text[:, text_span].astype(F32) + adapter).astype(BF)

        def head(index, carry):
            span = pl.ds(pl.multiple_of(index * HD, HD), HD)
            queries, keys, values = q_now[:, span], k_now[:, span], v_now[:, span]
            scores = dot(queries, keys, 1, 1) * SCALE
            largest = jnp.max(scores, axis=-1, keepdims=True)
            weights = jnp.exp(scores - largest)
            inverse = 1.0 / jnp.sum(weights, axis=-1, keepdims=True)
            weights = weights.astype(BF)
            attended = (dot(weights, values) * inverse).astype(BF)
            attended_now[:, span] = attended

            @save
            def _():
                q_ref[:, span] = queries
                k_ref[:, span] = keys
                v_ref[:, span] = values
                attended_ref[:, span] = attended
                weights_ref[index] = weights
                inverse_ref[index] = inverse

            return carry

        lax.fori_loop(0, HEADS, head, 0, unroll=2)
        return dot(velocity_out_ref[...], attended_now[...], 1, 1)

    latent = latent_ref[...]
    sample = latent - readout(latent, 1.0, 0, None, lambda f: f())
    sample_ref[...] = sample
    sample_again_ref[...] = sample
    noised = (1.0 - sigma) * sample + sigma * fresh_ref[...]
    velocity = readout(noised, sigma, 1, group.astype(F32), pl.when(group == 1))
    velocity_ref[...] = velocity
    narrow_velocity_ref[...] = velocity.astype(BF)


def backward_kernel(
    place_ref,
    sigma_ref,
    sample_ref,
    fresh_ref,
    own_ref,
    fake_ref,
    prompt_ref,
    velocity_out_ref,
    role_up_ref,
    q_ref,
    k_ref,
    v_ref,
    weights_ref,
    inverse_ref,
    attended_ref,
    reduced_ref,
    picture_ref,
    mine_ref,
    theirs_ref,
    grad_q,
    grad_k,
    grad_v,
    grads,
):
    flag = place_ref[0]
    sigma = sigma_ref[0, 0]
    sample = sample_ref[...]
    own = own_ref[...]
    noised = (1.0 - sigma) * sample + sigma * fresh_ref[...]
    clean_real = noised - sigma * own
    clean_fake = noised - sigma * fake_ref[...].astype(F32)
    distance = jnp.sum(jnp.sum(jnp.abs(sample - clean_real), axis=1, keepdims=True), axis=0, keepdims=True)
    spread = distance * (1.0 / (IMG * CH)) + 1e-05
    cot_gen = -(clean_fake - clean_real) / spread
    cot_critic = 2.0 * (own - (fresh_ref[...] - sample)) / (IMG * CH)
    cotangent = jnp.where(flag == 0, cot_gen, cot_critic).T.astype(BF)

    def head(index, carry):
        span = pl.ds(pl.multiple_of(index * HD, HD), HD)
        queries, keys, values = q_ref[:, span], k_ref[:, span], v_ref[:, span]
        weights = weights_ref[index]
        upstream = dot(cotangent, velocity_out_ref[:, span]) * inverse_ref[index]
        inner = jnp.sum(upstream * attended_ref[:, span].astype(F32), axis=-1, keepdims=True)
        upstream = upstream.astype(BF)
        grad_v[:, span] = dot(weights, upstream, 0, 0).astype(BF)
        grad_weights = dot(upstream, values, 1, 1)
        grad_scores = (weights.astype(F32) * (grad_weights - inner) * SCALE).astype(BF)
        grad_q[:, span] = dot(grad_scores, keys).astype(BF)
        grad_k[:, span] = dot(grad_scores, queries, 0, 0).astype(BF)
        return carry

    lax.fori_loop(0, HEADS, head, 0, unroll=12)
    spans = [slice(block * RANK, (block + 1) * RANK) for block in range(3)]
    reduced_q = dot(grad_q[...], role_up_ref[:, spans[0]]).astype(BF)
    reduced_k = dot(grad_k[...], role_up_ref[:, spans[1]]).astype(BF)
    reduced_v = dot(grad_v[...], role_up_ref[:, spans[2]]).astype(BF)
    reduced_kv = jnp.concatenate([reduced_k, reduced_v], axis=1)
    down_q = dot(reduced_q, picture_ref[...], 0, 0)
    down_kv = dot(reduced_kv[:TXT], prompt_ref[:TXT, :], 0, 0) + dot(reduced_kv[TXT:], picture_ref[...], 0, 0)
    up_q = dot(reduced_ref[TXT:, spans[0]], grad_q[...], 0, 0)
    up_k = dot(reduced_ref[:, spans[1]], grad_k[...], 0, 0)
    up_v = dot(reduced_ref[:, spans[2]], grad_v[...], 0, 0)
    grads[...] = jnp.concatenate([down_q, down_kv, up_q, up_k, up_v], axis=0).T
    core = place_ref[2]
    pairs, rows, _ = mine_ref.shape
    for pair in range(pairs):
        mine = pl.ds(pl.multiple_of((2 * pair + core) * rows, 8), rows)
        theirs = pl.ds(pl.multiple_of((2 * pair + 1 - core) * rows, 8), rows)
        mine_ref[pair] = grads[mine, :]
        theirs_ref[pair] = grads[theirs, :].astype(BF)


def add_kernel(mine_ref, received_ref, sums_ref):
    sums_ref[...] = (mine_ref[...] + received_ref[...].astype(F32)).astype(BF)


def run(kernel, name, megabytes, scalars, outputs, scratch, *operands, far=(), out_space=pltpu.VMEM):
    shapes = tuple(jax.ShapeDtypeStruct(*output) for output in outputs)
    return pl.pallas_call(
        kernel,
        out_shape=shapes,
        in_specs=[
            pl.BlockSpec(
                memory_space=pltpu.SMEM if k < scalars else pl.ANY if k in far else pltpu.VMEM
            )
            for k in range(len(operands))
        ],
        out_specs=tuple([pl.BlockSpec(memory_space=out_space)] * len(outputs)),
        scratch_shapes=scratch,
        compiler_params=pltpu.CompilerParams(vmem_limit_bytes=megabytes * 2**20),
        name=name,
    )(*operands)


def per_device(
    latent_noise,
    fresh_noise,
    text_states,
    step_index,
    base_qkv,
    latent_in,
    modulation,
    velocity_out,
    gen_down,
    gen_up,
    critic_down,
    critic_up,
):
    devices = lax.axis_size("fsdp")
    group = lax.axis_index("group")
    index = lax.axis_index("fsdp")
    place = jnp.stack([group, lax.rem(index, 4), lax.rem(index, 2)]).astype(jnp.int32)
    sigma = ((step_index + 1).astype(F32) / NSTEPS).reshape(1, 1)
    shard = base_qkv.shape[0]

    def move(array, across, near):
        pairs = [
            (g * devices + device, (g ^ across) * devices + (device ^ near))
            for g in range(2)
            for device in range(devices)
        ]
        return lax.ppermute(array, ("group", "fsdp"), pairs)

    latent = latent_noise[0].T
    fresh = fresh_noise[0].T
    text = text_states[0]
    gain = modulation.reshape(1, HW)
    out_map = velocity_out.T

    texts = [text, move(text, 0, 1), move(text, 1, 2), move(text, 1, 3)]
    (packed,) = run(
        pack_kernel,
        "pack",
        60,
        1,
        [((devices, shard, EIGHTH + SIDE + PART), BF)],
        [
            pltpu.VMEM((shard, 3 * HW), BF),
            pltpu.VMEM((2, shard, 3 * RANK), BF),
            pltpu.VMEM((2, 3, shard, RANK), BF),
            pltpu.VMEM((devices, shard, EIGHTH + SIDE + PART), BF),
            pltpu.SemaphoreType.DMA((5,)),
            pltpu.SemaphoreType.DMA((WRITES,)),
        ],
        place,
        base_qkv,
        gen_down,
        critic_down,
        gen_up.transpose(0, 2, 1),
        critic_up.transpose(0, 2, 1),
        far=(1, 2, 3, 4, 5),
        out_space=pl.ANY,
    )
    packed = lax.all_to_all(packed, "fsdp", 0, 0).reshape(HW, EIGHTH + SIDE + PART)
    (prompts,) = run(prompt_kernel, "prompts", 16, 0, [((4 * TXT, HW), BF)], [], *texts)
    packed, prompts = lax.optimization_barrier((packed, prompts))
    share, side_own = run(
        fold_kernel,
        "fold",
        16,
        0,
        [((devices, SHARE, PART), BF), ((HW, SIDE), BF)],
        [
            pltpu.VMEM((HW, PART), BF),
            pltpu.VMEM((HW, SIDE), BF),
            pltpu.VMEM((devices // 8, SHARE, PART), BF),
            pltpu.SemaphoreType.DMA((2,)),
            pltpu.SemaphoreType.DMA((8,)),
        ],
        latent_in,
        gain,
        packed,
        far=(2,),
        out_space=pl.ANY,
    )
    fold = lax.all_to_all(share, "fsdp", 0, 0).reshape(devices * SHARE, PART)
    side_core = move(side_own, 0, 1)
    prompts, side_core = lax.optimization_barrier((prompts, side_core))
    mine, theirs = run(
        mix_kernel,
        "mix",
        16,
        0,
        [((2 * TXT, EIGHTH), BF)] * 2,
        [pltpu.VMEM((HW, EIGHTH), BF), pltpu.SemaphoreType.DMA((1,))],
        prompts,
        packed,
        far=(1,),
    )
    received = move(theirs, 0, 1)
    own_pair, near_pair = run(
        pair_kernel, "pair", 16, 0, [((2, TXT, EIGHTH), BF)] * 2, [], mine, received
    )
    pieces = [own_pair, move(own_pair, 1, 0), move(near_pair, 0, 2), move(near_pair, 1, 2)]

    sample, sample_again, velocity, narrow_velocity, *saved, role_up = run(
        forward_kernel,
        "forward",
        32,
        2,
        [
            ((CH, IMG), F32),
            ((CH, IMG), F32),
            ((CH, IMG), F32),
            ((CH, IMG), BF),
            ((IMG, HW), BF),
            ((ROWS, HW), BF),
            ((ROWS, HW), BF),
            ((HEADS, IMG, ROWS), BF),
            ((HEADS, IMG, 1), F32),
            ((IMG, HW), BF),
            ((ROWS, 3 * RANK), BF),
            ((IMG, HW), BF),
            ((HW, 3 * RANK), BF),
        ],
        [
            pltpu.VMEM((CHUNK, 4 * CH), BF),
            pltpu.VMEM((IMG, HW), BF),
            pltpu.VMEM((ROWS, HW), BF),
            pltpu.VMEM((ROWS, HW), BF),
            pltpu.VMEM((IMG, HW), BF),
            pltpu.VMEM((TXT, 2 * HW), BF),
            pltpu.VMEM((HW, SIDE), BF),
            pltpu.VMEM((HW, SIDE), BF),
        ],
        place,
        sigma,
        latent,
        fresh,
        prompts,
        latent_in,
        gain,
        out_map,
        fold,
        *pieces,
        side_own,
        side_core,
    )
    fake_velocity = lax.ppermute(narrow_velocity, "group", [(1, 0)])
    half = (devices // 2, shard, SIDE)
    mine, theirs = run(
        backward_kernel,
        "backward",
        24,
        2,
        [(half, F32), (half, BF)],
        [
            pltpu.VMEM((IMG, HW), BF),
            pltpu.VMEM((ROWS, HW), BF),
            pltpu.VMEM((ROWS, HW), BF),
            pltpu.VMEM((HW, SIDE), F32),
        ],
        place,
        sigma,
        sample_again,
        fresh,
        velocity,
        fake_velocity,
        prompts,
        out_map,
        role_up,
        *saved,
    )
    (sums,) = run(add_kernel, "add", 16, 0, [(half, BF)], [], mine, move(theirs, 0, 1))
    parities = [list(range(core, devices, 2)) for core in range(2)]
    shares = lax.all_to_all(sums, "fsdp", 0, 0, axis_index_groups=parities)
    share_down, share_up = run(
        sum_kernel,
        "total",
        16,
        0,
        [((shard, 3 * RANK), F32), ((3, shard, RANK), F32)],
        [],
        shares,
    )
    return (sample.T[None], share_down[None], share_up.transpose(0, 2, 1)[None])


def solution(mesh):
    in_specs = (
        P("fsdp", None, None),
        P("fsdp", None, None),
        P("fsdp", None, None),
        P("fsdp"),
        P("fsdp", None),
        P(),
        P(),
        P(),
        P("fsdp", None),
        P(None, None, "fsdp"),
        P("fsdp", None),
        P(None, None, "fsdp"),
    )
    out_specs = (P("fsdp", None, None), P("group", "fsdp", None), P("group", None, None, "fsdp"))
    return jax.shard_map(
        per_device, mesh=mesh, in_specs=in_specs, out_specs=out_specs, check_vma=False
    )
```

```python
import jax
import jax.numpy as jnp
from jax import lax
from jax.experimental import pallas as pl
from jax.experimental.pallas import tpu as pltpu
from jax.sharding import PartitionSpec as P

HEADS = 12
HD = 128
CH = 64
RANK = 64
NSTEPS = 1000
IMG = 256
TXT = 128
ROWS = TXT + IMG
HW = HEADS * HD
CHUNK = 512
EIGHTH = HW // 4
SIDE = 6 * RANK
SHARE = 72
PART = 128
WRITES = 4
MOVES = ((0, 0), (1, 0), (0, 2), (1, 2))
BF = jnp.bfloat16
F32 = jnp.float32
SCALE = HD ** (-0.5)


def dot(left, right, left_dim=1, right_dim=0):
    dims = (((left_dim,), (right_dim,)), ((), ()))
    return lax.dot_general(left, right, dims, preferred_element_type=F32)


def high_low(values):
    high = values.astype(BF)
    return high, (values - high.astype(F32)).astype(BF)


def unit_rows(values):
    values = values.astype(F32)
    return (values * lax.rsqrt(jnp.mean(values * values, axis=-1, keepdims=True) + 1e-06)).astype(BF)


def pack_kernel(
    place_ref,
    base_ref,
    gen_down_ref,
    critic_down_ref,
    gen_up_ref,
    critic_up_ref,
    packed_ref,
    base,
    downs,
    ups,
    packed,
    read_sem,
    write_sem,
):
    reads = [
        pltpu.make_async_copy(base_ref, base, read_sem.at[0]),
        pltpu.make_async_copy(gen_down_ref, downs.at[0], read_sem.at[1]),
        pltpu.make_async_copy(critic_down_ref, downs.at[1], read_sem.at[2]),
        pltpu.make_async_copy(gen_up_ref, ups.at[0], read_sem.at[3]),
        pltpu.make_async_copy(critic_up_ref, ups.at[1], read_sem.at[4]),
    ]
    for read in reads:
        read.start()
    for read in reads:
        read.wait()
    group = place_ref[0]

    def both(gen, critic):
        gen, critic = gen.astype(F32), critic.astype(F32)
        return jnp.concatenate([gen, jnp.where(group == 0, gen, critic)], axis=1).astype(BF)

    up_rows = [jnp.concatenate([ups[role, block] for block in range(3)], axis=1) for role in range(2)]
    sides = (both(downs[0], downs[1]), both(up_rows[0], up_rows[1]))
    eighths = []
    for near in range(4):
        start = pl.multiple_of(HW + group * HW + near * EIGHTH, EIGHTH)
        eighths.append(base[:, pl.ds(start, EIGHTH)])
    rows = base.shape[0]
    batch = packed.shape[0] // WRITES
    writes = []
    for step in range(WRITES):
        for device in range(step * batch, (step + 1) * batch):
            packed[device, :, :EIGHTH] = eighths[device % 4]
            packed[device, :, EIGHTH : EIGHTH + SIDE] = sides[device % 2]
            columns = base[:, device * SHARE : (device + 1) * SHARE]
            packed[device, :, EIGHTH + SIDE :] = jnp.concatenate(
                [columns, jnp.zeros((rows, PART - SHARE), BF)], axis=1
            )
        span = pl.ds(step * batch, batch)
        write = pltpu.make_async_copy(packed.at[span], packed_ref.at[span], write_sem.at[step])
        write.start()
        writes.append(write)
    for write in writes:
        write.wait()


def prompt_kernel(text_0_ref, text_1_ref, text_2_ref, text_3_ref, prompts_ref):
    for index, text_ref in enumerate((text_0_ref, text_1_ref, text_2_ref, text_3_ref)):
        prompts_ref[index * TXT : (index + 1) * TXT, :] = unit_rows(text_ref[...])


def sum_kernel(shares_ref, down_ref, up_ref):
    total = jnp.sum(shares_ref[...].astype(F32), axis=0)
    down_ref[...] = total[:, : 3 * RANK]
    for block in range(3):
        up_ref[block] = total[:, (3 + block) * RANK : (4 + block) * RANK]


def mix_kernel(
    prompts_ref,
    latent_in_ref,
    modulation_ref,
    packed_ref,
    mine_ref,
    theirs_ref,
    share_ref,
    side_ref,
    columns,
    eighths,
    sides,
    shares,
    read_sem,
    write_sem,
):
    reads = [
        pltpu.make_async_copy(packed_ref.at[:, EIGHTH + SIDE :], columns, read_sem.at[0]),
        pltpu.make_async_copy(packed_ref.at[:, :EIGHTH], eighths, read_sem.at[1]),
        pltpu.make_async_copy(packed_ref.at[:, EIGHTH : EIGHTH + SIDE], sides, read_sem.at[2]),
    ]
    for read in reads:
        read.start()
    scaled_in = (latent_in_ref[...].astype(F32) * modulation_ref[...]).astype(BF)
    folds = jnp.concatenate([latent_in_ref[...], scaled_in], axis=0)
    reads[0].wait()
    share = dot(folds, columns[...]).T[:SHARE].astype(BF)
    batch = shares.shape[0]
    for device in range(batch):
        shares[device] = share
    writes = [
        pltpu.make_async_copy(shares, share_ref.at[pl.ds(step * batch, batch)], write_sem.at[step])
        for step in range(share_ref.shape[0] // batch)
    ]
    for write in writes:
        write.start()
    reads[1].wait()
    eighth = dot(prompts_ref[...], eighths[...]).astype(BF)
    reads[2].wait()
    side = pltpu.make_async_copy(sides, side_ref, read_sem.at[2])
    side.start()
    mine_ref[:TXT, :] = eighth[:TXT]
    theirs_ref[:TXT, :] = eighth[TXT : 2 * TXT]
    mine_ref[TXT:, :] = eighth[2 * TXT : 3 * TXT]
    theirs_ref[TXT:, :] = eighth[3 * TXT :]
    for write in writes:
        write.wait()
    side.wait()


def pair_kernel(mine_ref, received_ref, own_ref, near_ref):
    for place, part_ref in enumerate((mine_ref, received_ref)):
        own_ref[place] = part_ref[:TXT, :]
        near_ref[place] = part_ref[TXT:, :]


def forward_kernel(
    place_ref,
    sigma_ref,
    latent_ref,
    fresh_ref,
    prompt_ref,
    latent_in_ref,
    modulation_ref,
    velocity_out_ref,
    fold_ref,
    text_0_ref,
    text_1_ref,
    text_2_ref,
    text_3_ref,
    side_own_ref,
    side_core_ref,
    sample_ref,
    sample_again_ref,
    velocity_ref,
    narrow_velocity_ref,
    q_ref,
    k_ref,
    v_ref,
    weights_ref,
    inverse_ref,
    attended_ref,
    reduced_ref,
    picture_ref,
    role_up_ref,
    stacked,
    q_now,
    k_now,
    v_now,
    attended_now,
    text,
    downs,
    ups,
):
    group, near, core = place_ref[0], place_ref[1], place_ref[2]
    sigma = sigma_ref[0, 0]
    for (across, move), text_ref in zip(MOVES, (text_0_ref, text_1_ref, text_2_ref, text_3_ref)):
        for place in range(2):
            start = (group ^ across) * HW + (near ^ move ^ place) * EIGHTH
            text[:, pl.ds(pl.multiple_of(start, EIGHTH), EIGHTH)] = text_ref[place]

    @pl.when(core == 0)
    def _():
        downs[...] = side_own_ref[...]
        ups[...] = side_core_ref[...]

    @pl.when(core == 1)
    def _():
        downs[...] = side_core_ref[...]
        ups[...] = side_own_ref[...]

    role_up_ref[...] = ups[:, 3 * RANK :]

    def readout(latent, noise_level, role, switch, save):
        base = role * 3 * RANK
        narrow = latent.T.astype(BF)
        hidden = dot(narrow, latent_in_ref[...])
        inverse_rms = lax.rsqrt(jnp.mean(hidden * hidden, axis=-1, keepdims=True) + 1e-06)
        picture = (hidden * inverse_rms * (1.0 + noise_level * modulation_ref[...])).astype(BF)
        reduced_picture = dot(picture, downs[:, base : base + 3 * RANK]).astype(BF)
        reduced_prompt = dot(prompt_ref[:TXT, :], downs[:, base : base + 3 * RANK]).astype(BF)

        @save
        def _():
            picture_ref[...] = picture
            reduced_ref[TXT:, :] = reduced_picture
            reduced_ref[:TXT, :] = reduced_prompt

        if switch is not None:
            reduced_picture = reduced_picture * switch.astype(BF)
            reduced_prompt = reduced_prompt * switch.astype(BF)
        scaled_high, scaled_low = high_low(narrow.astype(F32) * inverse_rms)
        for block, now in enumerate((q_now, k_now, v_now)):
            rank_span = slice(block * RANK, (block + 1) * RANK)
            up_span = slice(base + block * RANK, base + (block + 1) * RANK)
            left = jnp.concatenate(
                [scaled_high, scaled_low, scaled_high, reduced_picture[:, rank_span]], axis=1
            )
            for start in range(0, HW, CHUNK):
                own = slice(start, start + CHUNK)
                wide = slice(block * HW + start, block * HW + start + CHUNK)
                parts = fold_ref[wide, :].astype(F32)
                fold_high, fold_low = high_low(parts[:, :CH] + noise_level * parts[:, CH:])
                up = ups[own, up_span]
                stacked[...] = jnp.concatenate([fold_high, fold_high, fold_low, up], axis=1)
                picture_part = dot(left, stacked[...], 1, 1).astype(BF)
                if block == 0:
                    now[:, own] = picture_part
                else:
                    now[TXT:, own] = picture_part
                    text_span = slice((block - 1) * HW + start, (block - 1) * HW + start + CHUNK)
                    adapter = dot(reduced_prompt[:, rank_span], up, 1, 1)
                    now[:TXT, own] = (text[:, text_span].astype(F32) + adapter).astype(BF)

        def head(index, carry):
            span = pl.ds(pl.multiple_of(index * HD, HD), HD)
            queries, keys, values = q_now[:, span], k_now[:, span], v_now[:, span]
            scores = dot(queries, keys, 1, 1) * SCALE
            largest = jnp.max(scores, axis=-1, keepdims=True)
            weights = jnp.exp(scores - largest)
            inverse = 1.0 / jnp.sum(weights, axis=-1, keepdims=True)
            weights = weights.astype(BF)
            attended = (dot(weights, values) * inverse).astype(BF)
            attended_now[:, span] = attended

            @save
            def _():
                q_ref[:, span] = queries
                k_ref[:, span] = keys
                v_ref[:, span] = values
                attended_ref[:, span] = attended
                weights_ref[index] = weights
                inverse_ref[index] = inverse

            return carry

        lax.fori_loop(0, HEADS, head, 0, unroll=2)
        return dot(velocity_out_ref[...], attended_now[...], 1, 1)

    latent = latent_ref[...]
    sample = latent - readout(latent, 1.0, 0, None, lambda f: f())
    sample_ref[...] = sample
    sample_again_ref[...] = sample
    noised = (1.0 - sigma) * sample + sigma * fresh_ref[...]
    velocity = readout(noised, sigma, 1, group.astype(F32), pl.when(group == 1))
    velocity_ref[...] = velocity
    narrow_velocity_ref[...] = velocity.astype(BF)


def backward_kernel(
    place_ref,
    sigma_ref,
    sample_ref,
    fresh_ref,
    own_ref,
    fake_ref,
    prompt_ref,
    velocity_out_ref,
    role_up_ref,
    q_ref,
    k_ref,
    v_ref,
    weights_ref,
    inverse_ref,
    attended_ref,
    reduced_ref,
    picture_ref,
    mine_ref,
    theirs_ref,
    grad_q,
    grad_k,
    grad_v,
    grads,
):
    flag = place_ref[0]
    sigma = sigma_ref[0, 0]
    sample = sample_ref[...]
    own = own_ref[...]
    noised = (1.0 - sigma) * sample + sigma * fresh_ref[...]
    clean_real = noised - sigma * own
    clean_fake = noised - sigma * fake_ref[...].astype(F32)
    distance = jnp.sum(jnp.sum(jnp.abs(sample - clean_real), axis=1, keepdims=True), axis=0, keepdims=True)
    spread = distance * (1.0 / (IMG * CH)) + 1e-05
    cot_gen = -(clean_fake - clean_real) / spread
    cot_critic = 2.0 * (own - (fresh_ref[...] - sample)) / (IMG * CH)
    cotangent = jnp.where(flag == 0, cot_gen, cot_critic).T.astype(BF)

    def head(index, carry):
        span = pl.ds(pl.multiple_of(index * HD, HD), HD)
        queries, keys, values = q_ref[:, span], k_ref[:, span], v_ref[:, span]
        weights = weights_ref[index]
        upstream = dot(cotangent, velocity_out_ref[:, span]) * inverse_ref[index]
        inner = jnp.sum(upstream * attended_ref[:, span].astype(F32), axis=-1, keepdims=True)
        upstream = upstream.astype(BF)
        grad_v[:, span] = dot(weights, upstream, 0, 0).astype(BF)
        grad_weights = dot(upstream, values, 1, 1)
        grad_scores = (weights.astype(F32) * (grad_weights - inner) * SCALE).astype(BF)
        grad_q[:, span] = dot(grad_scores, keys).astype(BF)
        grad_k[:, span] = dot(grad_scores, queries, 0, 0).astype(BF)
        return carry

    lax.fori_loop(0, HEADS, head, 0, unroll=12)
    spans = [slice(block * RANK, (block + 1) * RANK) for block in range(3)]
    reduced_q = dot(grad_q[...], role_up_ref[:, spans[0]]).astype(BF)
    reduced_k = dot(grad_k[...], role_up_ref[:, spans[1]]).astype(BF)
    reduced_v = dot(grad_v[...], role_up_ref[:, spans[2]]).astype(BF)
    reduced_kv = jnp.concatenate([reduced_k, reduced_v], axis=1)
    down_q = dot(reduced_q, picture_ref[...], 0, 0)
    down_kv = dot(reduced_kv[:TXT], prompt_ref[:TXT, :], 0, 0) + dot(reduced_kv[TXT:], picture_ref[...], 0, 0)
    up_q = dot(reduced_ref[TXT:, spans[0]], grad_q[...], 0, 0)
    up_k = dot(reduced_ref[:, spans[1]], grad_k[...], 0, 0)
    up_v = dot(reduced_ref[:, spans[2]], grad_v[...], 0, 0)
    grads[...] = jnp.concatenate([down_q, down_kv, up_q, up_k, up_v], axis=0).T
    core = place_ref[2]
    pairs, rows, _ = mine_ref.shape
    for pair in range(pairs):
        mine = pl.ds(pl.multiple_of((2 * pair + core) * rows, 8), rows)
        theirs = pl.ds(pl.multiple_of((2 * pair + 1 - core) * rows, 8), rows)
        mine_ref[pair] = grads[mine, :]
        theirs_ref[pair] = grads[theirs, :].astype(BF)


def add_kernel(mine_ref, received_ref, sums_ref):
    sums_ref[...] = (mine_ref[...] + received_ref[...].astype(F32)).astype(BF)


def run(kernel, name, megabytes, scalars, outputs, scratch, *operands, far=(), far_out=()):
    shapes = tuple(jax.ShapeDtypeStruct(*output) for output in outputs)
    return pl.pallas_call(
        kernel,
        out_shape=shapes,
        in_specs=[
            pl.BlockSpec(
                memory_space=pltpu.SMEM if k < scalars else pl.ANY if k in far else pltpu.VMEM
            )
            for k in range(len(operands))
        ],
        out_specs=tuple(
            pl.BlockSpec(memory_space=pl.ANY if k in far_out else pltpu.VMEM)
            for k in range(len(outputs))
        ),
        scratch_shapes=scratch,
        compiler_params=pltpu.CompilerParams(vmem_limit_bytes=megabytes * 2**20),
        name=name,
    )(*operands)


def per_device(
    latent_noise,
    fresh_noise,
    text_states,
    step_index,
    base_qkv,
    latent_in,
    modulation,
    velocity_out,
    gen_down,
    gen_up,
    critic_down,
    critic_up,
):
    devices = lax.axis_size("fsdp")
    group = lax.axis_index("group")
    index = lax.axis_index("fsdp")
    place = jnp.stack([group, lax.rem(index, 4), lax.rem(index, 2)]).astype(jnp.int32)
    sigma = ((step_index + 1).astype(F32) / NSTEPS).reshape(1, 1)
    shard = base_qkv.shape[0]

    def move(array, across, near):
        pairs = [
            (g * devices + device, (g ^ across) * devices + (device ^ near))
            for g in range(2)
            for device in range(devices)
        ]
        return lax.ppermute(array, ("group", "fsdp"), pairs)

    latent = latent_noise[0].T
    fresh = fresh_noise[0].T
    text = text_states[0]
    gain = modulation.reshape(1, HW)
    out_map = velocity_out.T

    texts = [text, move(text, 0, 1), move(text, 1, 2), move(text, 1, 3)]
    (packed,) = run(
        pack_kernel,
        "pack",
        60,
        1,
        [((devices, shard, EIGHTH + SIDE + PART), BF)],
        [
            pltpu.VMEM((shard, 3 * HW), BF),
            pltpu.VMEM((2, shard, 3 * RANK), BF),
            pltpu.VMEM((2, 3, shard, RANK), BF),
            pltpu.VMEM((devices, shard, EIGHTH + SIDE + PART), BF),
            pltpu.SemaphoreType.DMA((5,)),
            pltpu.SemaphoreType.DMA((WRITES,)),
        ],
        place,
        base_qkv,
        gen_down,
        critic_down,
        gen_up.transpose(0, 2, 1),
        critic_up.transpose(0, 2, 1),
        far=(1, 2, 3, 4, 5),
        far_out=(0,),
    )
    packed = lax.all_to_all(packed, "fsdp", 0, 0).reshape(HW, EIGHTH + SIDE + PART)
    (prompts,) = run(prompt_kernel, "prompts", 16, 0, [((4 * TXT, HW), BF)], [], *texts)
    packed, prompts = lax.optimization_barrier((packed, prompts))
    mine, theirs, share, side_own = run(
        mix_kernel,
        "mix",
        52,
        0,
        [
            ((2 * TXT, EIGHTH), BF),
            ((2 * TXT, EIGHTH), BF),
            ((devices, SHARE, PART), BF),
            ((HW, SIDE), BF),
        ],
        [
            pltpu.VMEM((HW, PART), BF),
            pltpu.VMEM((HW, EIGHTH), BF),
            pltpu.VMEM((HW, SIDE), BF),
            pltpu.VMEM((devices // 8, SHARE, PART), BF),
            pltpu.SemaphoreType.DMA((3,)),
            pltpu.SemaphoreType.DMA((8,)),
        ],
        prompts,
        latent_in,
        gain,
        packed,
        far=(3,),
        far_out=(2, 3),
    )
    received = move(theirs, 0, 1)
    fold = lax.all_to_all(share, "fsdp", 0, 0).reshape(devices * SHARE, PART)
    side_core = move(side_own, 0, 1)
    own_pair, near_pair = run(
        pair_kernel, "pair", 52, 0, [((2, TXT, EIGHTH), BF)] * 2, [], mine, received
    )
    pieces = [own_pair, move(own_pair, 1, 0), move(near_pair, 0, 2), move(near_pair, 1, 2)]

    sample, sample_again, velocity, narrow_velocity, *saved, role_up = run(
        forward_kernel,
        "forward",
        46,
        2,
        [
            ((CH, IMG), F32),
            ((CH, IMG), F32),
            ((CH, IMG), F32),
            ((CH, IMG), BF),
            ((IMG, HW), BF),
            ((ROWS, HW), BF),
            ((ROWS, HW), BF),
            ((HEADS, IMG, ROWS), BF),
            ((HEADS, IMG, 1), F32),
            ((IMG, HW), BF),
            ((ROWS, 3 * RANK), BF),
            ((IMG, HW), BF),
            ((HW, 3 * RANK), BF),
        ],
        [
            pltpu.VMEM((CHUNK, 4 * CH), BF),
            pltpu.VMEM((IMG, HW), BF),
            pltpu.VMEM((ROWS, HW), BF),
            pltpu.VMEM((ROWS, HW), BF),
            pltpu.VMEM((IMG, HW), BF),
            pltpu.VMEM((TXT, 2 * HW), BF),
            pltpu.VMEM((HW, SIDE), BF),
            pltpu.VMEM((HW, SIDE), BF),
        ],
        place,
        sigma,
        latent,
        fresh,
        prompts,
        latent_in,
        gain,
        out_map,
        fold,
        *pieces,
        side_own,
        side_core,
    )
    fake_velocity = lax.ppermute(narrow_velocity, "group", [(1, 0)])
    half = (devices // 2, shard, SIDE)
    mine, theirs = run(
        backward_kernel,
        "backward",
        46,
        2,
        [(half, F32), (half, BF)],
        [
            pltpu.VMEM((IMG, HW), BF),
            pltpu.VMEM((ROWS, HW), BF),
            pltpu.VMEM((ROWS, HW), BF),
            pltpu.VMEM((HW, SIDE), F32),
        ],
        place,
        sigma,
        sample_again,
        fresh,
        velocity,
        fake_velocity,
        prompts,
        out_map,
        role_up,
        *saved,
    )
    (sums,) = run(add_kernel, "add", 16, 0, [(half, BF)], [], mine, move(theirs, 0, 1))
    parities = [list(range(core, devices, 2)) for core in range(2)]
    shares = lax.all_to_all(sums, "fsdp", 0, 0, axis_index_groups=parities)
    share_down, share_up = run(
        sum_kernel,
        "total",
        16,
        0,
        [((shard, 3 * RANK), F32), ((3, shard, RANK), F32)],
        [],
        shares,
    )
    return (sample.T[None], share_down[None], share_up.transpose(0, 2, 1)[None])


def solution(mesh):
    in_specs = (
        P("fsdp", None, None),
        P("fsdp", None, None),
        P("fsdp", None, None),
        P("fsdp"),
        P("fsdp", None),
        P(),
        P(),
        P(),
        P("fsdp", None),
        P(None, None, "fsdp"),
        P("fsdp", None),
        P(None, None, "fsdp"),
    )
    out_specs = (P("fsdp", None, None), P("group", "fsdp", None), P("group", None, None, "fsdp"))
    return jax.shard_map(
        per_device, mesh=mesh, in_specs=in_specs, out_specs=out_specs, check_vma=False
    )
```

```python
import jax
import jax.numpy as jnp
from jax import lax
from jax.experimental import pallas as pl
from jax.experimental.pallas import tpu as pltpu
from jax.sharding import PartitionSpec as P

HEADS = 12
HD = 128
CH = 64
RANK = 64
NSTEPS = 1000
IMG = 256
TXT = 128
ROWS = TXT + IMG
HW = HEADS * HD
CHUNK = 512
EIGHTH = HW // 4
SIDE = 6 * RANK
SHARE = 72
PART = 128
WRITES = 4
MOVES = ((0, 0), (1, 0), (0, 2), (1, 2))
BF = jnp.bfloat16
F32 = jnp.float32
SCALE = HD ** (-0.5)


def dot(left, right, left_dim=1, right_dim=0):
    dims = (((left_dim,), (right_dim,)), ((), ()))
    return lax.dot_general(left, right, dims, preferred_element_type=F32)


def high_low(values):
    high = values.astype(BF)
    return high, (values - high.astype(F32)).astype(BF)


def unit_rows(values):
    values = values.astype(F32)
    return (values * lax.rsqrt(jnp.mean(values * values, axis=-1, keepdims=True) + 1e-06)).astype(BF)


def pack_kernel(
    place_ref,
    base_ref,
    gen_down_ref,
    critic_down_ref,
    gen_up_ref,
    critic_up_ref,
    packed_ref,
    base,
    downs,
    ups,
    packed,
    read_sem,
    write_sem,
):
    reads = [
        pltpu.make_async_copy(base_ref, base, read_sem.at[0]),
        pltpu.make_async_copy(gen_down_ref, downs.at[0], read_sem.at[1]),
        pltpu.make_async_copy(critic_down_ref, downs.at[1], read_sem.at[2]),
        pltpu.make_async_copy(gen_up_ref, ups.at[0], read_sem.at[3]),
        pltpu.make_async_copy(critic_up_ref, ups.at[1], read_sem.at[4]),
    ]
    for read in reads:
        read.start()
    for read in reads:
        read.wait()
    group = place_ref[0]

    def both(gen, critic):
        gen, critic = gen.astype(F32), critic.astype(F32)
        return jnp.concatenate([gen, jnp.where(group == 0, gen, critic)], axis=1).astype(BF)

    up_rows = [jnp.concatenate([ups[role, block] for block in range(3)], axis=1) for role in range(2)]
    sides = (both(downs[0], downs[1]), both(up_rows[0], up_rows[1]))
    eighths = []
    for near in range(4):
        start = pl.multiple_of(HW + group * HW + near * EIGHTH, EIGHTH)
        eighths.append(base[:, pl.ds(start, EIGHTH)])
    rows = base.shape[0]
    batch = packed.shape[0] // WRITES
    writes = []
    for step in range(WRITES):
        for device in range(step * batch, (step + 1) * batch):
            packed[device, :, :EIGHTH] = eighths[device % 4]
            packed[device, :, EIGHTH : EIGHTH + SIDE] = sides[device % 2]
            columns = base[:, device * SHARE : (device + 1) * SHARE]
            packed[device, :, EIGHTH + SIDE :] = jnp.concatenate(
                [columns, jnp.zeros((rows, PART - SHARE), BF)], axis=1
            )
        span = pl.ds(step * batch, batch)
        write = pltpu.make_async_copy(packed.at[span], packed_ref.at[span], write_sem.at[step])
        write.start()
        writes.append(write)
    for write in writes:
        write.wait()


def prompt_kernel(text_0_ref, text_1_ref, text_2_ref, text_3_ref, prompts_ref, prompt_ref):
    for index, text_ref in enumerate((text_0_ref, text_1_ref, text_2_ref, text_3_ref)):
        prompts_ref[index * TXT : (index + 1) * TXT, :] = unit_rows(text_ref[...])
    prompt_ref[...] = prompts_ref[:TXT, :]


def sum_kernel(shares_ref, down_ref, up_ref):
    total = jnp.sum(shares_ref[...].astype(F32), axis=0)
    down_ref[...] = total[:, : 3 * RANK]
    for block in range(3):
        up_ref[block] = total[:, (3 + block) * RANK : (4 + block) * RANK]


def fold_kernel(
    latent_in_ref, modulation_ref, packed_ref, share_ref, columns, shares, read_sem, write_sem
):
    read = pltpu.make_async_copy(packed_ref.at[:, EIGHTH + SIDE :], columns, read_sem.at[0])
    read.start()
    scaled_in = (latent_in_ref[...].astype(F32) * modulation_ref[...]).astype(BF)
    folds = jnp.concatenate([latent_in_ref[...], scaled_in], axis=0)
    read.wait()
    share = dot(folds, columns[...]).T[:SHARE].astype(BF)
    batch = shares.shape[0]
    for device in range(batch):
        shares[device] = share
    writes = [
        pltpu.make_async_copy(shares, share_ref.at[pl.ds(step * batch, batch)], write_sem.at[step])
        for step in range(share_ref.shape[0] // batch)
    ]
    for write in writes:
        write.start()
    for write in writes:
        write.wait()


def mix_kernel(prompts_ref, packed_ref, mine_ref, theirs_ref, columns, read_sem):
    read = pltpu.make_async_copy(packed_ref.at[:, :EIGHTH], columns, read_sem.at[0])
    read.start()
    read.wait()
    eighth = dot(prompts_ref[...], columns[...]).astype(BF)
    mine_ref[:TXT, :] = eighth[:TXT]
    theirs_ref[:TXT, :] = eighth[TXT : 2 * TXT]
    mine_ref[TXT:, :] = eighth[2 * TXT : 3 * TXT]
    theirs_ref[TXT:, :] = eighth[3 * TXT :]


def pair_kernel(mine_ref, received_ref, own_ref, near_ref):
    for place, part_ref in enumerate((mine_ref, received_ref)):
        own_ref[place] = part_ref[:TXT, :]
        near_ref[place] = part_ref[TXT:, :]


def forward_kernel(
    place_ref,
    sigma_ref,
    latent_ref,
    fresh_ref,
    prompt_ref,
    latent_in_ref,
    modulation_ref,
    velocity_out_ref,
    fold_ref,
    text_0_ref,
    text_1_ref,
    text_2_ref,
    text_3_ref,
    packed_own_ref,
    packed_core_ref,
    sample_ref,
    sample_again_ref,
    velocity_ref,
    narrow_velocity_ref,
    q_ref,
    k_ref,
    v_ref,
    weights_ref,
    inverse_ref,
    attended_ref,
    reduced_ref,
    picture_ref,
    role_up_ref,
    stacked,
    q_now,
    k_now,
    v_now,
    attended_now,
    text,
    sides,
    sem,
):
    group, near, core = place_ref[0], place_ref[1], place_ref[2]
    sigma = sigma_ref[0, 0]
    lanes = slice(EIGHTH, EIGHTH + SIDE)
    reads = [
        pltpu.make_async_copy(packed_own_ref.at[:, lanes], sides.at[core], sem.at[0]),
        pltpu.make_async_copy(packed_core_ref.at[:, lanes], sides.at[1 - core], sem.at[1]),
    ]
    for read in reads:
        read.start()
    downs, ups = sides.at[0], sides.at[1]
    for (across, move), text_ref in zip(MOVES, (text_0_ref, text_1_ref, text_2_ref, text_3_ref)):
        for place in range(2):
            start = (group ^ across) * HW + (near ^ move ^ place) * EIGHTH
            text[:, pl.ds(pl.multiple_of(start, EIGHTH), EIGHTH)] = text_ref[place]

    def readout(latent, noise_level, role, switch, save):
        base = role * 3 * RANK
        narrow = latent.T.astype(BF)
        hidden = dot(narrow, latent_in_ref[...])
        inverse_rms = lax.rsqrt(jnp.mean(hidden * hidden, axis=-1, keepdims=True) + 1e-06)
        picture = (hidden * inverse_rms * (1.0 + noise_level * modulation_ref[...])).astype(BF)
        if role == 0:
            for read in reads:
                read.wait()
            role_up_ref[...] = ups[:, 3 * RANK :]
        reduced_picture = dot(picture, downs[:, base : base + 3 * RANK]).astype(BF)
        reduced_prompt = dot(prompt_ref[:TXT, :], downs[:, base : base + 3 * RANK]).astype(BF)

        @save
        def _():
            picture_ref[...] = picture
            reduced_ref[TXT:, :] = reduced_picture
            reduced_ref[:TXT, :] = reduced_prompt

        if switch is not None:
            reduced_picture = reduced_picture * switch.astype(BF)
            reduced_prompt = reduced_prompt * switch.astype(BF)
        scaled_high, scaled_low = high_low(narrow.astype(F32) * inverse_rms)
        for block, now in enumerate((q_now, k_now, v_now)):
            rank_span = slice(block * RANK, (block + 1) * RANK)
            up_span = slice(base + block * RANK, base + (block + 1) * RANK)
            left = jnp.concatenate(
                [scaled_high, scaled_low, scaled_high, reduced_picture[:, rank_span]], axis=1
            )
            for start in range(0, HW, CHUNK):
                own = slice(start, start + CHUNK)
                wide = slice(block * HW + start, block * HW + start + CHUNK)
                parts = fold_ref[wide, :].astype(F32)
                fold_high, fold_low = high_low(parts[:, :CH] + noise_level * parts[:, CH:])
                up = ups[own, up_span]
                stacked[...] = jnp.concatenate([fold_high, fold_high, fold_low, up], axis=1)
                picture_part = dot(left, stacked[...], 1, 1).astype(BF)
                if block == 0:
                    now[:, own] = picture_part
                else:
                    now[TXT:, own] = picture_part
                    text_span = slice((block - 1) * HW + start, (block - 1) * HW + start + CHUNK)
                    adapter = dot(reduced_prompt[:, rank_span], up, 1, 1)
                    now[:TXT, own] = (text[:, text_span].astype(F32) + adapter).astype(BF)

        def head(index, carry):
            span = pl.ds(pl.multiple_of(index * HD, HD), HD)
            queries, keys, values = q_now[:, span], k_now[:, span], v_now[:, span]
            scores = dot(queries, keys, 1, 1) * SCALE
            largest = jnp.max(scores, axis=-1, keepdims=True)
            weights = jnp.exp(scores - largest)
            inverse = 1.0 / jnp.sum(weights, axis=-1, keepdims=True)
            weights = weights.astype(BF)
            attended = (dot(weights, values) * inverse).astype(BF)
            attended_now[:, span] = attended

            @save
            def _():
                q_ref[:, span] = queries
                k_ref[:, span] = keys
                v_ref[:, span] = values
                attended_ref[:, span] = attended
                weights_ref[index] = weights
                inverse_ref[index] = inverse

            return carry

        lax.fori_loop(0, HEADS, head, 0, unroll=2)
        return dot(velocity_out_ref[...], attended_now[...], 1, 1)

    latent = latent_ref[...]
    sample = latent - readout(latent, 1.0, 0, None, lambda f: f())
    sample_ref[...] = sample
    sample_again_ref[...] = sample
    noised = (1.0 - sigma) * sample + sigma * fresh_ref[...]
    velocity = readout(noised, sigma, 1, group.astype(F32), pl.when(group == 1))
    velocity_ref[...] = velocity
    narrow_velocity_ref[...] = velocity.astype(BF)


def backward_kernel(
    place_ref,
    sigma_ref,
    sample_ref,
    fresh_ref,
    own_ref,
    fake_ref,
    prompt_ref,
    velocity_out_ref,
    role_up_ref,
    q_ref,
    k_ref,
    v_ref,
    weights_ref,
    inverse_ref,
    attended_ref,
    reduced_ref,
    picture_ref,
    mine_ref,
    theirs_ref,
    grad_q,
    grad_k,
    grad_v,
    grads,
):
    flag = place_ref[0]
    sigma = sigma_ref[0, 0]
    sample = sample_ref[...]
    own = own_ref[...]
    noised = (1.0 - sigma) * sample + sigma * fresh_ref[...]
    clean_real = noised - sigma * own
    clean_fake = noised - sigma * fake_ref[...].astype(F32)
    distance = jnp.sum(jnp.sum(jnp.abs(sample - clean_real), axis=1, keepdims=True), axis=0, keepdims=True)
    spread = distance * (1.0 / (IMG * CH)) + 1e-05
    cot_gen = -(clean_fake - clean_real) / spread
    cot_critic = 2.0 * (own - (fresh_ref[...] - sample)) / (IMG * CH)
    cotangent = jnp.where(flag == 0, cot_gen, cot_critic).T.astype(BF)

    def head(index, carry):
        span = pl.ds(pl.multiple_of(index * HD, HD), HD)
        queries, keys, values = q_ref[:, span], k_ref[:, span], v_ref[:, span]
        weights = weights_ref[index]
        upstream = dot(cotangent, velocity_out_ref[:, span]) * inverse_ref[index]
        inner = jnp.sum(upstream * attended_ref[:, span].astype(F32), axis=-1, keepdims=True)
        upstream = upstream.astype(BF)
        grad_v[:, span] = dot(weights, upstream, 0, 0).astype(BF)
        grad_weights = dot(upstream, values, 1, 1)
        grad_scores = (weights.astype(F32) * (grad_weights - inner) * SCALE).astype(BF)
        grad_q[:, span] = dot(grad_scores, keys).astype(BF)
        grad_k[:, span] = dot(grad_scores, queries, 0, 0).astype(BF)
        return carry

    lax.fori_loop(0, HEADS, head, 0, unroll=12)
    spans = [slice(block * RANK, (block + 1) * RANK) for block in range(3)]
    reduced_q = dot(grad_q[...], role_up_ref[:, spans[0]]).astype(BF)
    reduced_k = dot(grad_k[...], role_up_ref[:, spans[1]]).astype(BF)
    reduced_v = dot(grad_v[...], role_up_ref[:, spans[2]]).astype(BF)
    reduced_kv = jnp.concatenate([reduced_k, reduced_v], axis=1)
    down_q = dot(reduced_q, picture_ref[...], 0, 0)
    down_kv = dot(reduced_kv[:TXT], prompt_ref[:TXT, :], 0, 0) + dot(reduced_kv[TXT:], picture_ref[...], 0, 0)
    up_q = dot(reduced_ref[TXT:, spans[0]], grad_q[...], 0, 0)
    up_k = dot(reduced_ref[:, spans[1]], grad_k[...], 0, 0)
    up_v = dot(reduced_ref[:, spans[2]], grad_v[...], 0, 0)
    grads[...] = jnp.concatenate([down_q, down_kv, up_q, up_k, up_v], axis=0).T
    core = place_ref[2]
    pairs, rows, _ = mine_ref.shape
    for pair in range(pairs):
        mine = pl.ds(pl.multiple_of((2 * pair + core) * rows, 8), rows)
        theirs = pl.ds(pl.multiple_of((2 * pair + 1 - core) * rows, 8), rows)
        mine_ref[pair] = grads[mine, :]
        theirs_ref[pair] = grads[theirs, :].astype(BF)


def add_kernel(mine_ref, received_ref, sums_ref):
    sums_ref[...] = (mine_ref[...] + received_ref[...].astype(F32)).astype(BF)


def run(kernel, name, megabytes, scalars, outputs, scratch, *operands, far=(), far_out=()):
    shapes = tuple(jax.ShapeDtypeStruct(*output) for output in outputs)
    return pl.pallas_call(
        kernel,
        out_shape=shapes,
        in_specs=[
            pl.BlockSpec(
                memory_space=pltpu.SMEM if k < scalars else pl.ANY if k in far else pltpu.VMEM
            )
            for k in range(len(operands))
        ],
        out_specs=tuple(
            pl.BlockSpec(memory_space=pl.ANY if k in far_out else pltpu.VMEM)
            for k in range(len(outputs))
        ),
        scratch_shapes=scratch,
        compiler_params=pltpu.CompilerParams(vmem_limit_bytes=megabytes * 2**20),
        name=name,
    )(*operands)


def per_device(
    latent_noise,
    fresh_noise,
    text_states,
    step_index,
    base_qkv,
    latent_in,
    modulation,
    velocity_out,
    gen_down,
    gen_up,
    critic_down,
    critic_up,
):
    devices = lax.axis_size("fsdp")
    group = lax.axis_index("group")
    index = lax.axis_index("fsdp")
    place = jnp.stack([group, lax.rem(index, 4), lax.rem(index, 2)]).astype(jnp.int32)
    sigma = ((step_index + 1).astype(F32) / NSTEPS).reshape(1, 1)
    shard = base_qkv.shape[0]

    def move(array, across, near):
        pairs = [
            (g * devices + device, (g ^ across) * devices + (device ^ near))
            for g in range(2)
            for device in range(devices)
        ]
        return lax.ppermute(array, ("group", "fsdp"), pairs)

    latent = latent_noise[0].T
    fresh = fresh_noise[0].T
    text = text_states[0]
    gain = modulation.reshape(1, HW)
    out_map = velocity_out.T

    texts = [text, move(text, 0, 1), move(text, 1, 2), move(text, 1, 3)]
    (packed,) = run(
        pack_kernel,
        "pack",
        60,
        1,
        [((devices, shard, EIGHTH + SIDE + PART), BF)],
        [
            pltpu.VMEM((shard, 3 * HW), BF),
            pltpu.VMEM((2, shard, 3 * RANK), BF),
            pltpu.VMEM((2, 3, shard, RANK), BF),
            pltpu.VMEM((devices, shard, EIGHTH + SIDE + PART), BF),
            pltpu.SemaphoreType.DMA((5,)),
            pltpu.SemaphoreType.DMA((WRITES,)),
        ],
        place,
        base_qkv,
        gen_down,
        critic_down,
        gen_up.transpose(0, 2, 1),
        critic_up.transpose(0, 2, 1),
        far=(1, 2, 3, 4, 5),
        far_out=(0,),
    )
    packed = lax.all_to_all(packed, "fsdp", 0, 0).reshape(HW, EIGHTH + SIDE + PART)
    prompts, prompt = run(
        prompt_kernel, "prompts", 16, 0, [((4 * TXT, HW), BF), ((TXT, HW), BF)], [], *texts
    )
    packed, prompts = lax.optimization_barrier((packed, prompts))
    (share,) = run(
        fold_kernel,
        "fold",
        16,
        0,
        [((devices, SHARE, PART), BF)],
        [
            pltpu.VMEM((HW, PART), BF),
            pltpu.VMEM((devices // 8, SHARE, PART), BF),
            pltpu.SemaphoreType.DMA((1,)),
            pltpu.SemaphoreType.DMA((8,)),
        ],
        latent_in,
        gain,
        packed,
        far=(2,),
        far_out=(0,),
    )
    fold = lax.all_to_all(share, "fsdp", 0, 0).reshape(devices * SHARE, PART)
    packed_core = move(packed, 0, 1)
    prompts, packed_core = lax.optimization_barrier((prompts, packed_core))
    mine, theirs = run(
        mix_kernel,
        "mix",
        16,
        0,
        [((2 * TXT, EIGHTH), BF)] * 2,
        [pltpu.VMEM((HW, EIGHTH), BF), pltpu.SemaphoreType.DMA((1,))],
        prompts,
        packed,
        far=(1,),
    )
    received = move(theirs, 0, 1)
    own_pair, near_pair = run(
        pair_kernel, "pair", 16, 0, [((2, TXT, EIGHTH), BF)] * 2, [], mine, received
    )
    pieces = [own_pair, move(own_pair, 1, 0), move(near_pair, 0, 2), move(near_pair, 1, 2)]

    sample, sample_again, velocity, narrow_velocity, *saved, role_up = run(
        forward_kernel,
        "forward",
        32,
        2,
        [
            ((CH, IMG), F32),
            ((CH, IMG), F32),
            ((CH, IMG), F32),
            ((CH, IMG), BF),
            ((IMG, HW), BF),
            ((ROWS, HW), BF),
            ((ROWS, HW), BF),
            ((HEADS, IMG, ROWS), BF),
            ((HEADS, IMG, 1), F32),
            ((IMG, HW), BF),
            ((ROWS, 3 * RANK), BF),
            ((IMG, HW), BF),
            ((HW, 3 * RANK), BF),
        ],
        [
            pltpu.VMEM((CHUNK, 4 * CH), BF),
            pltpu.VMEM((IMG, HW), BF),
            pltpu.VMEM((ROWS, HW), BF),
            pltpu.VMEM((ROWS, HW), BF),
            pltpu.VMEM((IMG, HW), BF),
            pltpu.VMEM((TXT, 2 * HW), BF),
            pltpu.VMEM((2, HW, SIDE), BF),
            pltpu.SemaphoreType.DMA((2,)),
        ],
        place,
        sigma,
        latent,
        fresh,
        prompt,
        latent_in,
        gain,
        out_map,
        fold,
        *pieces,
        packed,
        packed_core,
        far=(13, 14),
    )
    fake_velocity = lax.ppermute(narrow_velocity, "group", [(1, 0)])
    half = (devices // 2, shard, SIDE)
    mine, theirs = run(
        backward_kernel,
        "backward",
        24,
        2,
        [(half, F32), (half, BF)],
        [
            pltpu.VMEM((IMG, HW), BF),
            pltpu.VMEM((ROWS, HW), BF),
            pltpu.VMEM((ROWS, HW), BF),
            pltpu.VMEM((HW, SIDE), F32),
        ],
        place,
        sigma,
        sample_again,
        fresh,
        velocity,
        fake_velocity,
        prompt,
        out_map,
        role_up,
        *saved,
    )
    (sums,) = run(add_kernel, "add", 16, 0, [(half, BF)], [], mine, move(theirs, 0, 1))
    parities = [list(range(core, devices, 2)) for core in range(2)]
    shares = lax.all_to_all(sums, "fsdp", 0, 0, axis_index_groups=parities)
    share_down, share_up = run(
        sum_kernel,
        "total",
        16,
        0,
        [((shard, 3 * RANK), F32), ((3, shard, RANK), F32)],
        [],
        shares,
    )
    return (sample.T[None], share_down[None], share_up.transpose(0, 2, 1)[None])


def solution(mesh):
    in_specs = (
        P("fsdp", None, None),
        P("fsdp", None, None),
        P("fsdp", None, None),
        P("fsdp"),
        P("fsdp", None),
        P(),
        P(),
        P(),
        P("fsdp", None),
        P(None, None, "fsdp"),
        P("fsdp", None),
        P(None, None, "fsdp"),
    )
    out_specs = (P("fsdp", None, None), P("group", "fsdp", None), P("group", None, None, "fsdp"))
    return jax.shard_map(
        per_device, mesh=mesh, in_specs=in_specs, out_specs=out_specs, check_vma=False
    )
```

```python
import jax
import jax.numpy as jnp
from jax import lax
from jax.experimental import pallas as pl
from jax.experimental.pallas import tpu as pltpu
from jax.sharding import PartitionSpec as P

HEADS = 12
HD = 128
CH = 64
RANK = 64
NSTEPS = 1000
IMG = 256
TXT = 128
ROWS = TXT + IMG
HW = HEADS * HD
CHUNK = 512
EIGHTH = HW // 4
SIDE = 6 * RANK
SHARE = 72
PART = 128
WRITES = 4
MOVES = ((0, 0), (1, 0), (0, 2), (1, 2))
BF = jnp.bfloat16
F32 = jnp.float32
SCALE = HD ** (-0.5)


def dot(left, right, left_dim=1, right_dim=0):
    dims = (((left_dim,), (right_dim,)), ((), ()))
    return lax.dot_general(left, right, dims, preferred_element_type=F32)


def high_low(values):
    high = values.astype(BF)
    return high, (values - high.astype(F32)).astype(BF)


def unit_rows(values):
    values = values.astype(F32)
    return (values * lax.rsqrt(jnp.mean(values * values, axis=-1, keepdims=True) + 1e-06)).astype(BF)


def pack_kernel(
    place_ref,
    base_ref,
    gen_down_ref,
    critic_down_ref,
    gen_up_ref,
    critic_up_ref,
    packed_ref,
    base,
    downs,
    ups,
    packed,
    read_sem,
    write_sem,
):
    reads = [
        pltpu.make_async_copy(base_ref, base, read_sem.at[0]),
        pltpu.make_async_copy(gen_down_ref, downs.at[0], read_sem.at[1]),
        pltpu.make_async_copy(critic_down_ref, downs.at[1], read_sem.at[2]),
        pltpu.make_async_copy(gen_up_ref, ups.at[0], read_sem.at[3]),
        pltpu.make_async_copy(critic_up_ref, ups.at[1], read_sem.at[4]),
    ]
    for read in reads:
        read.start()
    for read in reads:
        read.wait()
    group = place_ref[0]

    def both(gen, critic):
        gen, critic = gen.astype(F32), critic.astype(F32)
        return jnp.concatenate([gen, jnp.where(group == 0, gen, critic)], axis=1).astype(BF)

    up_rows = [jnp.concatenate([ups[role, block] for block in range(3)], axis=1) for role in range(2)]
    sides = (both(downs[0], downs[1]), both(up_rows[0], up_rows[1]))
    eighths = []
    for near in range(4):
        start = pl.multiple_of(HW + group * HW + near * EIGHTH, EIGHTH)
        eighths.append(base[:, pl.ds(start, EIGHTH)])
    rows = base.shape[0]
    batch = packed.shape[0] // WRITES
    writes = []
    for step in range(WRITES):
        for device in range(step * batch, (step + 1) * batch):
            packed[device, :, :EIGHTH] = eighths[device % 4]
            packed[device, :, EIGHTH : EIGHTH + SIDE] = sides[device % 2]
            columns = base[:, device * SHARE : (device + 1) * SHARE]
            packed[device, :, EIGHTH + SIDE :] = jnp.concatenate(
                [columns, jnp.zeros((rows, PART - SHARE), BF)], axis=1
            )
        span = pl.ds(step * batch, batch)
        write = pltpu.make_async_copy(packed.at[span], packed_ref.at[span], write_sem.at[step])
        write.start()
        writes.append(write)
    for write in writes:
        write.wait()


def prompt_kernel(text_0_ref, text_1_ref, text_2_ref, text_3_ref, prompts_ref, prompt_ref):
    for index, text_ref in enumerate((text_0_ref, text_1_ref, text_2_ref, text_3_ref)):
        prompts_ref[index * TXT : (index + 1) * TXT, :] = unit_rows(text_ref[...])
    prompt_ref[...] = prompts_ref[:TXT, :]


def sum_kernel(shares_ref, down_ref, up_ref):
    total = jnp.sum(shares_ref[...].astype(F32), axis=0)
    down_ref[...] = total[:, : 3 * RANK]
    for block in range(3):
        up_ref[block] = total[:, (3 + block) * RANK : (4 + block) * RANK]


def fold_kernel(
    latent_in_ref, modulation_ref, packed_ref, share_ref, columns, shares, read_sem, write_sem
):
    read = pltpu.make_async_copy(packed_ref.at[:, EIGHTH + SIDE :], columns, read_sem.at[0])
    read.start()
    scaled_in = (latent_in_ref[...].astype(F32) * modulation_ref[...]).astype(BF)
    folds = jnp.concatenate([latent_in_ref[...], scaled_in], axis=0)
    read.wait()
    share = dot(folds, columns[...]).T[:SHARE].astype(BF)
    batch = shares.shape[0]
    for device in range(batch):
        shares[device] = share
    writes = [
        pltpu.make_async_copy(shares, share_ref.at[pl.ds(step * batch, batch)], write_sem.at[step])
        for step in range(share_ref.shape[0] // batch)
    ]
    for write in writes:
        write.start()
    for write in writes:
        write.wait()


def mix_kernel(prompts_ref, packed_ref, mine_ref, theirs_ref, columns, read_sem):
    read = pltpu.make_async_copy(packed_ref.at[:, :EIGHTH], columns, read_sem.at[0])
    read.start()
    read.wait()
    eighth = dot(prompts_ref[...], columns[...]).astype(BF)
    mine_ref[:TXT, :] = eighth[:TXT]
    theirs_ref[:TXT, :] = eighth[TXT : 2 * TXT]
    mine_ref[TXT:, :] = eighth[2 * TXT : 3 * TXT]
    theirs_ref[TXT:, :] = eighth[3 * TXT :]


def pair_kernel(mine_ref, received_ref, own_ref, near_ref):
    for place, part_ref in enumerate((mine_ref, received_ref)):
        own_ref[place] = part_ref[:TXT, :]
        near_ref[place] = part_ref[TXT:, :]


def forward_kernel(
    place_ref,
    sigma_ref,
    latent_ref,
    fresh_ref,
    prompt_ref,
    latent_in_ref,
    modulation_ref,
    velocity_out_ref,
    fold_ref,
    text_0_ref,
    text_1_ref,
    text_2_ref,
    text_3_ref,
    packed_own_ref,
    packed_core_ref,
    sample_ref,
    sample_again_ref,
    velocity_ref,
    narrow_velocity_ref,
    q_ref,
    k_ref,
    v_ref,
    weights_ref,
    inverse_ref,
    attended_ref,
    reduced_ref,
    picture_ref,
    role_up_ref,
    stacked,
    q_now,
    k_now,
    v_now,
    attended_now,
    text,
    sides,
    sem,
):
    group, near, core = place_ref[0], place_ref[1], place_ref[2]
    sigma = sigma_ref[0, 0]
    lanes = slice(EIGHTH, EIGHTH + SIDE)
    reads = [
        pltpu.make_async_copy(packed_own_ref.at[:, lanes], sides.at[core], sem.at[0]),
        pltpu.make_async_copy(packed_core_ref.at[:, lanes], sides.at[1 - core], sem.at[1]),
    ]
    for read in reads:
        read.start()
    downs, ups = sides.at[0], sides.at[1]
    for (across, move), text_ref in zip(MOVES, (text_0_ref, text_1_ref, text_2_ref, text_3_ref)):
        for place in range(2):
            start = (group ^ across) * HW + (near ^ move ^ place) * EIGHTH
            text[:, pl.ds(pl.multiple_of(start, EIGHTH), EIGHTH)] = text_ref[place]

    def readout(latent, noise_level, role, switch, save):
        base = role * 3 * RANK
        narrow = latent.T.astype(BF)
        hidden = dot(narrow, latent_in_ref[...])
        inverse_rms = lax.rsqrt(jnp.mean(hidden * hidden, axis=-1, keepdims=True) + 1e-06)
        picture = (hidden * inverse_rms * (1.0 + noise_level * modulation_ref[...])).astype(BF)
        if role == 0:
            for read in reads:
                read.wait()
            role_up_ref[...] = ups[:, 3 * RANK :]
        reduced_picture = dot(picture, downs[:, base : base + 3 * RANK]).astype(BF)
        reduced_prompt = dot(prompt_ref[:TXT, :], downs[:, base : base + 3 * RANK]).astype(BF)

        @save
        def _():
            picture_ref[...] = picture
            reduced_ref[TXT:, :] = reduced_picture
            reduced_ref[:TXT, :] = reduced_prompt

        if switch is not None:
            reduced_picture = reduced_picture * switch.astype(BF)
            reduced_prompt = reduced_prompt * switch.astype(BF)
        scaled_high, scaled_low = high_low(narrow.astype(F32) * inverse_rms)
        for block, now in enumerate((q_now, k_now, v_now)):
            rank_span = slice(block * RANK, (block + 1) * RANK)
            up_span = slice(base + block * RANK, base + (block + 1) * RANK)
            left = jnp.concatenate(
                [scaled_high, scaled_low, scaled_high, reduced_picture[:, rank_span]], axis=1
            )
            for start in range(0, HW, CHUNK):
                own = slice(start, start + CHUNK)
                wide = slice(block * HW + start, block * HW + start + CHUNK)
                parts = fold_ref[wide, :].astype(F32)
                fold_high, fold_low = high_low(parts[:, :CH] + noise_level * parts[:, CH:])
                up = ups[own, up_span]
                stacked[...] = jnp.concatenate([fold_high, fold_high, fold_low, up], axis=1)
                picture_part = dot(left, stacked[...], 1, 1).astype(BF)
                if block == 0:
                    now[:, own] = picture_part
                else:
                    now[TXT:, own] = picture_part
                    text_span = slice((block - 1) * HW + start, (block - 1) * HW + start + CHUNK)
                    adapter = dot(reduced_prompt[:, rank_span], up, 1, 1)
                    now[:TXT, own] = (text[:, text_span].astype(F32) + adapter).astype(BF)

        def head(index, carry):
            span = pl.ds(pl.multiple_of(index * HD, HD), HD)
            queries, keys, values = q_now[:, span], k_now[:, span], v_now[:, span]
            scores = dot(queries, keys, 1, 1) * SCALE
            largest = jnp.max(scores, axis=-1, keepdims=True)
            weights = jnp.exp(scores - largest)
            inverse = 1.0 / jnp.sum(weights, axis=-1, keepdims=True)
            weights = weights.astype(BF)
            attended = (dot(weights, values) * inverse).astype(BF)
            attended_now[:, span] = attended

            @save
            def _():
                q_ref[:, span] = queries
                k_ref[:, span] = keys
                v_ref[:, span] = values
                attended_ref[:, span] = attended
                weights_ref[index] = weights
                inverse_ref[index] = inverse

            return carry

        lax.fori_loop(0, HEADS, head, 0, unroll=2)
        return dot(velocity_out_ref[...], attended_now[...], 1, 1)

    latent = latent_ref[...]
    sample = latent - readout(latent, 1.0, 0, None, lambda f: f())
    sample_ref[...] = sample
    sample_again_ref[...] = sample
    noised = (1.0 - sigma) * sample + sigma * fresh_ref[...]
    velocity = readout(noised, sigma, 1, group.astype(F32), pl.when(group == 1))
    velocity_ref[...] = velocity
    narrow_velocity_ref[...] = velocity.astype(BF)


def backward_kernel(
    place_ref,
    sigma_ref,
    sample_ref,
    fresh_ref,
    own_ref,
    fake_ref,
    prompt_ref,
    velocity_out_ref,
    role_up_ref,
    q_ref,
    k_ref,
    v_ref,
    weights_ref,
    inverse_ref,
    attended_ref,
    reduced_ref,
    picture_ref,
    mine_ref,
    theirs_ref,
    grad_q,
    grad_k,
    grad_v,
    grads,
):
    flag = place_ref[0]
    sigma = sigma_ref[0, 0]
    sample = sample_ref[...]
    own = own_ref[...]
    noised = (1.0 - sigma) * sample + sigma * fresh_ref[...]
    clean_real = noised - sigma * own
    clean_fake = noised - sigma * fake_ref[...].astype(F32)
    distance = jnp.sum(jnp.sum(jnp.abs(sample - clean_real), axis=1, keepdims=True), axis=0, keepdims=True)
    spread = distance * (1.0 / (IMG * CH)) + 1e-05
    cot_gen = -(clean_fake - clean_real) / spread
    cot_critic = 2.0 * (own - (fresh_ref[...] - sample)) / (IMG * CH)
    cotangent = jnp.where(flag == 0, cot_gen, cot_critic).T.astype(BF)

    def head(index, carry):
        span = pl.ds(pl.multiple_of(index * HD, HD), HD)
        queries, keys, values = q_ref[:, span], k_ref[:, span], v_ref[:, span]
        weights = weights_ref[index]
        upstream = dot(cotangent, velocity_out_ref[:, span]) * inverse_ref[index]
        inner = jnp.sum(upstream * attended_ref[:, span].astype(F32), axis=-1, keepdims=True)
        upstream = upstream.astype(BF)
        grad_v[:, span] = dot(weights, upstream, 0, 0).astype(BF)
        grad_weights = dot(upstream, values, 1, 1)
        grad_scores = (weights.astype(F32) * (grad_weights - inner) * SCALE).astype(BF)
        grad_q[:, span] = dot(grad_scores, keys).astype(BF)
        grad_k[:, span] = dot(grad_scores, queries, 0, 0).astype(BF)
        return carry

    lax.fori_loop(0, HEADS, head, 0, unroll=12)
    spans = [slice(block * RANK, (block + 1) * RANK) for block in range(3)]
    reduced_q = dot(grad_q[...], role_up_ref[:, spans[0]]).astype(BF)
    reduced_k = dot(grad_k[...], role_up_ref[:, spans[1]]).astype(BF)
    reduced_v = dot(grad_v[...], role_up_ref[:, spans[2]]).astype(BF)
    reduced_kv = jnp.concatenate([reduced_k, reduced_v], axis=1)
    down_q = dot(reduced_q, picture_ref[...], 0, 0)
    down_kv = dot(reduced_kv[:TXT], prompt_ref[:TXT, :], 0, 0) + dot(reduced_kv[TXT:], picture_ref[...], 0, 0)
    up_q = dot(reduced_ref[TXT:, spans[0]], grad_q[...], 0, 0)
    up_k = dot(reduced_ref[:, spans[1]], grad_k[...], 0, 0)
    up_v = dot(reduced_ref[:, spans[2]], grad_v[...], 0, 0)
    grads[...] = jnp.concatenate([down_q, down_kv, up_q, up_k, up_v], axis=0).T
    core = place_ref[2]
    pairs, rows, _ = mine_ref.shape
    for pair in range(pairs):
        mine = pl.ds(pl.multiple_of((2 * pair + core) * rows, 8), rows)
        theirs = pl.ds(pl.multiple_of((2 * pair + 1 - core) * rows, 8), rows)
        mine_ref[pair] = grads[mine, :]
        theirs_ref[pair] = grads[theirs, :].astype(BF)


def add_kernel(mine_ref, received_ref, sums_ref):
    sums_ref[...] = (mine_ref[...] + received_ref[...].astype(F32)).astype(BF)


def run(kernel, name, megabytes, scalars, outputs, scratch, *operands, far=(), far_out=()):
    shapes = tuple(jax.ShapeDtypeStruct(*output) for output in outputs)
    return pl.pallas_call(
        kernel,
        out_shape=shapes,
        in_specs=[
            pl.BlockSpec(
                memory_space=pltpu.SMEM if k < scalars else pl.ANY if k in far else pltpu.VMEM
            )
            for k in range(len(operands))
        ],
        out_specs=tuple(
            pl.BlockSpec(memory_space=pl.ANY if k in far_out else pltpu.VMEM)
            for k in range(len(outputs))
        ),
        scratch_shapes=scratch,
        compiler_params=pltpu.CompilerParams(vmem_limit_bytes=megabytes * 2**20),
        name=name,
    )(*operands)


def per_device(
    latent_noise,
    fresh_noise,
    text_states,
    step_index,
    base_qkv,
    latent_in,
    modulation,
    velocity_out,
    gen_down,
    gen_up,
    critic_down,
    critic_up,
):
    devices = lax.axis_size("fsdp")
    group = lax.axis_index("group")
    index = lax.axis_index("fsdp")
    place = jnp.stack([group, lax.rem(index, 4), lax.rem(index, 2)]).astype(jnp.int32)
    sigma = ((step_index + 1).astype(F32) / NSTEPS).reshape(1, 1)
    shard = base_qkv.shape[0]

    def move(array, across, near):
        pairs = [
            (g * devices + device, (g ^ across) * devices + (device ^ near))
            for g in range(2)
            for device in range(devices)
        ]
        return lax.ppermute(array, ("group", "fsdp"), pairs)

    latent = latent_noise[0].T
    fresh = fresh_noise[0].T
    text = text_states[0]
    gain = modulation.reshape(1, HW)
    out_map = velocity_out.T

    texts = [text, move(text, 0, 1), move(text, 1, 2), move(text, 1, 3)]
    (packed,) = run(
        pack_kernel,
        "pack",
        60,
        1,
        [((devices, shard, EIGHTH + SIDE + PART), BF)],
        [
            pltpu.VMEM((shard, 3 * HW), BF),
            pltpu.VMEM((2, shard, 3 * RANK), BF),
            pltpu.VMEM((2, 3, shard, RANK), BF),
            pltpu.VMEM((devices, shard, EIGHTH + SIDE + PART), BF),
            pltpu.SemaphoreType.DMA((5,)),
            pltpu.SemaphoreType.DMA((WRITES,)),
        ],
        place,
        base_qkv,
        gen_down,
        critic_down,
        gen_up.transpose(0, 2, 1),
        critic_up.transpose(0, 2, 1),
        far=(1, 2, 3, 4, 5),
        far_out=(0,),
    )
    packed = lax.all_to_all(packed, "fsdp", 0, 0).reshape(HW, EIGHTH + SIDE + PART)
    prompts, prompt = run(
        prompt_kernel, "prompts", 16, 0, [((4 * TXT, HW), BF), ((TXT, HW), BF)], [], *texts
    )
    packed, prompts = lax.optimization_barrier((packed, prompts))
    (share,) = run(
        fold_kernel,
        "fold",
        60,
        0,
        [((devices, SHARE, PART), BF)],
        [
            pltpu.VMEM((HW, PART), BF),
            pltpu.VMEM((devices // 8, SHARE, PART), BF),
            pltpu.SemaphoreType.DMA((1,)),
            pltpu.SemaphoreType.DMA((8,)),
        ],
        latent_in,
        gain,
        packed,
        far=(2,),
        far_out=(0,),
    )
    fold = lax.all_to_all(share, "fsdp", 0, 0).reshape(devices * SHARE, PART)
    packed_core = move(packed, 0, 1)
    prompts, packed_core = lax.optimization_barrier((prompts, packed_core))
    mine, theirs = run(
        mix_kernel,
        "mix",
        60,
        0,
        [((2 * TXT, EIGHTH), BF)] * 2,
        [pltpu.VMEM((HW, EIGHTH), BF), pltpu.SemaphoreType.DMA((1,))],
        prompts,
        packed,
        far=(1,),
    )
    received = move(theirs, 0, 1)
    own_pair, near_pair = run(
        pair_kernel, "pair", 16, 0, [((2, TXT, EIGHTH), BF)] * 2, [], mine, received
    )
    pieces = [own_pair, move(own_pair, 1, 0), move(near_pair, 0, 2), move(near_pair, 1, 2)]

    sample, sample_again, velocity, narrow_velocity, *saved, role_up = run(
        forward_kernel,
        "forward",
        32,
        2,
        [
            ((CH, IMG), F32),
            ((CH, IMG), F32),
            ((CH, IMG), F32),
            ((CH, IMG), BF),
            ((IMG, HW), BF),
            ((ROWS, HW), BF),
            ((ROWS, HW), BF),
            ((HEADS, IMG, ROWS), BF),
            ((HEADS, IMG, 1), F32),
            ((IMG, HW), BF),
            ((ROWS, 3 * RANK), BF),
            ((IMG, HW), BF),
            ((HW, 3 * RANK), BF),
        ],
        [
            pltpu.VMEM((CHUNK, 4 * CH), BF),
            pltpu.VMEM((IMG, HW), BF),
            pltpu.VMEM((ROWS, HW), BF),
            pltpu.VMEM((ROWS, HW), BF),
            pltpu.VMEM((IMG, HW), BF),
            pltpu.VMEM((TXT, 2 * HW), BF),
            pltpu.VMEM((2, HW, SIDE), BF),
            pltpu.SemaphoreType.DMA((2,)),
        ],
        place,
        sigma,
        latent,
        fresh,
        prompt,
        latent_in,
        gain,
        out_map,
        fold,
        *pieces,
        packed,
        packed_core,
        far=(13, 14),
    )
    fake_velocity = lax.ppermute(narrow_velocity, "group", [(1, 0)])
    half = (devices // 2, shard, SIDE)
    mine, theirs = run(
        backward_kernel,
        "backward",
        24,
        2,
        [(half, F32), (half, BF)],
        [
            pltpu.VMEM((IMG, HW), BF),
            pltpu.VMEM((ROWS, HW), BF),
            pltpu.VMEM((ROWS, HW), BF),
            pltpu.VMEM((HW, SIDE), F32),
        ],
        place,
        sigma,
        sample_again,
        fresh,
        velocity,
        fake_velocity,
        prompt,
        out_map,
        role_up,
        *saved,
    )
    (sums,) = run(add_kernel, "add", 16, 0, [(half, BF)], [], mine, move(theirs, 0, 1))
    parities = [list(range(core, devices, 2)) for core in range(2)]
    shares = lax.all_to_all(sums, "fsdp", 0, 0, axis_index_groups=parities)
    share_down, share_up = run(
        sum_kernel,
        "total",
        16,
        0,
        [((shard, 3 * RANK), F32), ((3, shard, RANK), F32)],
        [],
        shares,
    )
    return (sample.T[None], share_down[None], share_up.transpose(0, 2, 1)[None])


def solution(mesh):
    in_specs = (
        P("fsdp", None, None),
        P("fsdp", None, None),
        P("fsdp", None, None),
        P("fsdp"),
        P("fsdp", None),
        P(),
        P(),
        P(),
        P("fsdp", None),
        P(None, None, "fsdp"),
        P("fsdp", None),
        P(None, None, "fsdp"),
    )
    out_specs = (P("fsdp", None, None), P("group", "fsdp", None), P("group", None, None, "fsdp"))
    return jax.shard_map(
        per_device, mesh=mesh, in_specs=in_specs, out_specs=out_specs, check_vma=False
    )
```

```python
import jax
import jax.numpy as jnp
from jax import lax
from jax.experimental import pallas as pl
from jax.experimental.pallas import tpu as pltpu
from jax.sharding import PartitionSpec as P

HEADS = 12
HD = 128
CH = 64
RANK = 64
NSTEPS = 1000
IMG = 256
TXT = 128
ROWS = TXT + IMG
HW = HEADS * HD
CHUNK = 512
EIGHTH = HW // 4
SIDE = 6 * RANK
SHARE = 72
PART = 128
WRITES = 4
MOVES = ((0, 0), (1, 0), (0, 2), (1, 2))
BF = jnp.bfloat16
F32 = jnp.float32
SCALE = HD ** (-0.5)


def dot(left, right, left_dim=1, right_dim=0):
    dims = (((left_dim,), (right_dim,)), ((), ()))
    return lax.dot_general(left, right, dims, preferred_element_type=F32)


def high_low(values):
    high = values.astype(BF)
    return high, (values - high.astype(F32)).astype(BF)


def unit_rows(values):
    values = values.astype(F32)
    return (values * lax.rsqrt(jnp.mean(values * values, axis=-1, keepdims=True) + 1e-06)).astype(BF)


def pack_kernel(
    base_ref,
    gen_down_ref,
    critic_down_ref,
    gen_up_ref,
    critic_up_ref,
    packed_ref,
    base,
    downs,
    ups,
    packed,
    read_sem,
    write_sem,
):
    reads = [
        pltpu.make_async_copy(base_ref, base, read_sem.at[0]),
        pltpu.make_async_copy(gen_down_ref, downs.at[0], read_sem.at[1]),
        pltpu.make_async_copy(critic_down_ref, downs.at[1], read_sem.at[2]),
        pltpu.make_async_copy(gen_up_ref, ups.at[0], read_sem.at[3]),
        pltpu.make_async_copy(critic_up_ref, ups.at[1], read_sem.at[4]),
    ]
    for read in reads:
        read.start()
    for read in reads:
        read.wait()
    group = lax.axis_index("group")

    def both(gen, critic):
        gen, critic = gen.astype(F32), critic.astype(F32)
        return jnp.concatenate([gen, jnp.where(group == 0, gen, critic)], axis=1).astype(BF)

    up_rows = [jnp.concatenate([ups[role, block] for block in range(3)], axis=1) for role in range(2)]
    sides = (both(downs[0], downs[1]), both(up_rows[0], up_rows[1]))
    eighths = []
    for near in range(4):
        start = pl.multiple_of(HW + group * HW + near * EIGHTH, EIGHTH)
        eighths.append(base[:, pl.ds(start, EIGHTH)])
    rows = base.shape[0]
    batch = packed.shape[0] // WRITES
    writes = []
    for step in range(WRITES):
        for device in range(step * batch, (step + 1) * batch):
            packed[device, :, :EIGHTH] = eighths[device % 4]
            packed[device, :, EIGHTH : EIGHTH + SIDE] = sides[device % 2]
            columns = base[:, device * SHARE : (device + 1) * SHARE]
            packed[device, :, EIGHTH + SIDE :] = jnp.concatenate(
                [columns, jnp.zeros((rows, PART - SHARE), BF)], axis=1
            )
        span = pl.ds(step * batch, batch)
        write = pltpu.make_async_copy(packed.at[span], packed_ref.at[span], write_sem.at[step])
        write.start()
        writes.append(write)
    for write in writes:
        write.wait()


def prompt_kernel(text_0_ref, text_1_ref, text_2_ref, text_3_ref, prompts_ref, prompt_ref):
    for index, text_ref in enumerate((text_0_ref, text_1_ref, text_2_ref, text_3_ref)):
        prompts_ref[index * TXT : (index + 1) * TXT, :] = unit_rows(text_ref[...])
    prompt_ref[...] = prompts_ref[:TXT, :]


def sum_kernel(shares_ref, down_ref, up_ref):
    total = jnp.sum(shares_ref[...].astype(F32), axis=0)
    down_ref[...] = total[:, : 3 * RANK]
    for block in range(3):
        up_ref[block] = total[:, (3 + block) * RANK : (4 + block) * RANK]


def fold_kernel(
    latent_in_ref, modulation_ref, packed_ref, share_ref, columns, shares, read_sem, write_sem
):
    read = pltpu.make_async_copy(packed_ref.at[:, EIGHTH + SIDE :], columns, read_sem.at[0])
    read.start()
    scaled_in = (latent_in_ref[...].astype(F32) * modulation_ref[...]).astype(BF)
    folds = jnp.concatenate([latent_in_ref[...], scaled_in], axis=0)
    read.wait()
    share = dot(folds, columns[...]).T[:SHARE].astype(BF)
    batch = shares.shape[0]
    for device in range(batch):
        shares[device] = share
    writes = [
        pltpu.make_async_copy(shares, share_ref.at[pl.ds(step * batch, batch)], write_sem.at[step])
        for step in range(share_ref.shape[0] // batch)
    ]
    for write in writes:
        write.start()
    for write in writes:
        write.wait()


def mix_kernel(prompts_ref, packed_ref, mine_ref, theirs_ref, columns, read_sem):
    read = pltpu.make_async_copy(packed_ref.at[:, :EIGHTH], columns, read_sem.at[0])
    read.start()
    read.wait()
    eighth = dot(prompts_ref[...], columns[...]).astype(BF)
    mine_ref[:TXT, :] = eighth[:TXT]
    theirs_ref[:TXT, :] = eighth[TXT : 2 * TXT]
    mine_ref[TXT:, :] = eighth[2 * TXT : 3 * TXT]
    theirs_ref[TXT:, :] = eighth[3 * TXT :]


def pair_kernel(mine_ref, received_ref, own_ref, near_ref):
    for place, part_ref in enumerate((mine_ref, received_ref)):
        own_ref[place] = part_ref[:TXT, :]
        near_ref[place] = part_ref[TXT:, :]


def forward_kernel(
    place_ref,
    sigma_ref,
    latents_ref,
    prompt_ref,
    latent_in_ref,
    modulation_ref,
    velocity_out_ref,
    fold_ref,
    text_0_ref,
    text_1_ref,
    text_2_ref,
    text_3_ref,
    packed_own_ref,
    packed_core_ref,
    sample_ref,
    sample_again_ref,
    velocity_ref,
    narrow_velocity_ref,
    q_ref,
    k_ref,
    v_ref,
    weights_ref,
    inverse_ref,
    attended_ref,
    reduced_ref,
    picture_ref,
    role_up_ref,
    stacked,
    q_now,
    k_now,
    v_now,
    attended_now,
    text,
    sides,
    sem,
):
    group, near, core = place_ref[0], place_ref[1], place_ref[2]
    sigma = sigma_ref[0, 0]
    lanes = slice(EIGHTH, EIGHTH + SIDE)
    reads = [
        pltpu.make_async_copy(packed_own_ref.at[:, lanes], sides.at[core], sem.at[0]),
        pltpu.make_async_copy(packed_core_ref.at[:, lanes], sides.at[1 - core], sem.at[1]),
    ]
    for read in reads:
        read.start()
    downs, ups = sides.at[0], sides.at[1]
    for (across, move), text_ref in zip(MOVES, (text_0_ref, text_1_ref, text_2_ref, text_3_ref)):
        for place in range(2):
            start = (group ^ across) * HW + (near ^ move ^ place) * EIGHTH
            text[:, pl.ds(pl.multiple_of(start, EIGHTH), EIGHTH)] = text_ref[place]

    def readout(latent, noise_level, role, switch, save):
        base = role * 3 * RANK
        narrow = latent.T.astype(BF)
        hidden = dot(narrow, latent_in_ref[...])
        inverse_rms = lax.rsqrt(jnp.mean(hidden * hidden, axis=-1, keepdims=True) + 1e-06)
        picture = (hidden * inverse_rms * (1.0 + noise_level * modulation_ref[...])).astype(BF)
        if role == 0:
            for read in reads:
                read.wait()
            role_up_ref[...] = ups[:, 3 * RANK :]
        reduced_picture = dot(picture, downs[:, base : base + 3 * RANK]).astype(BF)
        reduced_prompt = dot(prompt_ref[:TXT, :], downs[:, base : base + 3 * RANK]).astype(BF)

        @save
        def _():
            picture_ref[...] = picture
            reduced_ref[TXT:, :] = reduced_picture
            reduced_ref[:TXT, :] = reduced_prompt

        if switch is not None:
            reduced_picture = reduced_picture * switch.astype(BF)
            reduced_prompt = reduced_prompt * switch.astype(BF)
        scaled_high, scaled_low = high_low(narrow.astype(F32) * inverse_rms)
        for block, now in enumerate((q_now, k_now, v_now)):
            rank_span = slice(block * RANK, (block + 1) * RANK)
            up_span = slice(base + block * RANK, base + (block + 1) * RANK)
            left = jnp.concatenate(
                [scaled_high, scaled_low, scaled_high, reduced_picture[:, rank_span]], axis=1
            )
            for start in range(0, HW, CHUNK):
                own = slice(start, start + CHUNK)
                wide = slice(block * HW + start, block * HW + start + CHUNK)
                parts = fold_ref[wide, :].astype(F32)
                fold_high, fold_low = high_low(parts[:, :CH] + noise_level * parts[:, CH:])
                up = ups[own, up_span]
                stacked[...] = jnp.concatenate([fold_high, fold_high, fold_low, up], axis=1)
                picture_part = dot(left, stacked[...], 1, 1).astype(BF)
                if block == 0:
                    now[:, own] = picture_part
                else:
                    now[TXT:, own] = picture_part
                    text_span = slice((block - 1) * HW + start, (block - 1) * HW + start + CHUNK)
                    adapter = dot(reduced_prompt[:, rank_span], up, 1, 1)
                    now[:TXT, own] = (text[:, text_span].astype(F32) + adapter).astype(BF)

        def head(index, carry):
            span = pl.ds(pl.multiple_of(index * HD, HD), HD)
            queries, keys, values = q_now[:, span], k_now[:, span], v_now[:, span]
            scores = dot(queries, keys, 1, 1) * SCALE
            largest = jnp.max(scores, axis=-1, keepdims=True)
            weights = jnp.exp(scores - largest)
            inverse = 1.0 / jnp.sum(weights, axis=-1, keepdims=True)
            weights = weights.astype(BF)
            attended = (dot(weights, values) * inverse).astype(BF)
            attended_now[:, span] = attended

            @save
            def _():
                q_ref[:, span] = queries
                k_ref[:, span] = keys
                v_ref[:, span] = values
                attended_ref[:, span] = attended
                weights_ref[index] = weights
                inverse_ref[index] = inverse

            return carry

        lax.fori_loop(0, HEADS, head, 0, unroll=3)
        return dot(velocity_out_ref[...], attended_now[...], 1, 1)

    latent = latents_ref[0]
    sample = latent - readout(latent, 1.0, 0, None, lambda f: f())
    sample_ref[...] = sample
    sample_again_ref[...] = sample
    noised = (1.0 - sigma) * sample + sigma * latents_ref[1]
    velocity = readout(noised, sigma, 1, group.astype(F32), pl.when(group == 1))
    velocity_ref[...] = velocity
    narrow_velocity_ref[...] = velocity.astype(BF)


def backward_kernel(
    place_ref,
    sigma_ref,
    sample_ref,
    latents_ref,
    own_ref,
    fake_ref,
    prompt_ref,
    velocity_out_ref,
    role_up_ref,
    q_ref,
    k_ref,
    v_ref,
    weights_ref,
    inverse_ref,
    attended_ref,
    reduced_ref,
    picture_ref,
    mine_ref,
    theirs_ref,
    grad_q,
    grad_k,
    grad_v,
    grads,
):
    flag = place_ref[0]
    sigma = sigma_ref[0, 0]
    sample = sample_ref[...]
    own = own_ref[...]
    noised = (1.0 - sigma) * sample + sigma * latents_ref[1]
    clean_real = noised - sigma * own
    clean_fake = noised - sigma * fake_ref[...].astype(F32)
    distance = jnp.sum(jnp.sum(jnp.abs(sample - clean_real), axis=1, keepdims=True), axis=0, keepdims=True)
    spread = distance * (1.0 / (IMG * CH)) + 1e-05
    cot_gen = -(clean_fake - clean_real) / spread
    cot_critic = 2.0 * (own - (latents_ref[1] - sample)) / (IMG * CH)
    cotangent = jnp.where(flag == 0, cot_gen, cot_critic).T.astype(BF)

    def head(index, carry):
        span = pl.ds(pl.multiple_of(index * HD, HD), HD)
        queries, keys, values = q_ref[:, span], k_ref[:, span], v_ref[:, span]
        weights = weights_ref[index]
        upstream = dot(cotangent, velocity_out_ref[:, span]) * inverse_ref[index]
        inner = jnp.sum(upstream * attended_ref[:, span].astype(F32), axis=-1, keepdims=True)
        upstream = upstream.astype(BF)
        grad_v[:, span] = dot(weights, upstream, 0, 0).astype(BF)
        grad_weights = dot(upstream, values, 1, 1)
        grad_scores = (weights.astype(F32) * (grad_weights - inner) * SCALE).astype(BF)
        grad_q[:, span] = dot(grad_scores, keys).astype(BF)
        grad_k[:, span] = dot(grad_scores, queries, 0, 0).astype(BF)
        return carry

    lax.fori_loop(0, HEADS, head, 0, unroll=12)
    spans = [slice(block * RANK, (block + 1) * RANK) for block in range(3)]
    reduced_q = dot(grad_q[...], role_up_ref[:, spans[0]]).astype(BF)
    reduced_k = dot(grad_k[...], role_up_ref[:, spans[1]]).astype(BF)
    reduced_v = dot(grad_v[...], role_up_ref[:, spans[2]]).astype(BF)
    reduced_kv = jnp.concatenate([reduced_k, reduced_v], axis=1)
    down_q = dot(reduced_q, picture_ref[...], 0, 0)
    down_kv = dot(reduced_kv[:TXT], prompt_ref[:TXT, :], 0, 0) + dot(reduced_kv[TXT:], picture_ref[...], 0, 0)
    up_q = dot(reduced_ref[TXT:, spans[0]], grad_q[...], 0, 0)
    up_k = dot(reduced_ref[:, spans[1]], grad_k[...], 0, 0)
    up_v = dot(reduced_ref[:, spans[2]], grad_v[...], 0, 0)
    grads[...] = jnp.concatenate([down_q, down_kv, up_q, up_k, up_v], axis=0).T
    core = place_ref[2]
    pairs, rows, _ = mine_ref.shape
    for pair in range(pairs):
        mine = pl.ds(pl.multiple_of((2 * pair + core) * rows, 8), rows)
        theirs = pl.ds(pl.multiple_of((2 * pair + 1 - core) * rows, 8), rows)
        mine_ref[pair] = grads[mine, :]
        theirs_ref[pair] = grads[theirs, :].astype(BF)


def add_kernel(mine_ref, received_ref, sums_ref):
    sums_ref[...] = (mine_ref[...] + received_ref[...].astype(F32)).astype(BF)


def run(kernel, name, megabytes, scalars, outputs, scratch, *operands, far=(), far_out=()):
    shapes = tuple(jax.ShapeDtypeStruct(*output) for output in outputs)
    return pl.pallas_call(
        kernel,
        out_shape=shapes,
        in_specs=[
            pl.BlockSpec(
                memory_space=pltpu.SMEM if k < scalars else pl.ANY if k in far else pltpu.VMEM
            )
            for k in range(len(operands))
        ],
        out_specs=tuple(
            pl.BlockSpec(memory_space=pl.ANY if k in far_out else pltpu.VMEM)
            for k in range(len(outputs))
        ),
        scratch_shapes=scratch,
        compiler_params=pltpu.CompilerParams(vmem_limit_bytes=megabytes * 2**20),
        name=name,
    )(*operands)


def per_device(
    latent_noise,
    fresh_noise,
    text_states,
    step_index,
    base_qkv,
    latent_in,
    modulation,
    velocity_out,
    gen_down,
    gen_up,
    critic_down,
    critic_up,
):
    devices = lax.axis_size("fsdp")
    group = lax.axis_index("group")
    index = lax.axis_index("fsdp")
    place = jnp.stack([group, lax.rem(index, 4), lax.rem(index, 2)]).astype(jnp.int32)
    sigma = ((step_index + 1).astype(F32) / NSTEPS).reshape(1, 1)
    shard = base_qkv.shape[0]

    def move(array, across, near):
        pairs = [
            (g * devices + device, (g ^ across) * devices + (device ^ near))
            for g in range(2)
            for device in range(devices)
        ]
        return lax.ppermute(array, ("group", "fsdp"), pairs)

    latents = jnp.stack([latent_noise[0].T, fresh_noise[0].T])
    text = text_states[0]
    gain = modulation.reshape(1, HW)
    out_map = velocity_out.T

    texts = [text, move(text, 0, 1), move(text, 1, 2), move(text, 1, 3)]
    (packed,) = run(
        pack_kernel,
        "pack",
        60,
        0,
        [((devices, shard, EIGHTH + SIDE + PART), BF)],
        [
            pltpu.VMEM((shard, 3 * HW), BF),
            pltpu.VMEM((2, shard, 3 * RANK), BF),
            pltpu.VMEM((2, 3, shard, RANK), BF),
            pltpu.VMEM((devices, shard, EIGHTH + SIDE + PART), BF),
            pltpu.SemaphoreType.DMA((5,)),
            pltpu.SemaphoreType.DMA((WRITES,)),
        ],
        base_qkv,
        gen_down,
        critic_down,
        gen_up.transpose(0, 2, 1),
        critic_up.transpose(0, 2, 1),
        far=(0, 1, 2, 3, 4),
        far_out=(0,),
    )
    packed = lax.all_to_all(packed, "fsdp", 0, 0).reshape(HW, EIGHTH + SIDE + PART)
    prompts, prompt = run(
        prompt_kernel, "prompts", 16, 0, [((4 * TXT, HW), BF), ((TXT, HW), BF)], [], *texts
    )
    packed, prompts = lax.optimization_barrier((packed, prompts))
    (share,) = run(
        fold_kernel,
        "fold",
        16,
        0,
        [((devices, SHARE, PART), BF)],
        [
            pltpu.VMEM((HW, PART), BF),
            pltpu.VMEM((devices // 8, SHARE, PART), BF),
            pltpu.SemaphoreType.DMA((1,)),
            pltpu.SemaphoreType.DMA((8,)),
        ],
        latent_in,
        gain,
        packed,
        far=(2,),
        far_out=(0,),
    )
    fold = lax.all_to_all(share, "fsdp", 0, 0).reshape(devices * SHARE, PART)
    packed_core = move(packed, 0, 1)
    prompts, packed_core = lax.optimization_barrier((prompts, packed_core))
    mine, theirs = run(
        mix_kernel,
        "mix",
        16,
        0,
        [((2 * TXT, EIGHTH), BF)] * 2,
        [pltpu.VMEM((HW, EIGHTH), BF), pltpu.SemaphoreType.DMA((1,))],
        prompts,
        packed,
        far=(1,),
    )
    received = move(theirs, 0, 1)
    own_pair, near_pair = run(
        pair_kernel, "pair", 16, 0, [((2, TXT, EIGHTH), BF)] * 2, [], mine, received
    )
    pieces = [own_pair, move(own_pair, 1, 0), move(near_pair, 0, 2), move(near_pair, 1, 2)]

    sample, sample_again, velocity, narrow_velocity, *saved, role_up = run(
        forward_kernel,
        "forward",
        32,
        2,
        [
            ((CH, IMG), F32),
            ((CH, IMG), F32),
            ((CH, IMG), F32),
            ((CH, IMG), BF),
            ((IMG, HW), BF),
            ((ROWS, HW), BF),
            ((ROWS, HW), BF),
            ((HEADS, IMG, ROWS), BF),
            ((HEADS, IMG, 1), F32),
            ((IMG, HW), BF),
            ((ROWS, 3 * RANK), BF),
            ((IMG, HW), BF),
            ((HW, 3 * RANK), BF),
        ],
        [
            pltpu.VMEM((CHUNK, 4 * CH), BF),
            pltpu.VMEM((IMG, HW), BF),
            pltpu.VMEM((ROWS, HW), BF),
            pltpu.VMEM((ROWS, HW), BF),
            pltpu.VMEM((IMG, HW), BF),
            pltpu.VMEM((TXT, 2 * HW), BF),
            pltpu.VMEM((2, HW, SIDE), BF),
            pltpu.SemaphoreType.DMA((2,)),
        ],
        place,
        sigma,
        latents,
        prompt,
        latent_in,
        gain,
        out_map,
        fold,
        *pieces,
        packed,
        packed_core,
        far=(12, 13),
    )
    fake_velocity = lax.ppermute(narrow_velocity, "group", [(1, 0)])
    half = (devices // 2, shard, SIDE)
    mine, theirs = run(
        backward_kernel,
        "backward",
        24,
        2,
        [(half, F32), (half, BF)],
        [
            pltpu.VMEM((IMG, HW), BF),
            pltpu.VMEM((ROWS, HW), BF),
            pltpu.VMEM((ROWS, HW), BF),
            pltpu.VMEM((HW, SIDE), F32),
        ],
        place,
        sigma,
        sample_again,
        latents,
        velocity,
        fake_velocity,
        prompt,
        out_map,
        role_up,
        *saved,
    )
    (sums,) = run(add_kernel, "add", 16, 0, [(half, BF)], [], mine, move(theirs, 0, 1))
    parities = [list(range(core, devices, 2)) for core in range(2)]
    shares = lax.all_to_all(sums, "fsdp", 0, 0, axis_index_groups=parities)
    share_down, share_up = run(
        sum_kernel,
        "total",
        16,
        0,
        [((shard, 3 * RANK), F32), ((3, shard, RANK), F32)],
        [],
        shares,
    )
    return (sample.T[None], share_down[None], share_up.transpose(0, 2, 1)[None])


def solution(mesh):
    in_specs = (
        P("fsdp", None, None),
        P("fsdp", None, None),
        P("fsdp", None, None),
        P("fsdp"),
        P("fsdp", None),
        P(),
        P(),
        P(),
        P("fsdp", None),
        P(None, None, "fsdp"),
        P("fsdp", None),
        P(None, None, "fsdp"),
    )
    out_specs = (P("fsdp", None, None), P("group", "fsdp", None), P("group", None, None, "fsdp"))
    return jax.shard_map(
        per_device, mesh=mesh, in_specs=in_specs, out_specs=out_specs, check_vma=False
    )
```

```python
import jax
import jax.numpy as jnp
from jax import lax
from jax.experimental import pallas as pl
from jax.experimental.pallas import tpu as pltpu
from jax.sharding import PartitionSpec as P

HEADS = 12
HD = 128
CH = 64
RANK = 64
NSTEPS = 1000
IMG = 256
TXT = 128
ROWS = TXT + IMG
HW = HEADS * HD
CHUNK = 512
EIGHTH = HW // 4
SIDE = 6 * RANK
SHARE = 72
PART = 128
WRITES = 4
MOVES = ((0, 0), (1, 0), (0, 2), (1, 2))
BF = jnp.bfloat16
F32 = jnp.float32
SCALE = HD ** (-0.5)


def dot(left, right, left_dim=1, right_dim=0):
    dims = (((left_dim,), (right_dim,)), ((), ()))
    return lax.dot_general(left, right, dims, preferred_element_type=F32)


def high_low(values):
    high = values.astype(BF)
    return high, (values - high.astype(F32)).astype(BF)


def unit_rows(values):
    values = values.astype(F32)
    return (values * lax.rsqrt(jnp.mean(values * values, axis=-1, keepdims=True) + 1e-06)).astype(BF)


def pack_kernel(
    base_ref,
    gen_down_ref,
    critic_down_ref,
    gen_up_ref,
    critic_up_ref,
    packed_ref,
    base,
    downs,
    ups,
    packed,
    read_sem,
    write_sem,
):
    reads = [
        pltpu.make_async_copy(base_ref, base, read_sem.at[0]),
        pltpu.make_async_copy(gen_down_ref, downs.at[0], read_sem.at[1]),
        pltpu.make_async_copy(critic_down_ref, downs.at[1], read_sem.at[2]),
        pltpu.make_async_copy(gen_up_ref, ups.at[0], read_sem.at[3]),
        pltpu.make_async_copy(critic_up_ref, ups.at[1], read_sem.at[4]),
    ]
    for read in reads:
        read.start()
    for read in reads:
        read.wait()
    group = lax.axis_index("group")

    def both(gen, critic):
        gen, critic = gen.astype(F32), critic.astype(F32)
        return jnp.concatenate([gen, jnp.where(group == 0, gen, critic)], axis=1).astype(BF)

    up_rows = [jnp.concatenate([ups[role, block] for block in range(3)], axis=1) for role in range(2)]
    sides = (both(downs[0], downs[1]), both(up_rows[0], up_rows[1]))
    eighths = []
    for near in range(4):
        start = pl.multiple_of(HW + group * HW + near * EIGHTH, EIGHTH)
        eighths.append(base[:, pl.ds(start, EIGHTH)])
    rows = base.shape[0]
    batch = packed.shape[0] // WRITES
    writes = []
    for step in range(WRITES):
        for device in range(step * batch, (step + 1) * batch):
            packed[device, :, :EIGHTH] = eighths[device % 4]
            packed[device, :, EIGHTH : EIGHTH + SIDE] = sides[device % 2]
            columns = base[:, device * SHARE : (device + 1) * SHARE]
            packed[device, :, EIGHTH + SIDE :] = jnp.concatenate(
                [columns, jnp.zeros((rows, PART - SHARE), BF)], axis=1
            )
        span = pl.ds(step * batch, batch)
        write = pltpu.make_async_copy(packed.at[span], packed_ref.at[span], write_sem.at[step])
        write.start()
        writes.append(write)
    for write in writes:
        write.wait()


def prompt_kernel(text_0_ref, text_1_ref, text_2_ref, text_3_ref, prompts_ref):
    for index, text_ref in enumerate((text_0_ref, text_1_ref, text_2_ref, text_3_ref)):
        prompts_ref[index * TXT : (index + 1) * TXT, :] = unit_rows(text_ref[...])


def sum_kernel(shares_ref, down_ref, up_ref):
    total = jnp.sum(shares_ref[...].astype(F32), axis=0)
    down_ref[...] = total[:, : 3 * RANK]
    for block in range(3):
        up_ref[block] = total[:, (3 + block) * RANK : (4 + block) * RANK]


def fold_kernel(
    latent_in_ref,
    modulation_ref,
    packed_ref,
    share_ref,
    side_ref,
    columns,
    sides,
    shares,
    read_sem,
    write_sem,
):
    read = pltpu.make_async_copy(packed_ref.at[:, EIGHTH + SIDE :], columns, read_sem.at[0])
    read.start()
    side = pltpu.make_async_copy(packed_ref.at[:, EIGHTH : EIGHTH + SIDE], sides, read_sem.at[1])
    side.start()
    scaled_in = (latent_in_ref[...].astype(F32) * modulation_ref[...]).astype(BF)
    folds = jnp.concatenate([latent_in_ref[...], scaled_in], axis=0)
    read.wait()
    side.wait()
    side = pltpu.make_async_copy(sides, side_ref, read_sem.at[1])
    side.start()
    share = dot(folds, columns[...]).T[:SHARE].astype(BF)
    batch = shares.shape[0]
    for device in range(batch):
        shares[device] = share
    writes = [
        pltpu.make_async_copy(shares, share_ref.at[pl.ds(step * batch, batch)], write_sem.at[step])
        for step in range(share_ref.shape[0] // batch)
    ]
    for write in writes:
        write.start()
    for write in writes:
        write.wait()
    side.wait()


def mix_kernel(prompts_ref, packed_ref, mine_ref, theirs_ref, columns, read_sem):
    read = pltpu.make_async_copy(packed_ref.at[:, :EIGHTH], columns, read_sem.at[0])
    read.start()
    read.wait()
    eighth = dot(prompts_ref[...], columns[...]).astype(BF)
    mine_ref[:TXT, :] = eighth[:TXT]
    theirs_ref[:TXT, :] = eighth[TXT : 2 * TXT]
    mine_ref[TXT:, :] = eighth[2 * TXT : 3 * TXT]
    theirs_ref[TXT:, :] = eighth[3 * TXT :]


def pair_kernel(mine_ref, received_ref, own_ref, near_ref):
    for place, part_ref in enumerate((mine_ref, received_ref)):
        own_ref[place] = part_ref[:TXT, :]
        near_ref[place] = part_ref[TXT:, :]


def forward_kernel(
    place_ref,
    sigma_ref,
    latent_ref,
    fresh_ref,
    prompt_ref,
    latent_in_ref,
    modulation_ref,
    velocity_out_ref,
    fold_ref,
    text_0_ref,
    text_1_ref,
    text_2_ref,
    text_3_ref,
    side_own_ref,
    side_core_ref,
    sample_ref,
    sample_again_ref,
    velocity_ref,
    narrow_velocity_ref,
    q_ref,
    k_ref,
    v_ref,
    weights_ref,
    inverse_ref,
    attended_ref,
    reduced_ref,
    picture_ref,
    role_up_ref,
    stacked,
    q_now,
    k_now,
    v_now,
    attended_now,
    text,
    downs,
    ups,
):
    group, near, core = place_ref[0], place_ref[1], place_ref[2]
    sigma = sigma_ref[0, 0]
    for (across, move), text_ref in zip(MOVES, (text_0_ref, text_1_ref, text_2_ref, text_3_ref)):
        for place in range(2):
            start = (group ^ across) * HW + (near ^ move ^ place) * EIGHTH
            text[:, pl.ds(pl.multiple_of(start, EIGHTH), EIGHTH)] = text_ref[place]

    @pl.when(core == 0)
    def _():
        downs[...] = side_own_ref[...]
        ups[...] = side_core_ref[...]

    @pl.when(core == 1)
    def _():
        downs[...] = side_core_ref[...]
        ups[...] = side_own_ref[...]

    role_up_ref[...] = ups[:, 3 * RANK :]

    def readout(latent, noise_level, role, switch, save):
        base = role * 3 * RANK
        narrow = latent.T.astype(BF)
        hidden = dot(narrow, latent_in_ref[...])
        inverse_rms = lax.rsqrt(jnp.mean(hidden * hidden, axis=-1, keepdims=True) + 1e-06)
        picture = (hidden * inverse_rms * (1.0 + noise_level * modulation_ref[...])).astype(BF)
        reduced_picture = dot(picture, downs[:, base : base + 3 * RANK]).astype(BF)
        reduced_prompt = dot(prompt_ref[:TXT, :], downs[:, base : base + 3 * RANK]).astype(BF)

        @save
        def _():
            picture_ref[...] = picture
            reduced_ref[TXT:, :] = reduced_picture
            reduced_ref[:TXT, :] = reduced_prompt

        if switch is not None:
            reduced_picture = reduced_picture * switch.astype(BF)
            reduced_prompt = reduced_prompt * switch.astype(BF)
        scaled_high, scaled_low = high_low(narrow.astype(F32) * inverse_rms)
        for block, now in enumerate((q_now, k_now, v_now)):
            rank_span = slice(block * RANK, (block + 1) * RANK)
            up_span = slice(base + block * RANK, base + (block + 1) * RANK)
            left = jnp.concatenate(
                [scaled_high, scaled_low, scaled_high, reduced_picture[:, rank_span]], axis=1
            )
            for start in range(0, HW, CHUNK):
                own = slice(start, start + CHUNK)
                wide = slice(block * HW + start, block * HW + start + CHUNK)
                parts = fold_ref[wide, :].astype(F32)
                fold_high, fold_low = high_low(parts[:, :CH] + noise_level * parts[:, CH:])
                up = ups[own, up_span]
                stacked[...] = jnp.concatenate([fold_high, fold_high, fold_low, up], axis=1)
                picture_part = dot(left, stacked[...], 1, 1).astype(BF)
                if block == 0:
                    now[:, own] = picture_part
                else:
                    now[TXT:, own] = picture_part
                    text_span = slice((block - 1) * HW + start, (block - 1) * HW + start + CHUNK)
                    adapter = dot(reduced_prompt[:, rank_span], up, 1, 1)
                    now[:TXT, own] = (text[:, text_span].astype(F32) + adapter).astype(BF)

        def head(index, carry):
            span = pl.ds(pl.multiple_of(index * HD, HD), HD)
            queries, keys, values = q_now[:, span], k_now[:, span], v_now[:, span]
            scores = dot(queries, keys, 1, 1) * SCALE
            largest = jnp.max(scores, axis=-1, keepdims=True)
            weights = jnp.exp(scores - largest)
            inverse = 1.0 / jnp.sum(weights, axis=-1, keepdims=True)
            weights = weights.astype(BF)
            attended = (dot(weights, values) * inverse).astype(BF)
            attended_now[:, span] = attended

            @save
            def _():
                q_ref[:, span] = queries
                k_ref[:, span] = keys
                v_ref[:, span] = values
                attended_ref[:, span] = attended
                weights_ref[index] = weights
                inverse_ref[index] = inverse

            return carry

        lax.fori_loop(0, HEADS, head, 0, unroll=2)
        return dot(velocity_out_ref[...], attended_now[...], 1, 1)

    latent = latent_ref[...]
    sample = latent - readout(latent, 1.0, 0, None, lambda f: f())
    sample_ref[...] = sample
    sample_again_ref[...] = sample
    noised = (1.0 - sigma) * sample + sigma * fresh_ref[...]
    velocity = readout(noised, sigma, 1, group.astype(F32), pl.when(group == 1))
    velocity_ref[...] = velocity
    narrow_velocity_ref[...] = velocity.astype(BF)


def backward_kernel(
    place_ref,
    sigma_ref,
    sample_ref,
    fresh_ref,
    own_ref,
    fake_ref,
    prompt_ref,
    velocity_out_ref,
    role_up_ref,
    q_ref,
    k_ref,
    v_ref,
    weights_ref,
    inverse_ref,
    attended_ref,
    reduced_ref,
    picture_ref,
    mine_ref,
    theirs_ref,
    grad_q,
    grad_k,
    grad_v,
    grads,
):
    flag = place_ref[0]
    sigma = sigma_ref[0, 0]
    sample = sample_ref[...]
    own = own_ref[...]
    noised = (1.0 - sigma) * sample + sigma * fresh_ref[...]
    clean_real = noised - sigma * own
    clean_fake = noised - sigma * fake_ref[...].astype(F32)
    distance = jnp.sum(jnp.sum(jnp.abs(sample - clean_real), axis=1, keepdims=True), axis=0, keepdims=True)
    spread = distance * (1.0 / (IMG * CH)) + 1e-05
    cot_gen = -(clean_fake - clean_real) / spread
    cot_critic = 2.0 * (own - (fresh_ref[...] - sample)) / (IMG * CH)
    cotangent = jnp.where(flag == 0, cot_gen, cot_critic).T.astype(BF)

    def head(index, carry):
        span = pl.ds(pl.multiple_of(index * HD, HD), HD)
        queries, keys, values = q_ref[:, span], k_ref[:, span], v_ref[:, span]
        weights = weights_ref[index]
        upstream = dot(cotangent, velocity_out_ref[:, span]) * inverse_ref[index]
        inner = jnp.sum(upstream * attended_ref[:, span].astype(F32), axis=-1, keepdims=True)
        upstream = upstream.astype(BF)
        grad_v[:, span] = dot(weights, upstream, 0, 0).astype(BF)
        grad_weights = dot(upstream, values, 1, 1)
        grad_scores = (weights.astype(F32) * (grad_weights - inner) * SCALE).astype(BF)
        grad_q[:, span] = dot(grad_scores, keys).astype(BF)
        grad_k[:, span] = dot(grad_scores, queries, 0, 0).astype(BF)
        return carry

    lax.fori_loop(0, HEADS, head, 0, unroll=12)
    spans = [slice(block * RANK, (block + 1) * RANK) for block in range(3)]
    reduced_q = dot(grad_q[...], role_up_ref[:, spans[0]]).astype(BF)
    reduced_k = dot(grad_k[...], role_up_ref[:, spans[1]]).astype(BF)
    reduced_v = dot(grad_v[...], role_up_ref[:, spans[2]]).astype(BF)
    reduced_kv = jnp.concatenate([reduced_k, reduced_v], axis=1)
    down_q = dot(reduced_q, picture_ref[...], 0, 0)
    down_kv = dot(reduced_kv[:TXT], prompt_ref[:TXT, :], 0, 0) + dot(reduced_kv[TXT:], picture_ref[...], 0, 0)
    up_q = dot(reduced_ref[TXT:, spans[0]], grad_q[...], 0, 0)
    up_k = dot(reduced_ref[:, spans[1]], grad_k[...], 0, 0)
    up_v = dot(reduced_ref[:, spans[2]], grad_v[...], 0, 0)
    grads[...] = jnp.concatenate([down_q, down_kv, up_q, up_k, up_v], axis=0).T
    core = place_ref[2]
    pairs, rows, _ = mine_ref.shape
    for pair in range(pairs):
        mine = pl.ds(pl.multiple_of((2 * pair + core) * rows, 8), rows)
        theirs = pl.ds(pl.multiple_of((2 * pair + 1 - core) * rows, 8), rows)
        mine_ref[pair] = grads[mine, :]
        theirs_ref[pair] = grads[theirs, :].astype(BF)


def add_kernel(mine_ref, received_ref, sums_ref):
    sums_ref[...] = (mine_ref[...] + received_ref[...].astype(F32)).astype(BF)


def run(kernel, name, megabytes, scalars, outputs, scratch, *operands, far=(), out_space=pltpu.VMEM):
    shapes = tuple(jax.ShapeDtypeStruct(*output) for output in outputs)
    return pl.pallas_call(
        kernel,
        out_shape=shapes,
        in_specs=[
            pl.BlockSpec(
                memory_space=pltpu.SMEM if k < scalars else pl.ANY if k in far else pltpu.VMEM
            )
            for k in range(len(operands))
        ],
        out_specs=tuple([pl.BlockSpec(memory_space=out_space)] * len(outputs)),
        scratch_shapes=scratch,
        compiler_params=pltpu.CompilerParams(vmem_limit_bytes=megabytes * 2**20),
        name=name,
    )(*operands)


def per_device(
    latent_noise,
    fresh_noise,
    text_states,
    step_index,
    base_qkv,
    latent_in,
    modulation,
    velocity_out,
    gen_down,
    gen_up,
    critic_down,
    critic_up,
):
    devices = lax.axis_size("fsdp")
    group = lax.axis_index("group")
    index = lax.axis_index("fsdp")
    place = jnp.stack([group, lax.rem(index, 4), lax.rem(index, 2)]).astype(jnp.int32)
    sigma = ((step_index + 1).astype(F32) / NSTEPS).reshape(1, 1)
    shard = base_qkv.shape[0]

    def move(array, across, near):
        pairs = [
            (g * devices + device, (g ^ across) * devices + (device ^ near))
            for g in range(2)
            for device in range(devices)
        ]
        return lax.ppermute(array, ("group", "fsdp"), pairs)

    latent = latent_noise[0].T
    fresh = fresh_noise[0].T
    text = text_states[0]
    gain = modulation.reshape(1, HW)
    out_map = velocity_out.T

    texts = [text, move(text, 0, 1), move(text, 1, 2), move(text, 1, 3)]
    (packed,) = run(
        pack_kernel,
        "pack",
        60,
        0,
        [((devices, shard, EIGHTH + SIDE + PART), BF)],
        [
            pltpu.VMEM((shard, 3 * HW), BF),
            pltpu.VMEM((2, shard, 3 * RANK), BF),
            pltpu.VMEM((2, 3, shard, RANK), BF),
            pltpu.VMEM((devices, shard, EIGHTH + SIDE + PART), BF),
            pltpu.SemaphoreType.DMA((5,)),
            pltpu.SemaphoreType.DMA((WRITES,)),
        ],
        base_qkv,
        gen_down,
        critic_down,
        gen_up.transpose(0, 2, 1),
        critic_up.transpose(0, 2, 1),
        far=(0, 1, 2, 3, 4),
        out_space=pl.ANY,
    )
    packed = lax.all_to_all(packed, "fsdp", 0, 0).reshape(HW, EIGHTH + SIDE + PART)
    (prompts,) = run(prompt_kernel, "prompts", 16, 0, [((4 * TXT, HW), BF)], [], *texts)
    packed, prompts = lax.optimization_barrier((packed, prompts))
    share, side_own = run(
        fold_kernel,
        "fold",
        16,
        0,
        [((devices, SHARE, PART), BF), ((HW, SIDE), BF)],
        [
            pltpu.VMEM((HW, PART), BF),
            pltpu.VMEM((HW, SIDE), BF),
            pltpu.VMEM((devices // 8, SHARE, PART), BF),
            pltpu.SemaphoreType.DMA((2,)),
            pltpu.SemaphoreType.DMA((8,)),
        ],
        latent_in,
        gain,
        packed,
        far=(2,),
        out_space=pl.ANY,
    )
    fold = lax.all_to_all(share, "fsdp", 0, 0).reshape(devices * SHARE, PART)
    side_core = move(side_own, 0, 1)
    prompts, side_core = lax.optimization_barrier((prompts, side_core))
    mine, theirs = run(
        mix_kernel,
        "mix",
        16,
        0,
        [((2 * TXT, EIGHTH), BF)] * 2,
        [pltpu.VMEM((HW, EIGHTH), BF), pltpu.SemaphoreType.DMA((1,))],
        prompts,
        packed,
        far=(1,),
    )
    received = move(theirs, 0, 1)
    own_pair, near_pair = run(
        pair_kernel, "pair", 16, 0, [((2, TXT, EIGHTH), BF)] * 2, [], mine, received
    )
    pieces = [own_pair, move(own_pair, 1, 0), move(near_pair, 0, 2), move(near_pair, 1, 2)]

    sample, sample_again, velocity, narrow_velocity, *saved, role_up = run(
        forward_kernel,
        "forward",
        32,
        2,
        [
            ((CH, IMG), F32),
            ((CH, IMG), F32),
            ((CH, IMG), F32),
            ((CH, IMG), BF),
            ((IMG, HW), BF),
            ((ROWS, HW), BF),
            ((ROWS, HW), BF),
            ((HEADS, IMG, ROWS), BF),
            ((HEADS, IMG, 1), F32),
            ((IMG, HW), BF),
            ((ROWS, 3 * RANK), BF),
            ((IMG, HW), BF),
            ((HW, 3 * RANK), BF),
        ],
        [
            pltpu.VMEM((CHUNK, 4 * CH), BF),
            pltpu.VMEM((IMG, HW), BF),
            pltpu.VMEM((ROWS, HW), BF),
            pltpu.VMEM((ROWS, HW), BF),
            pltpu.VMEM((IMG, HW), BF),
            pltpu.VMEM((TXT, 2 * HW), BF),
            pltpu.VMEM((HW, SIDE), BF),
            pltpu.VMEM((HW, SIDE), BF),
        ],
        place,
        sigma,
        latent,
        fresh,
        prompts,
        latent_in,
        gain,
        out_map,
        fold,
        *pieces,
        side_own,
        side_core,
    )
    fake_velocity = lax.ppermute(narrow_velocity, "group", [(1, 0)])
    half = (devices // 2, shard, SIDE)
    mine, theirs = run(
        backward_kernel,
        "backward",
        24,
        2,
        [(half, F32), (half, BF)],
        [
            pltpu.VMEM((IMG, HW), BF),
            pltpu.VMEM((ROWS, HW), BF),
            pltpu.VMEM((ROWS, HW), BF),
            pltpu.VMEM((HW, SIDE), F32),
        ],
        place,
        sigma,
        sample_again,
        fresh,
        velocity,
        fake_velocity,
        prompts,
        out_map,
        role_up,
        *saved,
    )
    (sums,) = run(add_kernel, "add", 16, 0, [(half, BF)], [], mine, move(theirs, 0, 1))
    parities = [list(range(core, devices, 2)) for core in range(2)]
    shares = lax.all_to_all(sums, "fsdp", 0, 0, axis_index_groups=parities)
    share_down, share_up = run(
        sum_kernel,
        "total",
        16,
        0,
        [((shard, 3 * RANK), F32), ((3, shard, RANK), F32)],
        [],
        shares,
    )
    return (sample.T[None], share_down[None], share_up.transpose(0, 2, 1)[None])


def solution(mesh):
    in_specs = (
        P("fsdp", None, None),
        P("fsdp", None, None),
        P("fsdp", None, None),
        P("fsdp"),
        P("fsdp", None),
        P(),
        P(),
        P(),
        P("fsdp", None),
        P(None, None, "fsdp"),
        P("fsdp", None),
        P(None, None, "fsdp"),
    )
    out_specs = (P("fsdp", None, None), P("group", "fsdp", None), P("group", None, None, "fsdp"))
    return jax.shard_map(
        per_device, mesh=mesh, in_specs=in_specs, out_specs=out_specs, check_vma=False
    )
```

```python
import jax
import jax.numpy as jnp
from jax import lax
from jax.experimental import pallas as pl
from jax.experimental.pallas import tpu as pltpu
from jax.sharding import PartitionSpec as P

HEADS = 12
HD = 128
CH = 64
RANK = 64
NSTEPS = 1000
IMG = 256
TXT = 128
ROWS = TXT + IMG
HW = HEADS * HD
CHUNK = 512
EIGHTH = HW // 4
SIDE = 6 * RANK
SHARE = 72
PART = 128
WRITES = 4
MOVES = ((0, 0), (1, 0), (0, 2), (1, 2))
BF = jnp.bfloat16
F32 = jnp.float32
SCALE = HD ** (-0.5)


def dot(left, right, left_dim=1, right_dim=0):
    dims = (((left_dim,), (right_dim,)), ((), ()))
    return lax.dot_general(left, right, dims, preferred_element_type=F32)


def high_low(values):
    high = values.astype(BF)
    return high, (values - high.astype(F32)).astype(BF)


def unit_rows(values):
    values = values.astype(F32)
    return (values * lax.rsqrt(jnp.mean(values * values, axis=-1, keepdims=True) + 1e-06)).astype(BF)


def pack_kernel(
    base_ref,
    gen_down_ref,
    critic_down_ref,
    gen_up_ref,
    critic_up_ref,
    packed_ref,
    base,
    downs,
    ups,
    packed,
    read_sem,
    write_sem,
):
    reads = [
        pltpu.make_async_copy(base_ref, base, read_sem.at[0]),
        pltpu.make_async_copy(gen_down_ref, downs.at[0], read_sem.at[1]),
        pltpu.make_async_copy(critic_down_ref, downs.at[1], read_sem.at[2]),
        pltpu.make_async_copy(gen_up_ref, ups.at[0], read_sem.at[3]),
        pltpu.make_async_copy(critic_up_ref, ups.at[1], read_sem.at[4]),
    ]
    for read in reads:
        read.start()
    for read in reads:
        read.wait()
    group = lax.axis_index("group")

    def both(gen, critic):
        gen, critic = gen.astype(F32), critic.astype(F32)
        return jnp.concatenate([gen, jnp.where(group == 0, gen, critic)], axis=1).astype(BF)

    up_rows = [jnp.concatenate([ups[role, block] for block in range(3)], axis=1) for role in range(2)]
    sides = (both(downs[0], downs[1]), both(up_rows[0], up_rows[1]))
    eighths = []
    for near in range(4):
        start = pl.multiple_of(HW + group * HW + near * EIGHTH, EIGHTH)
        eighths.append(base[:, pl.ds(start, EIGHTH)])
    rows = base.shape[0]
    batch = packed.shape[0] // WRITES
    writes = []
    for step in range(WRITES):
        for device in range(step * batch, (step + 1) * batch):
            packed[device, :, :EIGHTH] = eighths[device % 4]
            packed[device, :, EIGHTH : EIGHTH + SIDE] = sides[device % 2]
            columns = base[:, device * SHARE : (device + 1) * SHARE]
            packed[device, :, EIGHTH + SIDE :] = jnp.concatenate(
                [columns, jnp.zeros((rows, PART - SHARE), BF)], axis=1
            )
        span = pl.ds(step * batch, batch)
        write = pltpu.make_async_copy(packed.at[span], packed_ref.at[span], write_sem.at[step])
        write.start()
        writes.append(write)
    for write in writes:
        write.wait()


def prompt_kernel(text_0_ref, text_1_ref, text_2_ref, text_3_ref, prompts_ref):
    for index, text_ref in enumerate((text_0_ref, text_1_ref, text_2_ref, text_3_ref)):
        prompts_ref[index * TXT : (index + 1) * TXT, :] = unit_rows(text_ref[...])


def sum_kernel(shares_ref, down_ref, up_ref):
    total = jnp.sum(shares_ref[...].astype(F32), axis=0)
    down_ref[...] = total[:, : 3 * RANK]
    for block in range(3):
        up_ref[block] = total[:, (3 + block) * RANK : (4 + block) * RANK]


def fold_kernel(
    latent_in_ref,
    modulation_ref,
    packed_ref,
    share_ref,
    side_ref,
    columns,
    sides,
    shares,
    read_sem,
    write_sem,
):
    read = pltpu.make_async_copy(packed_ref.at[:, EIGHTH + SIDE :], columns, read_sem.at[0])
    read.start()
    side = pltpu.make_async_copy(packed_ref.at[:, EIGHTH : EIGHTH + SIDE], sides, read_sem.at[1])
    side.start()
    scaled_in = (latent_in_ref[...].astype(F32) * modulation_ref[...]).astype(BF)
    folds = jnp.concatenate([latent_in_ref[...], scaled_in], axis=0)
    read.wait()
    side.wait()
    side = pltpu.make_async_copy(sides, side_ref, read_sem.at[1])
    side.start()
    share = dot(folds, columns[...]).T[:SHARE].astype(BF)
    batch = shares.shape[0]
    for device in range(batch):
        shares[device] = share
    writes = [
        pltpu.make_async_copy(shares, share_ref.at[pl.ds(step * batch, batch)], write_sem.at[step])
        for step in range(share_ref.shape[0] // batch)
    ]
    for write in writes:
        write.start()
    for write in writes:
        write.wait()
    side.wait()


def mix_kernel(prompts_ref, packed_ref, mine_ref, theirs_ref, columns, read_sem):
    read = pltpu.make_async_copy(packed_ref.at[:, :EIGHTH], columns, read_sem.at[0])
    read.start()
    read.wait()
    eighth = dot(prompts_ref[...], columns[...]).astype(BF)
    mine_ref[:TXT, :] = eighth[:TXT]
    theirs_ref[:TXT, :] = eighth[TXT : 2 * TXT]
    mine_ref[TXT:, :] = eighth[2 * TXT : 3 * TXT]
    theirs_ref[TXT:, :] = eighth[3 * TXT :]


def pair_kernel(mine_ref, received_ref, own_ref, near_ref):
    for place, part_ref in enumerate((mine_ref, received_ref)):
        own_ref[place] = part_ref[:TXT, :]
        near_ref[place] = part_ref[TXT:, :]


def forward_kernel(
    place_ref,
    sigma_ref,
    latent_ref,
    fresh_ref,
    prompt_ref,
    latent_in_ref,
    modulation_ref,
    velocity_out_ref,
    fold_ref,
    text_0_ref,
    text_1_ref,
    text_2_ref,
    text_3_ref,
    side_own_ref,
    side_core_ref,
    sample_ref,
    sample_again_ref,
    velocity_ref,
    narrow_velocity_ref,
    q_ref,
    k_ref,
    v_ref,
    weights_ref,
    inverse_ref,
    attended_ref,
    reduced_ref,
    picture_ref,
    role_up_ref,
    stacked,
    q_now,
    k_now,
    v_now,
    attended_now,
    text,
    downs,
    ups,
):
    group, near, core = place_ref[0], place_ref[1], place_ref[2]
    sigma = sigma_ref[0, 0]
    for (across, move), text_ref in zip(MOVES, (text_0_ref, text_1_ref, text_2_ref, text_3_ref)):
        for place in range(2):
            start = (group ^ across) * HW + (near ^ move ^ place) * EIGHTH
            text[:, pl.ds(pl.multiple_of(start, EIGHTH), EIGHTH)] = text_ref[place]

    @pl.when(core == 0)
    def _():
        downs[...] = side_own_ref[...]
        ups[...] = side_core_ref[...]

    @pl.when(core == 1)
    def _():
        downs[...] = side_core_ref[...]
        ups[...] = side_own_ref[...]

    role_up_ref[...] = ups[:, 3 * RANK :]

    def readout(latent, noise_level, role, switch, save):
        base = role * 3 * RANK
        narrow = latent.T.astype(BF)
        hidden = dot(narrow, latent_in_ref[...])
        inverse_rms = lax.rsqrt(jnp.mean(hidden * hidden, axis=-1, keepdims=True) + 1e-06)
        picture = (hidden * inverse_rms * (1.0 + noise_level * modulation_ref[...])).astype(BF)
        reduced_picture = dot(picture, downs[:, base : base + 3 * RANK]).astype(BF)
        reduced_prompt = dot(prompt_ref[:TXT, :], downs[:, base : base + 3 * RANK]).astype(BF)

        @save
        def _():
            picture_ref[...] = picture
            reduced_ref[TXT:, :] = reduced_picture
            reduced_ref[:TXT, :] = reduced_prompt

        if switch is not None:
            reduced_picture = reduced_picture * switch.astype(BF)
            reduced_prompt = reduced_prompt * switch.astype(BF)
        scaled_high, scaled_low = high_low(narrow.astype(F32) * inverse_rms)
        for block, now in enumerate((q_now, k_now, v_now)):
            rank_span = slice(block * RANK, (block + 1) * RANK)
            up_span = slice(base + block * RANK, base + (block + 1) * RANK)
            left = jnp.concatenate(
                [scaled_high, scaled_low, scaled_high, reduced_picture[:, rank_span]], axis=1
            )
            for start in range(0, HW, CHUNK):
                own = slice(start, start + CHUNK)
                wide = slice(block * HW + start, block * HW + start + CHUNK)
                parts = fold_ref[wide, :].astype(F32)
                fold_high, fold_low = high_low(parts[:, :CH] + noise_level * parts[:, CH:])
                up = ups[own, up_span]
                stacked[...] = jnp.concatenate([fold_high, fold_high, fold_low, up], axis=1)
                picture_part = dot(left, stacked[...], 1, 1).astype(BF)
                if block == 0:
                    now[:, own] = picture_part
                else:
                    now[TXT:, own] = picture_part
                    text_span = slice((block - 1) * HW + start, (block - 1) * HW + start + CHUNK)
                    adapter = dot(reduced_prompt[:, rank_span], up, 1, 1)
                    now[:TXT, own] = (text[:, text_span].astype(F32) + adapter).astype(BF)

        def head(index, carry):
            span = pl.ds(pl.multiple_of(index * HD, HD), HD)
            queries, keys, values = q_now[:, span], k_now[:, span], v_now[:, span]
            scores = dot(queries, keys, 1, 1) * SCALE
            largest = jnp.max(scores, axis=-1, keepdims=True)
            weights = jnp.exp(scores - largest)
            inverse = 1.0 / jnp.sum(weights, axis=-1, keepdims=True)
            weights = weights.astype(BF)
            attended = (dot(weights, values) * inverse).astype(BF)
            attended_now[:, span] = attended

            @save
            def _():
                q_ref[:, span] = queries
                k_ref[:, span] = keys
                v_ref[:, span] = values
                attended_ref[:, span] = attended
                weights_ref[index] = weights
                inverse_ref[index] = inverse

            return carry

        lax.fori_loop(0, HEADS, head, 0, unroll=2)
        return dot(velocity_out_ref[...], attended_now[...], 1, 1)

    latent = latent_ref[...]
    sample = latent - readout(latent, 1.0, 0, None, lambda f: f())
    sample_ref[...] = sample
    sample_again_ref[...] = sample
    noised = (1.0 - sigma) * sample + sigma * fresh_ref[...]
    velocity = readout(noised, sigma, 1, group.astype(F32), pl.when(group == 1))
    velocity_ref[...] = velocity
    narrow_velocity_ref[...] = velocity.astype(BF)


def backward_kernel(
    place_ref,
    sigma_ref,
    sample_ref,
    fresh_ref,
    own_ref,
    fake_ref,
    prompt_ref,
    velocity_out_ref,
    role_up_ref,
    q_ref,
    k_ref,
    v_ref,
    weights_ref,
    inverse_ref,
    attended_ref,
    reduced_ref,
    picture_ref,
    mine_ref,
    theirs_ref,
    grad_q,
    grad_k,
    grad_v,
    grads,
):
    flag = place_ref[0]
    sigma = sigma_ref[0, 0]
    sample = sample_ref[...]
    own = own_ref[...]
    noised = (1.0 - sigma) * sample + sigma * fresh_ref[...]
    clean_real = noised - sigma * own
    clean_fake = noised - sigma * fake_ref[...].astype(F32)
    distance = jnp.sum(jnp.sum(jnp.abs(sample - clean_real), axis=1, keepdims=True), axis=0, keepdims=True)
    spread = distance * (1.0 / (IMG * CH)) + 1e-05
    cot_gen = -(clean_fake - clean_real) / spread
    cot_critic = 2.0 * (own - (fresh_ref[...] - sample)) / (IMG * CH)
    cotangent = jnp.where(flag == 0, cot_gen, cot_critic).T.astype(BF)

    def head(index, carry):
        span = pl.ds(pl.multiple_of(index * HD, HD), HD)
        queries, keys, values = q_ref[:, span], k_ref[:, span], v_ref[:, span]
        weights = weights_ref[index]
        upstream = dot(cotangent, velocity_out_ref[:, span]) * inverse_ref[index]
        inner = jnp.sum(upstream * attended_ref[:, span].astype(F32), axis=-1, keepdims=True)
        upstream = upstream.astype(BF)
        grad_v[:, span] = dot(weights, upstream, 0, 0).astype(BF)
        grad_weights = dot(upstream, values, 1, 1)
        grad_scores = (weights.astype(F32) * (grad_weights - inner) * SCALE).astype(BF)
        grad_q[:, span] = dot(grad_scores, keys).astype(BF)
        grad_k[:, span] = dot(grad_scores, queries, 0, 0).astype(BF)
        return carry

    lax.fori_loop(0, HEADS, head, 0, unroll=12)
    spans = [slice(block * RANK, (block + 1) * RANK) for block in range(3)]
    reduced_q = dot(grad_q[...], role_up_ref[:, spans[0]]).astype(BF)
    reduced_k = dot(grad_k[...], role_up_ref[:, spans[1]]).astype(BF)
    reduced_v = dot(grad_v[...], role_up_ref[:, spans[2]]).astype(BF)
    reduced_kv = jnp.concatenate([reduced_k, reduced_v], axis=1)
    down_q = dot(reduced_q, picture_ref[...], 0, 0)
    down_kv = dot(reduced_kv[:TXT], prompt_ref[:TXT, :], 0, 0) + dot(reduced_kv[TXT:], picture_ref[...], 0, 0)
    up_q = dot(reduced_ref[TXT:, spans[0]], grad_q[...], 0, 0)
    up_k = dot(reduced_ref[:, spans[1]], grad_k[...], 0, 0)
    up_v = dot(reduced_ref[:, spans[2]], grad_v[...], 0, 0)
    grads[...] = jnp.concatenate([down_q, down_kv, up_q, up_k, up_v], axis=0).T
    core = place_ref[2]
    pairs, rows, _ = mine_ref.shape
    for pair in range(pairs):
        mine = pl.ds(pl.multiple_of((2 * pair + core) * rows, 8), rows)
        theirs = pl.ds(pl.multiple_of((2 * pair + 1 - core) * rows, 8), rows)
        mine_ref[pair] = grads[mine, :]
        theirs_ref[pair] = grads[theirs, :].astype(BF)


def add_kernel(mine_ref, received_ref, sums_ref):
    sums_ref[...] = (mine_ref[...] + received_ref[...].astype(F32)).astype(BF)


def run(kernel, name, megabytes, scalars, outputs, scratch, *operands, far=(), out_space=pltpu.VMEM):
    shapes = tuple(jax.ShapeDtypeStruct(*output) for output in outputs)
    return pl.pallas_call(
        kernel,
        out_shape=shapes,
        in_specs=[
            pl.BlockSpec(
                memory_space=pltpu.SMEM if k < scalars else pl.ANY if k in far else pltpu.VMEM
            )
            for k in range(len(operands))
        ],
        out_specs=tuple([pl.BlockSpec(memory_space=out_space)] * len(outputs)),
        scratch_shapes=scratch,
        compiler_params=pltpu.CompilerParams(vmem_limit_bytes=megabytes * 2**20),
        name=name,
    )(*operands)


def per_device(
    latent_noise,
    fresh_noise,
    text_states,
    step_index,
    base_qkv,
    latent_in,
    modulation,
    velocity_out,
    gen_down,
    gen_up,
    critic_down,
    critic_up,
):
    devices = lax.axis_size("fsdp")
    group = lax.axis_index("group")
    index = lax.axis_index("fsdp")
    place = jnp.stack([group, lax.rem(index, 4), lax.rem(index, 2)]).astype(jnp.int32)
    sigma = ((step_index + 1).astype(F32) / NSTEPS).reshape(1, 1)
    shard = base_qkv.shape[0]

    def move(array, across, near):
        pairs = [
            (g * devices + device, (g ^ across) * devices + (device ^ near))
            for g in range(2)
            for device in range(devices)
        ]
        return lax.ppermute(array, ("group", "fsdp"), pairs)

    latent = latent_noise[0].T
    fresh = fresh_noise[0].T
    text = text_states[0]
    gain = modulation.reshape(1, HW)
    out_map = velocity_out.T

    texts = [text, move(text, 0, 1), move(text, 1, 2), move(text, 1, 3)]
    (packed,) = run(
        pack_kernel,
        "pack",
        60,
        0,
        [((devices, shard, EIGHTH + SIDE + PART), BF)],
        [
            pltpu.VMEM((shard, 3 * HW), BF),
            pltpu.VMEM((2, shard, 3 * RANK), BF),
            pltpu.VMEM((2, 3, shard, RANK), BF),
            pltpu.VMEM((devices, shard, EIGHTH + SIDE + PART), BF),
            pltpu.SemaphoreType.DMA((5,)),
            pltpu.SemaphoreType.DMA((WRITES,)),
        ],
        base_qkv,
        gen_down,
        critic_down,
        gen_up.transpose(0, 2, 1),
        critic_up.transpose(0, 2, 1),
        far=(0, 1, 2, 3, 4),
        out_space=pl.ANY,
    )
    packed = lax.all_to_all(packed, "fsdp", 0, 0).reshape(HW, EIGHTH + SIDE + PART)
    (prompts,) = run(prompt_kernel, "prompts", 16, 0, [((4 * TXT, HW), BF)], [], *texts)
    packed, prompts = lax.optimization_barrier((packed, prompts))
    share, side_own = run(
        fold_kernel,
        "fold",
        60,
        0,
        [((devices, SHARE, PART), BF), ((HW, SIDE), BF)],
        [
            pltpu.VMEM((HW, PART), BF),
            pltpu.VMEM((HW, SIDE), BF),
            pltpu.VMEM((devices // 8, SHARE, PART), BF),
            pltpu.SemaphoreType.DMA((2,)),
            pltpu.SemaphoreType.DMA((8,)),
        ],
        latent_in,
        gain,
        packed,
        far=(2,),
        out_space=pl.ANY,
    )
    fold = lax.all_to_all(share, "fsdp", 0, 0).reshape(devices * SHARE, PART)
    side_core = move(side_own, 0, 1)
    prompts, side_core = lax.optimization_barrier((prompts, side_core))
    mine, theirs = run(
        mix_kernel,
        "mix",
        16,
        0,
        [((2 * TXT, EIGHTH), BF)] * 2,
        [pltpu.VMEM((HW, EIGHTH), BF), pltpu.SemaphoreType.DMA((1,))],
        prompts,
        packed,
        far=(1,),
    )
    received = move(theirs, 0, 1)
    own_pair, near_pair = run(
        pair_kernel, "pair", 16, 0, [((2, TXT, EIGHTH), BF)] * 2, [], mine, received
    )
    pieces = [own_pair, move(own_pair, 1, 0), move(near_pair, 0, 2), move(near_pair, 1, 2)]

    sample, sample_again, velocity, narrow_velocity, *saved, role_up = run(
        forward_kernel,
        "forward",
        32,
        2,
        [
            ((CH, IMG), F32),
            ((CH, IMG), F32),
            ((CH, IMG), F32),
            ((CH, IMG), BF),
            ((IMG, HW), BF),
            ((ROWS, HW), BF),
            ((ROWS, HW), BF),
            ((HEADS, IMG, ROWS), BF),
            ((HEADS, IMG, 1), F32),
            ((IMG, HW), BF),
            ((ROWS, 3 * RANK), BF),
            ((IMG, HW), BF),
            ((HW, 3 * RANK), BF),
        ],
        [
            pltpu.VMEM((CHUNK, 4 * CH), BF),
            pltpu.VMEM((IMG, HW), BF),
            pltpu.VMEM((ROWS, HW), BF),
            pltpu.VMEM((ROWS, HW), BF),
            pltpu.VMEM((IMG, HW), BF),
            pltpu.VMEM((TXT, 2 * HW), BF),
            pltpu.VMEM((HW, SIDE), BF),
            pltpu.VMEM((HW, SIDE), BF),
        ],
        place,
        sigma,
        latent,
        fresh,
        prompts,
        latent_in,
        gain,
        out_map,
        fold,
        *pieces,
        side_own,
        side_core,
    )
    fake_velocity = lax.ppermute(narrow_velocity, "group", [(1, 0)])
    half = (devices // 2, shard, SIDE)
    mine, theirs = run(
        backward_kernel,
        "backward",
        24,
        2,
        [(half, F32), (half, BF)],
        [
            pltpu.VMEM((IMG, HW), BF),
            pltpu.VMEM((ROWS, HW), BF),
            pltpu.VMEM((ROWS, HW), BF),
            pltpu.VMEM((HW, SIDE), F32),
        ],
        place,
        sigma,
        sample_again,
        fresh,
        velocity,
        fake_velocity,
        prompts,
        out_map,
        role_up,
        *saved,
    )
    (sums,) = run(add_kernel, "add", 16, 0, [(half, BF)], [], mine, move(theirs, 0, 1))
    parities = [list(range(core, devices, 2)) for core in range(2)]
    shares = lax.all_to_all(sums, "fsdp", 0, 0, axis_index_groups=parities)
    share_down, share_up = run(
        sum_kernel,
        "total",
        16,
        0,
        [((shard, 3 * RANK), F32), ((3, shard, RANK), F32)],
        [],
        shares,
    )
    return (sample.T[None], share_down[None], share_up.transpose(0, 2, 1)[None])


def solution(mesh):
    in_specs = (
        P("fsdp", None, None),
        P("fsdp", None, None),
        P("fsdp", None, None),
        P("fsdp"),
        P("fsdp", None),
        P(),
        P(),
        P(),
        P("fsdp", None),
        P(None, None, "fsdp"),
        P("fsdp", None),
        P(None, None, "fsdp"),
    )
    out_specs = (P("fsdp", None, None), P("group", "fsdp", None), P("group", None, None, "fsdp"))
    return jax.shard_map(
        per_device, mesh=mesh, in_specs=in_specs, out_specs=out_specs, check_vma=False
    )
```

```python
import jax
import jax.numpy as jnp
from jax import lax
from jax.experimental import pallas as pl
from jax.experimental.pallas import tpu as pltpu
from jax.sharding import PartitionSpec as P

HEADS = 12
HD = 128
CH = 64
RANK = 64
NSTEPS = 1000
IMG = 256
TXT = 128
ROWS = TXT + IMG
HW = HEADS * HD
CHUNK = 512
EIGHTH = HW // 4
SIDE = 6 * RANK
SHARE = 72
PART = 128
WRITES = 4
MOVES = ((0, 0), (1, 0), (0, 2), (1, 2))
BF = jnp.bfloat16
F32 = jnp.float32
SCALE = HD ** (-0.5)


def dot(left, right, left_dim=1, right_dim=0):
    dims = (((left_dim,), (right_dim,)), ((), ()))
    return lax.dot_general(left, right, dims, preferred_element_type=F32)


def high_low(values):
    high = values.astype(BF)
    return high, (values - high.astype(F32)).astype(BF)


def unit_rows(values):
    values = values.astype(F32)
    return (values * lax.rsqrt(jnp.mean(values * values, axis=-1, keepdims=True) + 1e-06)).astype(BF)


def pack_kernel(
    base_ref,
    gen_down_ref,
    critic_down_ref,
    gen_up_ref,
    critic_up_ref,
    packed_ref,
    base,
    downs,
    ups,
    packed,
    read_sem,
    write_sem,
):
    reads = [
        pltpu.make_async_copy(base_ref, base, read_sem.at[0]),
        pltpu.make_async_copy(gen_down_ref, downs.at[0], read_sem.at[1]),
        pltpu.make_async_copy(critic_down_ref, downs.at[1], read_sem.at[2]),
        pltpu.make_async_copy(gen_up_ref, ups.at[0], read_sem.at[3]),
        pltpu.make_async_copy(critic_up_ref, ups.at[1], read_sem.at[4]),
    ]
    for read in reads:
        read.start()
    for read in reads:
        read.wait()
    group = lax.axis_index("group")

    def both(gen, critic):
        gen, critic = gen.astype(F32), critic.astype(F32)
        return jnp.concatenate([gen, jnp.where(group == 0, gen, critic)], axis=1).astype(BF)

    up_rows = [jnp.concatenate([ups[role, block] for block in range(3)], axis=1) for role in range(2)]
    sides = (both(downs[0], downs[1]), both(up_rows[0], up_rows[1]))
    eighths = []
    for near in range(4):
        start = pl.multiple_of(HW + group * HW + near * EIGHTH, EIGHTH)
        eighths.append(base[:, pl.ds(start, EIGHTH)])
    rows = base.shape[0]
    batch = packed.shape[0] // WRITES
    writes = []
    for step in range(WRITES):
        for device in range(step * batch, (step + 1) * batch):
            packed[device, :, :EIGHTH] = eighths[device % 4]
            packed[device, :, EIGHTH : EIGHTH + SIDE] = sides[device % 2]
            columns = base[:, device * SHARE : (device + 1) * SHARE]
            packed[device, :, EIGHTH + SIDE :] = jnp.concatenate(
                [columns, jnp.zeros((rows, PART - SHARE), BF)], axis=1
            )
        span = pl.ds(step * batch, batch)
        write = pltpu.make_async_copy(packed.at[span], packed_ref.at[span], write_sem.at[step])
        write.start()
        writes.append(write)
    for write in writes:
        write.wait()


def prompt_kernel(text_0_ref, text_1_ref, text_2_ref, text_3_ref, prompts_ref):
    for index, text_ref in enumerate((text_0_ref, text_1_ref, text_2_ref, text_3_ref)):
        prompts_ref[index * TXT : (index + 1) * TXT, :] = unit_rows(text_ref[...])


def sum_kernel(shares_ref, down_ref, up_ref):
    total = jnp.sum(shares_ref[...].astype(F32), axis=0)
    down_ref[...] = total[:, : 3 * RANK]
    for block in range(3):
        up_ref[block] = total[:, (3 + block) * RANK : (4 + block) * RANK]


def fold_kernel(
    latent_in_ref,
    modulation_ref,
    packed_ref,
    share_ref,
    side_ref,
    columns,
    sides,
    shares,
    read_sem,
    write_sem,
):
    read = pltpu.make_async_copy(packed_ref.at[:, EIGHTH + SIDE :], columns, read_sem.at[0])
    read.start()
    side = pltpu.make_async_copy(packed_ref.at[:, EIGHTH : EIGHTH + SIDE], sides, read_sem.at[1])
    side.start()
    scaled_in = (latent_in_ref[...].astype(F32) * modulation_ref[...]).astype(BF)
    folds = jnp.concatenate([latent_in_ref[...], scaled_in], axis=0)
    read.wait()
    side.wait()
    side = pltpu.make_async_copy(sides, side_ref, read_sem.at[1])
    side.start()
    share = dot(folds, columns[...]).T[:SHARE].astype(BF)
    batch = shares.shape[0]
    for device in range(batch):
        shares[device] = share
    writes = [
        pltpu.make_async_copy(shares, share_ref.at[pl.ds(step * batch, batch)], write_sem.at[step])
        for step in range(share_ref.shape[0] // batch)
    ]
    for write in writes:
        write.start()
    for write in writes:
        write.wait()
    side.wait()


def mix_kernel(prompts_ref, packed_ref, mine_ref, theirs_ref, columns, read_sem):
    read = pltpu.make_async_copy(packed_ref.at[:, :EIGHTH], columns, read_sem.at[0])
    read.start()
    read.wait()
    eighth = dot(prompts_ref[...], columns[...]).astype(BF)
    mine_ref[:TXT, :] = eighth[:TXT]
    theirs_ref[:TXT, :] = eighth[TXT : 2 * TXT]
    mine_ref[TXT:, :] = eighth[2 * TXT : 3 * TXT]
    theirs_ref[TXT:, :] = eighth[3 * TXT :]


def pair_kernel(mine_ref, received_ref, own_ref, near_ref):
    for place, part_ref in enumerate((mine_ref, received_ref)):
        own_ref[place] = part_ref[:TXT, :]
        near_ref[place] = part_ref[TXT:, :]


def forward_kernel(
    place_ref,
    sigma_ref,
    latent_ref,
    fresh_ref,
    prompt_ref,
    latent_in_ref,
    modulation_ref,
    velocity_out_ref,
    fold_ref,
    text_0_ref,
    text_1_ref,
    text_2_ref,
    text_3_ref,
    side_own_ref,
    side_core_ref,
    sample_ref,
    sample_again_ref,
    velocity_ref,
    narrow_velocity_ref,
    q_ref,
    k_ref,
    v_ref,
    weights_ref,
    inverse_ref,
    attended_ref,
    reduced_ref,
    picture_ref,
    role_up_ref,
    stacked,
    q_now,
    k_now,
    v_now,
    attended_now,
    text,
    downs,
    ups,
):
    group, near, core = place_ref[0], place_ref[1], place_ref[2]
    sigma = sigma_ref[0, 0]
    for (across, move), text_ref in zip(MOVES, (text_0_ref, text_1_ref, text_2_ref, text_3_ref)):
        for place in range(2):
            start = (group ^ across) * HW + (near ^ move ^ place) * EIGHTH
            text[:, pl.ds(pl.multiple_of(start, EIGHTH), EIGHTH)] = text_ref[place]

    @pl.when(core == 0)
    def _():
        downs[...] = side_own_ref[...]
        ups[...] = side_core_ref[...]

    @pl.when(core == 1)
    def _():
        downs[...] = side_core_ref[...]
        ups[...] = side_own_ref[...]

    role_up_ref[...] = ups[:, 3 * RANK :]

    def readout(latent, noise_level, role, switch, save):
        base = role * 3 * RANK
        narrow = latent.T.astype(BF)
        hidden = dot(narrow, latent_in_ref[...])
        inverse_rms = lax.rsqrt(jnp.mean(hidden * hidden, axis=-1, keepdims=True) + 1e-06)
        picture = (hidden * inverse_rms * (1.0 + noise_level * modulation_ref[...])).astype(BF)
        reduced_picture = dot(picture, downs[:, base : base + 3 * RANK]).astype(BF)
        reduced_prompt = dot(prompt_ref[:TXT, :], downs[:, base : base + 3 * RANK]).astype(BF)

        @save
        def _():
            picture_ref[...] = picture
            reduced_ref[TXT:, :] = reduced_picture
            reduced_ref[:TXT, :] = reduced_prompt

        if switch is not None:
            reduced_picture = reduced_picture * switch.astype(BF)
            reduced_prompt = reduced_prompt * switch.astype(BF)
        scaled_high, scaled_low = high_low(narrow.astype(F32) * inverse_rms)
        for block, now in enumerate((q_now, k_now, v_now)):
            rank_span = slice(block * RANK, (block + 1) * RANK)
            up_span = slice(base + block * RANK, base + (block + 1) * RANK)
            left = jnp.concatenate(
                [scaled_high, scaled_low, scaled_high, reduced_picture[:, rank_span]], axis=1
            )
            if block > 0:
                prompt_left = jnp.concatenate(
                    [jnp.zeros((TXT, 3 * CH), BF), reduced_prompt[:, rank_span]], axis=1
                )
                left = jnp.concatenate([prompt_left, left], axis=0)
            for start in range(0, HW, CHUNK):
                own = slice(start, start + CHUNK)
                wide = slice(block * HW + start, block * HW + start + CHUNK)
                parts = fold_ref[wide, :].astype(F32)
                fold_high, fold_low = high_low(parts[:, :CH] + noise_level * parts[:, CH:])
                up = ups[own, up_span]
                stacked[...] = jnp.concatenate([fold_high, fold_high, fold_low, up], axis=1)
                part = dot(left, stacked[...], 1, 1)
                if block == 0:
                    now[:, own] = part.astype(BF)
                else:
                    text_span = slice((block - 1) * HW + start, (block - 1) * HW + start + CHUNK)
                    now[TXT:, own] = part[TXT:].astype(BF)
                    now[:TXT, own] = (text[:, text_span].astype(F32) + part[:TXT]).astype(BF)

        def head(index, carry):
            span = pl.ds(pl.multiple_of(index * HD, HD), HD)
            queries, keys, values = q_now[:, span], k_now[:, span], v_now[:, span]
            scores = dot(queries, keys, 1, 1) * SCALE
            largest = jnp.max(scores, axis=-1, keepdims=True)
            weights = jnp.exp(scores - largest)
            inverse = 1.0 / jnp.sum(weights, axis=-1, keepdims=True)
            weights = weights.astype(BF)
            attended = (dot(weights, values) * inverse).astype(BF)
            attended_now[:, span] = attended

            @save
            def _():
                q_ref[:, span] = queries
                k_ref[:, span] = keys
                v_ref[:, span] = values
                attended_ref[:, span] = attended
                weights_ref[index] = weights
                inverse_ref[index] = inverse

            return carry

        lax.fori_loop(0, HEADS, head, 0, unroll=12)
        return dot(velocity_out_ref[...], attended_now[...], 1, 1)

    latent = latent_ref[...]
    sample = latent - readout(latent, 1.0, 0, None, lambda f: f())
    sample_ref[...] = sample
    sample_again_ref[...] = sample
    noised = (1.0 - sigma) * sample + sigma * fresh_ref[...]
    velocity = readout(noised, sigma, 1, group.astype(F32), pl.when(group == 1))
    velocity_ref[...] = velocity
    narrow_velocity_ref[...] = velocity.astype(BF)


def backward_kernel(
    place_ref,
    sigma_ref,
    sample_ref,
    fresh_ref,
    own_ref,
    fake_ref,
    prompt_ref,
    velocity_out_ref,
    role_up_ref,
    q_ref,
    k_ref,
    v_ref,
    weights_ref,
    inverse_ref,
    attended_ref,
    reduced_ref,
    picture_ref,
    mine_ref,
    theirs_ref,
    grad_q,
    grad_k,
    grad_v,
    grads,
):
    flag = place_ref[0]
    sigma = sigma_ref[0, 0]
    sample = sample_ref[...]
    own = own_ref[...]
    noised = (1.0 - sigma) * sample + sigma * fresh_ref[...]
    clean_real = noised - sigma * own
    clean_fake = noised - sigma * fake_ref[...].astype(F32)
    distance = jnp.sum(jnp.sum(jnp.abs(sample - clean_real), axis=1, keepdims=True), axis=0, keepdims=True)
    spread = distance * (1.0 / (IMG * CH)) + 1e-05
    cot_gen = -(clean_fake - clean_real) / spread
    cot_critic = 2.0 * (own - (fresh_ref[...] - sample)) / (IMG * CH)
    cotangent = jnp.where(flag == 0, cot_gen, cot_critic).T.astype(BF)

    def head(index, carry):
        span = pl.ds(pl.multiple_of(index * HD, HD), HD)
        queries, keys, values = q_ref[:, span], k_ref[:, span], v_ref[:, span]
        weights = weights_ref[index]
        upstream = dot(cotangent, velocity_out_ref[:, span]) * inverse_ref[index]
        inner = jnp.sum(upstream * attended_ref[:, span].astype(F32), axis=-1, keepdims=True)
        upstream = upstream.astype(BF)
        grad_v[:, span] = dot(weights, upstream, 0, 0).astype(BF)
        grad_weights = dot(upstream, values, 1, 1)
        grad_scores = (weights.astype(F32) * (grad_weights - inner) * SCALE).astype(BF)
        grad_q[:, span] = dot(grad_scores, keys).astype(BF)
        grad_k[:, span] = dot(grad_scores, queries, 0, 0).astype(BF)
        return carry

    lax.fori_loop(0, HEADS, head, 0, unroll=12)
    spans = [slice(block * RANK, (block + 1) * RANK) for block in range(3)]
    reduced_q = dot(grad_q[...], role_up_ref[:, spans[0]]).astype(BF)
    reduced_k = dot(grad_k[...], role_up_ref[:, spans[1]]).astype(BF)
    reduced_v = dot(grad_v[...], role_up_ref[:, spans[2]]).astype(BF)
    reduced_kv = jnp.concatenate([reduced_k, reduced_v], axis=1)
    down_q = dot(reduced_q, picture_ref[...], 0, 0)
    down_kv = dot(reduced_kv[:TXT], prompt_ref[:TXT, :], 0, 0) + dot(reduced_kv[TXT:], picture_ref[...], 0, 0)
    up_q = dot(reduced_ref[TXT:, spans[0]], grad_q[...], 0, 0)
    up_k = dot(reduced_ref[:, spans[1]], grad_k[...], 0, 0)
    up_v = dot(reduced_ref[:, spans[2]], grad_v[...], 0, 0)
    grads[...] = jnp.concatenate([down_q, down_kv, up_q, up_k, up_v], axis=0).T
    core = place_ref[2]
    pairs, rows, _ = mine_ref.shape
    for pair in range(pairs):
        mine = pl.ds(pl.multiple_of((2 * pair + core) * rows, 8), rows)
        theirs = pl.ds(pl.multiple_of((2 * pair + 1 - core) * rows, 8), rows)
        mine_ref[pair] = grads[mine, :]
        theirs_ref[pair] = grads[theirs, :].astype(BF)


def add_kernel(mine_ref, received_ref, sums_ref):
    sums_ref[...] = (mine_ref[...] + received_ref[...].astype(F32)).astype(BF)


def run(kernel, name, megabytes, scalars, outputs, scratch, *operands, far=(), out_space=pltpu.VMEM):
    shapes = tuple(jax.ShapeDtypeStruct(*output) for output in outputs)
    return pl.pallas_call(
        kernel,
        out_shape=shapes,
        in_specs=[
            pl.BlockSpec(
                memory_space=pltpu.SMEM if k < scalars else pl.ANY if k in far else pltpu.VMEM
            )
            for k in range(len(operands))
        ],
        out_specs=tuple([pl.BlockSpec(memory_space=out_space)] * len(outputs)),
        scratch_shapes=scratch,
        compiler_params=pltpu.CompilerParams(vmem_limit_bytes=megabytes * 2**20),
        name=name,
    )(*operands)


def per_device(
    latent_noise,
    fresh_noise,
    text_states,
    step_index,
    base_qkv,
    latent_in,
    modulation,
    velocity_out,
    gen_down,
    gen_up,
    critic_down,
    critic_up,
):
    devices = lax.axis_size("fsdp")
    group = lax.axis_index("group")
    index = lax.axis_index("fsdp")
    place = jnp.stack([group, lax.rem(index, 4), lax.rem(index, 2)]).astype(jnp.int32)
    sigma = ((step_index + 1).astype(F32) / NSTEPS).reshape(1, 1)
    shard = base_qkv.shape[0]

    def move(array, across, near):
        pairs = [
            (g * devices + device, (g ^ across) * devices + (device ^ near))
            for g in range(2)
            for device in range(devices)
        ]
        return lax.ppermute(array, ("group", "fsdp"), pairs)

    latent = latent_noise[0].T
    fresh = fresh_noise[0].T
    text = text_states[0]
    gain = modulation.reshape(1, HW)
    out_map = velocity_out.T

    texts = [text, move(text, 0, 1), move(text, 1, 2), move(text, 1, 3)]
    (packed,) = run(
        pack_kernel,
        "pack",
        60,
        0,
        [((devices, shard, EIGHTH + SIDE + PART), BF)],
        [
            pltpu.VMEM((shard, 3 * HW), BF),
            pltpu.VMEM((2, shard, 3 * RANK), BF),
            pltpu.VMEM((2, 3, shard, RANK), BF),
            pltpu.VMEM((devices, shard, EIGHTH + SIDE + PART), BF),
            pltpu.SemaphoreType.DMA((5,)),
            pltpu.SemaphoreType.DMA((WRITES,)),
        ],
        base_qkv,
        gen_down,
        critic_down,
        gen_up.transpose(0, 2, 1),
        critic_up.transpose(0, 2, 1),
        far=(0, 1, 2, 3, 4),
        out_space=pl.ANY,
    )
    packed = lax.all_to_all(packed, "fsdp", 0, 0).reshape(HW, EIGHTH + SIDE + PART)
    (prompts,) = run(prompt_kernel, "prompts", 16, 0, [((4 * TXT, HW), BF)], [], *texts)
    packed, prompts = lax.optimization_barrier((packed, prompts))
    share, side_own = run(
        fold_kernel,
        "fold",
        16,
        0,
        [((devices, SHARE, PART), BF), ((HW, SIDE), BF)],
        [
            pltpu.VMEM((HW, PART), BF),
            pltpu.VMEM((HW, SIDE), BF),
            pltpu.VMEM((devices // 8, SHARE, PART), BF),
            pltpu.SemaphoreType.DMA((2,)),
            pltpu.SemaphoreType.DMA((8,)),
        ],
        latent_in,
        gain,
        packed,
        far=(2,),
        out_space=pl.ANY,
    )
    fold = lax.all_to_all(share, "fsdp", 0, 0).reshape(devices * SHARE, PART)
    side_core = move(side_own, 0, 1)
    prompts, side_core = lax.optimization_barrier((prompts, side_core))
    mine, theirs = run(
        mix_kernel,
        "mix",
        16,
        0,
        [((2 * TXT, EIGHTH), BF)] * 2,
        [pltpu.VMEM((HW, EIGHTH), BF), pltpu.SemaphoreType.DMA((1,))],
        prompts,
        packed,
        far=(1,),
    )
    received = move(theirs, 0, 1)
    own_pair, near_pair = run(
        pair_kernel, "pair", 16, 0, [((2, TXT, EIGHTH), BF)] * 2, [], mine, received
    )
    pieces = [own_pair, move(own_pair, 1, 0), move(near_pair, 0, 2), move(near_pair, 1, 2)]

    sample, sample_again, velocity, narrow_velocity, *saved, role_up = run(
        forward_kernel,
        "forward",
        32,
        2,
        [
            ((CH, IMG), F32),
            ((CH, IMG), F32),
            ((CH, IMG), F32),
            ((CH, IMG), BF),
            ((IMG, HW), BF),
            ((ROWS, HW), BF),
            ((ROWS, HW), BF),
            ((HEADS, IMG, ROWS), BF),
            ((HEADS, IMG, 1), F32),
            ((IMG, HW), BF),
            ((ROWS, 3 * RANK), BF),
            ((IMG, HW), BF),
            ((HW, 3 * RANK), BF),
        ],
        [
            pltpu.VMEM((CHUNK, 4 * CH), BF),
            pltpu.VMEM((IMG, HW), BF),
            pltpu.VMEM((ROWS, HW), BF),
            pltpu.VMEM((ROWS, HW), BF),
            pltpu.VMEM((IMG, HW), BF),
            pltpu.VMEM((TXT, 2 * HW), BF),
            pltpu.VMEM((HW, SIDE), BF),
            pltpu.VMEM((HW, SIDE), BF),
        ],
        place,
        sigma,
        latent,
        fresh,
        prompts,
        latent_in,
        gain,
        out_map,
        fold,
        *pieces,
        side_own,
        side_core,
    )
    fake_velocity = lax.ppermute(narrow_velocity, "group", [(1, 0)])
    half = (devices // 2, shard, SIDE)
    mine, theirs = run(
        backward_kernel,
        "backward",
        24,
        2,
        [(half, F32), (half, BF)],
        [
            pltpu.VMEM((IMG, HW), BF),
            pltpu.VMEM((ROWS, HW), BF),
            pltpu.VMEM((ROWS, HW), BF),
            pltpu.VMEM((HW, SIDE), F32),
        ],
        place,
        sigma,
        sample_again,
        fresh,
        velocity,
        fake_velocity,
        prompts,
        out_map,
        role_up,
        *saved,
    )
    (sums,) = run(add_kernel, "add", 16, 0, [(half, BF)], [], mine, move(theirs, 0, 1))
    parities = [list(range(core, devices, 2)) for core in range(2)]
    shares = lax.all_to_all(sums, "fsdp", 0, 0, axis_index_groups=parities)
    share_down, share_up = run(
        sum_kernel,
        "total",
        16,
        0,
        [((shard, 3 * RANK), F32), ((3, shard, RANK), F32)],
        [],
        shares,
    )
    return (sample.T[None], share_down[None], share_up.transpose(0, 2, 1)[None])


def solution(mesh):
    in_specs = (
        P("fsdp", None, None),
        P("fsdp", None, None),
        P("fsdp", None, None),
        P("fsdp"),
        P("fsdp", None),
        P(),
        P(),
        P(),
        P("fsdp", None),
        P(None, None, "fsdp"),
        P("fsdp", None),
        P(None, None, "fsdp"),
    )
    out_specs = (P("fsdp", None, None), P("group", "fsdp", None), P("group", None, None, "fsdp"))
    return jax.shard_map(
        per_device, mesh=mesh, in_specs=in_specs, out_specs=out_specs, check_vma=False
    )
```
